128 devices in a mesh: strike: 4 (over x), dip: 8 (over y, core), layer: 4 (over z).
Axes of the slice: x: 4, y: 4, z: 4, core: 2. Of those that a mesh axis runs over, the one named last changes fastest.
Arguments:
- perm_class: int32 [64, 128, 512], P('strike', 'dip', 'layer'), may hold values from 0 to 15
- perm_table: float32 [16], replicated, may hold values from 0.3 to 3
- boreholes: int32 [32], replicated, may hold values from 0 to 4194303
- start_guess: float32 [32, 64, 128, 512], P(None, 'strike', 'dip', 'layer'), may hold values from -0.005859375 to 0.005859375
Outputs:
- solution: float32 [32, 64, 128, 512], P(None, 'strike', 'dip', 'layer')
- residual: float32 [32, 64, 128, 512], P(None, 'strike', 'dip', 'layer')
The draws below stay inside these ranges and needn't reach their ends.
Inputs may be any that keep to these rules, and one draw needn't show every extreme that they name: boreholes[j] is the flat index (x * 128 + y) * 512 + z of the cell that right-hand side j drains.
All inputs are finite; a program needn't handle non-finite values.
Results may differ from the reference program's by a relative error of at most 0.0003.
Values sent between devices are 32-bit elements; how exact they have to be, the bound alone decides.
No kernel may reach another device: no remote copies, remote signals or barrier semaphores. Data moves between devices by JAX's collectives and lax.ppermute only.
A program may use at most 128 MiB of HBM per device.

```python
import math
import jax
import jax.numpy as jnp
from jax import lax

NRHS = 32
CLASSES = 16
ITERS = 2
NX = 64
NY = 128
NZ = 512


def draw_start_guess(key, part):
    key = jax.random.fold_in(key, 7)
    key_own, key_shared, key_weight, key_scale, key_texture = jax.random.split(key, 5)
    private = jnp.clip(jax.random.normal(key_own, (NRHS, NX, NY, NZ), jnp.float32), -4.0, 4.0)
    shared = jnp.clip(jax.random.normal(key_shared, (1, NX, NY, NZ), jnp.float32), -4.0, 4.0)
    weight = jax.random.uniform(key_weight, (NRHS, 1, 1, 1), jnp.float32, 0.3, 1.2)
    column_scale = jnp.exp(jax.random.uniform(key_scale, (NRHS, 1, 1, 1), jnp.float32, -0.5, 0.5))
    texture = jnp.exp(jax.random.uniform(key_texture, (1, NX, NY, NZ), jnp.float32, -0.7, 0.7))
    along_x = jnp.arange(NX, dtype=jnp.float32).reshape(1, NX, 1, 1) / NX
    along_y = jnp.arange(NY, dtype=jnp.float32).reshape(1, 1, NY, 1) / NY
    along_z = jnp.arange(NZ, dtype=jnp.float32).reshape(1, 1, 1, NZ) / NZ
    position = along_x + along_y + along_z
    cell_root = math.sqrt(float(NX * NY * NZ))
    limit = 12.0 / cell_root
    growth = 0.02 / cell_root * jnp.exp(math.log(3.0) * position)
    values = private + weight * shared
    return jnp.clip(values * column_scale * texture * growth, -limit, limit)


def plant(values, own_key, low, top_value):
    extent = values.shape
    index_at = [jax.random.randint(jax.random.fold_in(own_key, axis), (), 0, extent[axis]) for axis in range(len(extent))]
    values = values.at[tuple(index_at)].set(low)
    longest = extent.index(max(extent))
    index_at[longest] = (index_at[longest] + 1) % extent[longest]
    return values.at[tuple(index_at)].set(top_value)


def setup_inputs(seed: int = 0) -> dict:
    seeds = jax.random.split(jax.random.key(seed), 5)
    perm_class = plant(jax.random.randint(seeds[0], (NX, NY, NZ), 0, CLASSES), jax.random.fold_in(seeds[0], 1), 0, CLASSES - 1).astype(jnp.int32)
    perm_table = jnp.clip(jnp.exp(jax.random.uniform(seeds[1], (CLASSES,), jnp.float32, math.log(0.3), math.log(3.0))), 0.3, 3.0)
    boreholes = plant(jax.random.randint(seeds[2], (NRHS,), 0, NX * NY * NZ), jax.random.fold_in(seeds[2], 1), 0, (NX * NY * NZ) - 1).astype(jnp.int32)
    start_guess = draw_start_guess(jax.random.fold_in(seeds[4], 71), 0)
    return dict(perm_class=perm_class, perm_table=perm_table, boreholes=boreholes, start_guess=start_guess)


leakage = 0.01
highest = lax.Precision.HIGHEST

def face_weight(center_k, beside_k):
    summed = center_k + beside_k
    divisor = jnp.where(summed > 0.0, summed, 1.0)
    return jnp.where(summed > 0.0, 2.0 * center_k * beside_k / divisor, 0.0)

def face_weights(padded_perm):
    center = padded_perm[1:-1, 1:-1, 1:-1]
    return (face_weight(center, padded_perm[:-2, 1:-1, 1:-1]), face_weight(center, padded_perm[2:, 1:-1, 1:-1]), face_weight(center, padded_perm[1:-1, :-2, 1:-1]), face_weight(center, padded_perm[1:-1, 2:, 1:-1]), face_weight(center, padded_perm[1:-1, 1:-1, :-2]), face_weight(center, padded_perm[1:-1, 1:-1, 2:]))

def operate(padded, weights):
    center = padded[:, 1:-1, 1:-1, 1:-1]
    result = leakage * center
    result = result + weights[0][None] * (center - padded[:, :-2, 1:-1, 1:-1])
    result = result + weights[1][None] * (center - padded[:, 2:, 1:-1, 1:-1])
    result = result + weights[2][None] * (center - padded[:, 1:-1, :-2, 1:-1])
    result = result + weights[3][None] * (center - padded[:, 1:-1, 2:, 1:-1])
    result = result + weights[4][None] * (center - padded[:, 1:-1, 1:-1, :-2])
    result = result + weights[5][None] * (center - padded[:, 1:-1, 1:-1, 2:])
    return result

def products(former, latter):
    left_rows = former.reshape(former.shape[0], -1)
    right_rows = latter.reshape(latter.shape[0], -1)
    return lax.dot_general(left_rows.astype(jnp.float32), right_rows.astype(jnp.float32), (((1,), (1,)), ((), ())), precision=highest, preferred_element_type=jnp.float32)

def combine(mixing, field):
    rows = field.reshape(field.shape[0], -1)
    mixed = lax.dot_general(mixing.astype(jnp.float32), rows.astype(jnp.float32), (((0,), (0,)), ((), ())), precision=highest, preferred_element_type=jnp.float32)
    return mixed.reshape(field.shape)

def spd_solve(matrix, targets):
    factor = jnp.linalg.cholesky(matrix)
    partial_sol = lax.linalg.triangular_solve(factor, targets, left_side=True, lower=True)
    return lax.linalg.triangular_solve(factor, partial_sol, left_side=True, lower=True, transpose_a=True)

def pad_cells(field):
    return jnp.pad(field, ((0, 0), (1, 1), (1, 1), (1, 1)))

def reference(perm_class, perm_table, boreholes, start_guess):
    columns = start_guess.shape[0]
    permeability = perm_table[perm_class]
    weights = face_weights(jnp.pad(permeability, 1))
    flat_sources = jnp.zeros((columns, NX * NY * NZ), start_guess.dtype)
    flat_sources = flat_sources.at[jnp.arange(columns), boreholes].set(1.0)
    sources = flat_sources.reshape(start_guess.shape)
    solution = start_guess
    residual = sources - operate(pad_cells(start_guess), weights)
    direction = residual
    norm_now = products(residual, residual)
    for iteration in range(ITERS):
        if iteration > 0:
            norm_next = products(residual, residual)
            conjugate = spd_solve(norm_now, norm_next)
            direction = residual + combine(conjugate, direction)
            norm_now = norm_next
        applied = operate(pad_cells(direction), weights)
        curvature = products(direction, applied)
        advance = spd_solve(curvature, norm_now)
        solution = solution + combine(advance, direction)
        residual = residual - combine(advance, applied)
    return (solution, residual)
```

```python
import functools

import jax
import jax.numpy as jnp
from jax import lax
from jax.experimental import pallas as pl
from jax.experimental.pallas import tpu as pltpu
from jax.sharding import PartitionSpec as P

LEAKAGE = 0.01
HIGHEST = lax.Precision.HIGHEST
F32 = jnp.float32
BF16 = jnp.bfloat16
VMEM_LIMIT = 24 * 1024 * 1024
AXES = ("strike", "dip", "layer")
VMEM = pl.BlockSpec(memory_space=pltpu.VMEM)
SMEM = pl.BlockSpec(memory_space=pltpu.SMEM)
HBM = pl.BlockSpec(memory_space=pltpu.HBM)


def params(**more):
    return pltpu.CompilerParams(vmem_limit_bytes=VMEM_LIMIT, **more)


def shaped(*shape):
    return jax.ShapeDtypeStruct(shape, F32)


def lanes(rows):
    return lax.broadcasted_iota(jnp.int32, (rows, 128), 1)


def rows_of(count):
    return lax.broadcasted_iota(jnp.int32, (count, 128), 0)


def packed_ends(cells, y, into):
    turned = pltpu.roll(cells, 2 * y + 1, 1)
    lane = lanes(cells.shape[0])
    return jnp.where((lane == 2 * y) | (lane == 2 * y + 1), turned, into)


def place_x(tile, x, ref, plane, rows):
    turned = pltpu.roll(tile, (x % 4) * 32, 1)
    lane = lanes(tile.shape[0])
    mine = (lane // 32) == (x % 4)
    ref[plane, rows, :] = jnp.where(mine, turned, ref[plane, rows, :])


def pack_kernel(
    class_hbm, table_hbm, guess_hbm, field_ref, perm_ref, xlo, xhi, ylo, yhi, ends_ref,
    classes, table, guess, plane_sem, class_sem, table_sem,
):
    columns, nx, ny, nz = guess_hbm.shape

    def plane(x):
        return pltpu.make_async_copy(guess_hbm.at[:, x], guess.at[x], plane_sem.at[x])

    class_copy = pltpu.make_async_copy(class_hbm, classes, class_sem)
    table_copy = pltpu.make_async_copy(table_hbm, table, table_sem)
    table_copy.start()
    class_copy.start()
    for x in range(nx):
        plane(x).start()
    ends_ref[...] = jnp.zeros_like(ends_ref)
    for ref in (xlo, xhi, ylo, yhi):
        ref[ny] = jnp.zeros((columns, nz), F32)
    table_copy.wait()
    class_copy.wait()
    lane = lanes(ny)
    row = rows_of(ny)

    def permeability(x, carry):
        perm = jnp.zeros((ny, nz), F32)
        for level in range(table.shape[0]):
            perm = jnp.where(classes[x] == level, table[level], perm)
        perm_ref[x] = perm
        ylo[ny, pl.ds(x, 1), :] = perm[0:1]
        yhi[ny, pl.ds(x, 1), :] = perm[ny - 1 : ny]
        first = jnp.broadcast_to(perm[:, 0:1], (ny, nz))
        final = jnp.broadcast_to(perm[:, nz - 1 : nz], (ny, nz))
        both = jnp.where(lane == 2 * row, final, jnp.where(lane == 2 * row + 1, first, 0.0))
        edge = jnp.sum(both, axis=0, keepdims=True)
        place_x(edge, x, ends_ref, 4, pl.ds(x // 4, 1))
        return carry

    lax.fori_loop(0, nx, permeability, 0)
    xlo[ny, 0:ny, :] = perm_ref[0]
    xhi[ny, 0:ny, :] = perm_ref[nx - 1]

    def cells_of(x, carry):
        plane(x).wait()
        flat = guess.at[x].reshape(columns * ny, nz)
        ends = jnp.zeros((columns, nz), F32)
        for y in range(ny):
            cells = flat[pl.ds(y, columns, stride=ny), :]
            field_ref[x, y] = cells
            ends = packed_ends(cells, y, ends)
            if y == 0:
                ylo[x] = cells
            if y == ny - 1:
                yhi[x] = cells
        place_x(ends, x, ends_ref, x // 4, slice(None))
        return carry

    lax.fori_loop(0, nx, cells_of, 0)
    for y in range(ny):
        xlo[y] = field_ref[0, y]
        xhi[y] = field_ref[nx - 1, y]


def pack(perm_class, perm_table, start_guess):
    columns, nx, ny, nz = start_guess.shape
    face = shaped(ny + 1, columns, nz)
    return pl.pallas_call(
        pack_kernel,
        in_specs=[HBM] * 3,
        out_specs=[VMEM] * 7,
        out_shape=[
            shaped(nx, ny, columns, nz),
            shaped(nx, ny, nz),
            face,
            face,
            shaped(nx + 1, columns, nz),
            shaped(nx + 1, columns, nz),
            shaped(5, columns, nz),
        ],
        scratch_shapes=[
            pltpu.VMEM((nx, ny, nz), jnp.int32),
            pltpu.SMEM(perm_table.shape, F32),
            pltpu.VMEM((nx, columns, ny, nz), F32),
            pltpu.SemaphoreType.DMA((nx,)),
            pltpu.SemaphoreType.DMA(()),
            pltpu.SemaphoreType.DMA(()),
        ],
        compiler_params=params(),
        name="pack_guess",
    )(perm_class, perm_table, start_guess)


def face_weight(center_k, beside_k):
    summed = center_k + beside_k
    divisor = jnp.where(summed > 0.0, summed, 1.0)
    return jnp.where(summed > 0.0, 2.0 * center_k * beside_k / divisor, 0.0)


def arrived(left, right, left_scale=None, right_scale=None):
    after = pltpu.roll(right, 127, 1)
    before = pltpu.roll(left, 1, 1)
    if left_scale is not None:
        after, before = after * right_scale, before * left_scale
    return jnp.where(lanes(left.shape[0]) % 2 == 0, after, before)


def inner_weights(perm_ref, inside, hz, wx, wy, wzm, wzp):
    nx, ny, nz = perm_ref.shape
    lane = lanes(ny)
    row = rows_of(ny)

    def at_x(x, carry):
        center = perm_ref[x]
        wx[x] = face_weight(center, perm_ref[jnp.maximum(x - 1, 0)])
        below = jnp.concatenate([center[:1], center[: ny - 1]], axis=0)
        wy[x, 0:ny, :] = face_weight(center, below)
        ends = arrived(
            hz[0][4, pl.ds(x // 4, 1), :], hz[1][4, pl.ds(x // 4, 1), :], inside[4], inside[5]
        )
        ends = jnp.broadcast_to(ends, (ny, nz))
        offset = (x % 4) * 32 + 2 * row
        after = jnp.sum(jnp.where(lane == offset, ends, 0.0), axis=1, keepdims=True)
        ahead = jnp.sum(jnp.where(lane == offset + 1, ends, 0.0), axis=1, keepdims=True)
        wzm[x] = face_weight(center, jnp.where(lane == 0, ahead, pltpu.roll(center, 1, 1)))
        wzp[x] = face_weight(center, jnp.where(lane == nz - 1, after, pltpu.roll(center, nz - 1, 1)))
        return carry

    lax.fori_loop(0, nx, at_x, 0)


def outer_weights(perm_ref, inside, hx, hy, wx, wy):
    nx, ny, nz = perm_ref.shape
    wx[0] = face_weight(perm_ref[0], hx[0][...] * inside[0])
    wx[nx] = face_weight(perm_ref[nx - 1], hx[1][...] * inside[1])
    low = jnp.concatenate([perm_ref[x, 0:1, :] for x in range(nx)], axis=0)
    high = jnp.concatenate([perm_ref[x, ny - 1 : ny, :] for x in range(nx)], axis=0)
    low = face_weight(low, hy[0][0:nx] * inside[2])
    high = face_weight(high, hy[1][0:nx] * inside[3])
    for x in range(nx):
        wy[x, 0:1, :] = low[x : x + 1]
        wy[x, ny : ny + 1, :] = high[x : x + 1]


def local_sources(boreholes, anchors, nx, ny, nz, total_y, total_z):
    cell = jnp.broadcast_to(boreholes, (boreholes.shape[0], nz))
    along_z = cell % total_z - anchors[2]
    along_y = (cell // total_z) % total_y - anchors[1]
    along_x = cell // (total_z * total_y) - anchors[0]
    inside = (along_x >= 0) & (along_x < nx) & (along_y >= 0) & (along_y < ny)
    matched = inside & (along_z == lanes(boreholes.shape[0]))
    return jnp.where(matched, along_x * ny + along_y, -1)


def inner_kernel(first, last, totals, *refs):
    refs = list(refs)
    take = lambda count: [refs.pop(0) for _ in range(count)]
    field, hzl, hzr = take(3)
    if first:
        perm, inside, anchors, boreholes = take(4)
    else:
        wx, wy, wzm, wzp = take(4)
    (out,) = take(1)
    if not last:
        (ends,) = take(1)
    if first:
        wx, wy, wzm, wzp = take(4)
    else:
        (total,) = take(1)
    (flux,) = take(1)
    nx, ny, columns, nz = field.shape
    if not last:
        ends[...] = jnp.zeros_like(ends)
    if first:
        inner_weights(perm, inside, (hzl, hzr), wx, wy, wzm, wzp)
        code = local_sources(boreholes[...], anchors, nx, ny, nz, totals[1], totals[2])
    else:
        total[...] = jnp.zeros_like(total)
    flux[...] = jnp.zeros_like(flux)
    lane = lanes(columns)

    def at_x(x, beside):
        block = lax.div(x, 4)
        beyond = arrived(hzl[block], hzr[block])
        beyond = pltpu.roll(beyond, lax.rem(128 - lax.rem(x, 4) * 32, 128), 1)
        center = field[x, 0]
        flux_y = None
        mine = jnp.zeros((columns, nz), F32)
        for y in range(ny):
            applied = LEAKAGE * center - flux[y]
            if beside is not None:
                flux_x = wx[x + 1, y : y + 1, :] * (center - beside[y])
                applied = applied + flux_x
                flux[y] = flux_x
            if flux_y is not None:
                applied = applied - flux_y
            if y + 1 < ny:
                following = field[x, y + 1]
                flux_y = wy[x, y + 1 : y + 2, :] * (center - following)
                applied = applied + flux_y
            edge = pltpu.roll(beyond, (128 - (2 * y + 1)) % 128, 1)
            after = jnp.where(lane == nz - 1, edge, pltpu.roll(center, nz - 1, 1))
            before = jnp.where(lane == 0, edge, pltpu.roll(center, 1, 1))
            applied = applied + wzp[x, y : y + 1, :] * (center - after)
            applied = applied + wzm[x, y : y + 1, :] * (center - before)
            if first:
                applied = jnp.where(code == x * ny + y, 1.0, 0.0) - applied
            out[x, y] = applied
            if not last:
                mine = packed_ends(applied, y, mine)
            center = following
        if not last:
            place_x(mine, x, ends, block, slice(None))
        if not first:
            left = split([jnp.concatenate([field[x, y] for y in range(ny)], axis=1)])
            right = split([jnp.concatenate([out[x, y] for y in range(ny)], axis=1)])
            total[...] += gram(left, jnp.concatenate([left, right], axis=0))

    def inner(x, carry):
        at_x(x, field.at[x + 1])
        return carry

    lax.fori_loop(0, nx - 1, inner, 0)
    at_x(jnp.int32(nx - 1), None)


def sides_kernel(first, last, *refs):
    refs = list(refs)
    take = lambda count: [refs.pop(0) for _ in range(count)]
    _, field, hxl, hxr, hyl, hyr = take(6)
    if not last:
        take(1)
    if first:
        take(2)
        perm, inside = take(2)
    else:
        wx, wy, total = take(3)
    if last:
        (earlier,) = take(1)
    (out,) = take(1)
    if not last:
        (ends,) = take(1)
    if first:
        wx, wy = take(2)
    else:
        (sums,) = take(1)
    if not last:
        xlo, xhi, ylo, yhi = take(4)
    nx, ny, columns, nz = field.shape
    lane = lanes(columns)
    if first:
        hx = (hxl.at[ny, 0:ny], hxr.at[ny, 0:ny])
        outer_weights(perm, inside, hx, (hyl.at[ny], hyr.at[ny]), wx, wy)

    added = None
    faces = (
        (hxl, [(0, y) for y in range(ny)], [(0, y) for y in range(ny)], wx),
        (hxr, [(nx - 1, y) for y in range(ny)], [(nx, y) for y in range(ny)], wx),
        (hyl, [(x, 0) for x in range(nx)], [(x, 0) for x in range(nx)], wy),
        (hyr, [(x, ny - 1) for x in range(nx)], [(x, ny) for x in range(nx)], wy),
    )
    for halo, rows, weight_rows, weight in faces:
        own, fluxes = [], []
        for place, ((x, y), (p, q)) in enumerate(zip(rows, weight_rows)):
            center = field[x, y]
            flux = weight[p, q : q + 1, :] * (center - halo[place])
            if first:
                out[x, y] -= flux
            else:
                out[x, y] += flux
                own.append(center)
                fluxes.append(flux)
        if not first:
            left = split([jnp.concatenate(own, axis=1)])
            right = split([jnp.concatenate(fluxes, axis=1)])
            part = gram(left, right)
            added = part if added is None else added + part
    if not last:
        for x in range(nx):
            tile = ends[x // 4]
            for y in range(ny):
                if x in (0, nx - 1) or y in (0, ny - 1):
                    tile = packed_ends(out[x, y], (x % 4) * 16 + y, tile)
            ends[x // 4] = tile
        for y in range(ny):
            xlo[y] = out[0, y]
            xhi[y] = out[nx - 1, y]
        for x in range(nx):
            ylo[x] = out[x, 0]
            yhi[x] = out[x, ny - 1]
    if not first:
        held = total[...]
        held = held[0:32] + held[32:64]
        held = held + pltpu.roll(held, 96, 1)
        held = jnp.where(lane < 32, held, pltpu.roll(held, 96, 1))
        fixed = added[0:32] + added[32:64]
        fixed = fixed[:, 0:32] + fixed[:, 32:64]
        fixed = jnp.concatenate([fixed, jnp.zeros((columns, 96), F32)], axis=1)
        held = jnp.where(lane < 32, held, held + pltpu.roll(fixed, 32, 1))
        if last:
            held = jnp.where(lane < 64, earlier[...], pltpu.roll(held, 64, 1))
        sums[...] = held


def split(fields):
    high = [field.astype(BF16) for field in fields]
    low = [(field - top.astype(F32)).astype(BF16) for field, top in zip(fields, high)]
    return jnp.concatenate(high + low, axis=0)


def gram(left, right):
    return lax.dot_general(left, right, (((1,), (1,)), ((), ())), preferred_element_type=F32)


def fold(products, fields):
    half = products.shape[0] // 2
    summed = products[:half] + products[half:]
    return summed[:, :half] + summed[:, half:]


def inner_part(field, halos, extra, first, last, totals):
    nx, ny, columns, nz = field.shape
    in_specs = [VMEM] * 3
    if first:
        in_specs += [VMEM, SMEM, SMEM, VMEM]
    else:
        in_specs += [VMEM] * 4
    out_shape = [shaped(nx, ny, columns, nz)]
    if not last:
        out_shape += [shaped(4, columns, nz)]
    if first:
        out_shape += [
            shaped(nx + 1, ny, nz),
            shaped(nx, ny + 8, nz),
            shaped(nx, ny, nz),
            shaped(nx, ny, nz),
        ]
    else:
        out_shape += [shaped(2 * columns, 4 * columns)]
    return pl.pallas_call(
        functools.partial(inner_kernel, first, last, totals),
        in_specs=in_specs,
        out_specs=[VMEM] * len(out_shape),
        out_shape=out_shape,
        scratch_shapes=[pltpu.VMEM((ny, columns, nz), F32)],
        compiler_params=params(),
        cost_estimate=pl.CostEstimate(
            flops=20 * field.size, bytes_accessed=6 * field.size * 4, transcendentals=0
        ),
        name="inner_first" if first else "inner_last" if last else "inner_next",
    )(field, *halos, *extra)


def sides_part(part, field, halos, ends, extra, first, last):
    nx, ny, columns, nz = field.shape
    operands = [part, field, *halos]
    if not last:
        operands += [ends]
    operands += extra
    in_specs = [VMEM] * len(operands)
    aliases = {0: 0}
    out_shape = [shaped(*part.shape)]
    if not last:
        aliases[6] = 1
        out_shape += [shaped(*ends.shape)]
    if first:
        in_specs[-1] = SMEM
        aliases[7] = 2
        aliases[8] = 3
        out_shape += [shaped(*extra[0].shape), shaped(*extra[1].shape)]
    else:
        out_shape += [shaped(columns, 128)]
    if not last:
        out_shape += [shaped(ny, columns, nz)] * 2 + [shaped(nx, columns, nz)] * 2
    return pl.pallas_call(
        functools.partial(sides_kernel, first, last),
        in_specs=in_specs,
        out_specs=[VMEM] * len(out_shape),
        out_shape=out_shape,
        input_output_aliases=aliases,
        compiler_params=params(),
        name="sides_first" if first else "sides_last" if last else "sides_next",
    )(*operands)


def exchanged(xlo, xhi, ylo, yhi, ends):
    ahead = lambda axis: [(i, (i + 1) % lax.axis_size(axis)) for i in range(lax.axis_size(axis))]
    back = lambda axis: [(j, i) for i, j in ahead(axis)]
    near = (
        lax.ppermute(ends, "layer", ahead("layer")),
        lax.ppermute(ends, "layer", back("layer")),
    )
    far = (
        lax.ppermute(xhi, "strike", ahead("strike")),
        lax.ppermute(xlo, "strike", back("strike")),
        lax.ppermute(yhi, "dip", ahead("dip")),
        lax.ppermute(ylo, "dip", back("dip")),
    )
    return near, far


def dot(left, right, contract=(1, 0)):
    dims = (((contract[0],), (contract[1],)), ((), ()))
    return lax.dot_general(left, right, dims, precision=HIGHEST, preferred_element_type=F32)


def eliminate(tables):
    row = rows_of(32)
    for k in range(32):
        done = []
        for table in tables:
            column = jnp.broadcast_to(table[:, k : k + 1], table.shape)
            scaled = table[k : k + 1, :] / column[k : k + 1, :]
            done.append(jnp.where(row == k, scaled, table - column * scaled))
        tables = done
    return tables


def solve_kernel(own_ref, other_ref, out_ref):
    sums = own_ref[...] + other_ref[...]
    lane = lanes(32)
    row = rows_of(32)
    unit = jnp.where(lane == row + 32, 1.0, 0.0)
    advance_table = jnp.where(lane < 32, pltpu.roll(sums, 96, 1), pltpu.roll(sums, 32, 1))
    norm_table = jnp.where(lane < 32, sums, unit)
    advance_table, norm_table = eliminate([advance_table, norm_table])
    norm = sums[:, 0:32]
    moment = sums[:, 32:64]
    square = sums[:, 64:96]
    cube = sums[:, 96:128]
    advance = advance_table[:, 32:64]
    inverse = norm_table[:, 32:64]
    turned = dot(square, advance)
    tripled = dot(dot(advance, cube, (0, 0)), advance)
    norm_next = dot(advance, turned, (0, 0)) - norm
    eye = jnp.where(lane[:, 0:32] == row[:, 0:32], 1.0, 0.0)
    mixing = eye + dot(inverse, norm_next)
    curvature = dot(mixing, dot(moment, mixing) - turned, (0, 0))
    curvature = curvature - dot(turned, mixing, (0, 0)) + tripled
    wide = jnp.concatenate([curvature, norm_next, jnp.zeros((32, 64), F32)], axis=1)
    (wide,) = eliminate([wide])
    later = wide[:, 32:64]
    taken = advance + dot(mixing, later)
    beyond = dot(advance, later)
    taken_t = taken.T
    beyond_t = beyond.T
    nothing = jnp.zeros((32, 32), F32)
    out_ref[0:32, :] = jnp.concatenate([taken_t, -beyond_t, nothing, nothing], axis=1)
    out_ref[32:64, :] = jnp.concatenate([nothing, -taken_t, beyond_t, nothing], axis=1)


def solve(own, other):
    return pl.pallas_call(
        solve_kernel,
        in_specs=[VMEM] * 2,
        out_specs=VMEM,
        out_shape=shaped(64, 128),
        compiler_params=params(),
        name="solve_small",
    )(own, other)


def combine_kernel(
    mix_ref, guess_ref, one_ref, two_ref, three_ref, solution_hbm, residual_hbm,
    solution, residual, sem,
):
    nx, ny, columns, nz = guess_ref.shape
    slots = solution.shape[0]
    mix = mix_ref[...]
    high = mix.astype(BF16)
    low = (mix - high.astype(F32)).astype(BF16)
    mixing = jnp.concatenate(
        [jnp.concatenate([high, high], axis=1), jnp.concatenate([low, low], axis=1)], axis=0
    )
    nothing = jnp.zeros((columns, 2 * nz), F32)

    def leaving(x):
        slot = lax.rem(x, slots)
        return (
            pltpu.make_async_copy(solution.at[slot], solution_hbm.at[:, x], sem.at[0, slot]),
            pltpu.make_async_copy(residual.at[slot], residual_hbm.at[:, x], sem.at[1, slot]),
        )

    def at_x(x, carry):
        slot = lax.rem(x, slots)

        @pl.when(x >= slots)
        def _():
            for copy in leaving(x - slots):
                copy.wait()

        solution_rows = solution.at[slot].reshape(columns * ny, nz)
        residual_rows = residual.at[slot].reshape(columns * ny, nz)
        for y in range(0, ny, 2):
            fields = [
                jnp.concatenate([ref[x, y], ref[x, y + 1]], axis=1)
                for ref in (one_ref, two_ref, three_ref)
            ]
            halves = split(fields + [nothing])
            mixed = jnp.dot(mixing, halves, preferred_element_type=F32)
            mixed = mixed[0:64] + mixed[64:128]
            for step in range(2):
                rows = pl.ds(y + step, columns, stride=ny)
                part = mixed[:, step * nz : (step + 1) * nz]
                solution_rows[rows, :] = guess_ref[x, y + step] + part[0:32]
                residual_rows[rows, :] = one_ref[x, y + step] + part[32:64]
        for copy in leaving(x):
            copy.start()
        return carry

    lax.fori_loop(0, nx, at_x, 0)
    for x in range(nx - slots, nx):
        for copy in leaving(jnp.int32(x)):
            copy.wait()


def combine(mix, guess, one, two, three):
    nx, ny, columns, nz = guess.shape
    return pl.pallas_call(
        combine_kernel,
        in_specs=[VMEM] * 5,
        out_specs=[HBM] * 2,
        out_shape=[shaped(columns, nx, ny, nz)] * 2,
        scratch_shapes=[
            pltpu.VMEM((8, columns, ny, nz), F32),
            pltpu.VMEM((8, columns, ny, nz), F32),
            pltpu.SemaphoreType.DMA((2, 8)),
        ],
        compiler_params=params(),
        name="combine_fields",
    )(mix, guess, one, two, three)


def summed_but_last(values):
    steps = []
    for axis in AXES[1:] + AXES[:1]:
        size, mask = lax.axis_size(axis), 1
        while mask < size:
            steps.append((axis, [(i, i ^ mask) for i in range(size)]))
            mask *= 2
    for axis, pairs in steps[:-1]:
        values = values + lax.ppermute(values, axis, pairs)
    axis, pairs = steps[-1]
    return values, lax.ppermute(values, axis, pairs)


def shards(perm_class, perm_table, boreholes, start_guess):
    columns, nx, ny, nz = start_guess.shape
    places = [lax.axis_index(axis) for axis in AXES]
    sizes = [lax.axis_size(axis) for axis in AXES]
    anchors = jnp.stack([place * size for place, size in zip(places, (nx, ny, nz))])
    totals = tuple(size * count for size, count in zip((nx, ny, nz), sizes))
    inside = []
    for place, size in zip(places, sizes):
        inside += [place > 0, place < size - 1]
    inside = jnp.stack(inside).astype(F32)

    guess, perm, *faces = pack(perm_class, perm_table, start_guess)
    near, far = exchanged(*faces)
    extra = (perm, inside, anchors.astype(jnp.int32), boreholes[:, None])
    part, ends, wx, wy, *along_z = inner_part(guess, near, extra, True, False, totals)
    residual, ends, wx, wy, *faces = sides_part(
        part, guess, far, ends, [wx, wy, perm, inside], True, False
    )
    weights = (wx, wy, *along_z)
    near, far = exchanged(*faces, ends)
    part, ends, total = inner_part(residual, near, weights, False, False, totals)
    once, ends, sums, *faces = sides_part(
        part, residual, far, ends, [wx, wy, total], False, False
    )
    near, far = exchanged(*faces, ends)
    part, total = inner_part(once, near, weights, False, True, totals)
    twice, sums = sides_part(part, once, far, None, [wx, wy, total, sums], False, True)
    mix = solve(*summed_but_last(sums))
    return tuple(combine(mix, guess, residual, once, twice))


def solution(mesh):
    placed = (P("strike", "dip", "layer"), P(), P(), P(None, "strike", "dip", "layer"))
    return jax.shard_map(
        shards,
        mesh=mesh,
        in_specs=placed,
        out_specs=(P(None, "strike", "dip", "layer"), P(None, "strike", "dip", "layer")),
        check_vma=False,
    )
```

```python
import functools

import jax
import jax.numpy as jnp
from jax import lax
from jax.experimental import pallas as pl
from jax.experimental.pallas import tpu as pltpu
from jax.sharding import PartitionSpec as P

LEAKAGE = 0.01
HIGHEST = lax.Precision.HIGHEST
F32 = jnp.float32
BF16 = jnp.bfloat16
VMEM_LIMIT = 24 * 1024 * 1024
AXES = ("strike", "dip", "layer")
VMEM = pl.BlockSpec(memory_space=pltpu.VMEM)
SMEM = pl.BlockSpec(memory_space=pltpu.SMEM)
HBM = pl.BlockSpec(memory_space=pltpu.HBM)


def params(**more):
    return pltpu.CompilerParams(vmem_limit_bytes=VMEM_LIMIT, **more)


def shaped(*shape):
    return pltpu.VMEM(shape, F32)


def lanes(rows):
    return lax.broadcasted_iota(jnp.int32, (rows, 128), 1)


def rows_of(count):
    return lax.broadcasted_iota(jnp.int32, (count, 128), 0)


def packed_ends(cells, y, into):
    turned = pltpu.roll(cells, 2 * y + 1, 1)
    lane = lanes(cells.shape[0])
    return jnp.where((lane == 2 * y) | (lane == 2 * y + 1), turned, into)


def place_x(tile, x, ref, plane, rows):
    turned = pltpu.roll(tile, (x % 4) * 32, 1)
    lane = lanes(tile.shape[0])
    mine = (lane // 32) == (x % 4)
    ref[plane, rows, :] = jnp.where(mine, turned, ref[plane, rows, :])


def pack_kernel(
    class_hbm, table_hbm, guess_hbm, field_ref, perm_ref, xlo, xhi, ylo, yhi, ends_ref,
    classes, table, guess, plane_sem, class_sem, table_sem,
):
    columns, nx, ny, nz = guess_hbm.shape

    def plane(x):
        return pltpu.make_async_copy(guess_hbm.at[:, x], guess.at[x], plane_sem.at[x])

    class_copy = pltpu.make_async_copy(class_hbm, classes, class_sem)
    table_copy = pltpu.make_async_copy(table_hbm, table, table_sem)
    table_copy.start()
    class_copy.start()
    for x in range(nx):
        plane(x).start()
    ends_ref[...] = jnp.zeros_like(ends_ref)
    for ref in (xlo, xhi, ylo, yhi):
        ref[ny] = jnp.zeros((columns, nz), F32)
    table_copy.wait()
    class_copy.wait()
    lane = lanes(ny)
    row = rows_of(ny)

    def permeability(x, carry):
        perm = jnp.zeros((ny, nz), F32)
        for level in range(table.shape[0]):
            perm = jnp.where(classes[x] == level, table[level], perm)
        perm_ref[x] = perm
        ylo[ny, pl.ds(x, 1), :] = perm[0:1]
        yhi[ny, pl.ds(x, 1), :] = perm[ny - 1 : ny]
        first = jnp.broadcast_to(perm[:, 0:1], (ny, nz))
        final = jnp.broadcast_to(perm[:, nz - 1 : nz], (ny, nz))
        both = jnp.where(lane == 2 * row, final, jnp.where(lane == 2 * row + 1, first, 0.0))
        edge = jnp.sum(both, axis=0, keepdims=True)
        place_x(edge, x, ends_ref, 4, pl.ds(x // 4, 1))
        return carry

    lax.fori_loop(0, nx, permeability, 0)
    xlo[ny, 0:ny, :] = perm_ref[0]
    xhi[ny, 0:ny, :] = perm_ref[nx - 1]

    def cells_of(x, carry):
        plane(x).wait()
        flat = guess.at[x].reshape(columns * ny, nz)
        ends = jnp.zeros((columns, nz), F32)
        for y in range(ny):
            cells = flat[pl.ds(y, columns, stride=ny), :]
            field_ref[x, y] = cells
            ends = packed_ends(cells, y, ends)
            if y == 0:
                ylo[x] = cells
            if y == ny - 1:
                yhi[x] = cells
        place_x(ends, x, ends_ref, x // 4, slice(None))
        return carry

    lax.fori_loop(0, nx, cells_of, 0)
    for y in range(ny):
        xlo[y] = field_ref[0, y]
        xhi[y] = field_ref[nx - 1, y]


def pack(perm_class, perm_table, start_guess):
    columns, nx, ny, nz = start_guess.shape
    face = shaped(ny + 1, columns, nz)
    return pl.pallas_call(
        pack_kernel,
        in_specs=[HBM] * 3,
        out_specs=[VMEM] * 7,
        out_shape=[
            shaped(nx, ny, columns, nz),
            shaped(nx, ny, nz),
            face,
            face,
            shaped(nx + 1, columns, nz),
            shaped(nx + 1, columns, nz),
            shaped(5, columns, nz),
        ],
        scratch_shapes=[
            pltpu.VMEM((nx, ny, nz), jnp.int32),
            pltpu.SMEM(perm_table.shape, F32),
            pltpu.VMEM((nx, columns, ny, nz), F32),
            pltpu.SemaphoreType.DMA((nx,)),
            pltpu.SemaphoreType.DMA(()),
            pltpu.SemaphoreType.DMA(()),
        ],
        compiler_params=pltpu.CompilerParams(vmem_limit_bytes=VMEM_LIMIT),
        name="pack_guess",
    )(perm_class, perm_table, start_guess)


def face_weight(center_k, beside_k):
    summed = center_k + beside_k
    divisor = jnp.where(summed > 0.0, summed, 1.0)
    return jnp.where(summed > 0.0, 2.0 * center_k * beside_k / divisor, 0.0)


def arrived(left, right, left_scale=None, right_scale=None):
    after = pltpu.roll(right, 127, 1)
    before = pltpu.roll(left, 1, 1)
    if left_scale is not None:
        after, before = after * right_scale, before * left_scale
    return jnp.where(lanes(left.shape[0]) % 2 == 0, after, before)


def inner_weights(perm_ref, inside, hz, wx, wy, wzm, wzp):
    nx, ny, nz = perm_ref.shape
    lane = lanes(ny)
    row = rows_of(ny)

    def at_x(x, carry):
        center = perm_ref[x]
        wx[x] = face_weight(center, perm_ref[jnp.maximum(x - 1, 0)])
        below = jnp.concatenate([center[:1], center[: ny - 1]], axis=0)
        wy[x, 0:ny, :] = face_weight(center, below)
        ends = arrived(
            hz[0][4, pl.ds(x // 4, 1), :], hz[1][4, pl.ds(x // 4, 1), :], inside[4], inside[5]
        )
        ends = jnp.broadcast_to(ends, (ny, nz))
        offset = (x % 4) * 32 + 2 * row
        after = jnp.sum(jnp.where(lane == offset, ends, 0.0), axis=1, keepdims=True)
        ahead = jnp.sum(jnp.where(lane == offset + 1, ends, 0.0), axis=1, keepdims=True)
        wzm[x] = face_weight(center, jnp.where(lane == 0, ahead, pltpu.roll(center, 1, 1)))
        wzp[x] = face_weight(center, jnp.where(lane == nz - 1, after, pltpu.roll(center, nz - 1, 1)))
        return carry

    lax.fori_loop(0, nx, at_x, 0)


def outer_weights(perm_ref, inside, hx, hy, wx, wy):
    nx, ny, nz = perm_ref.shape
    wx[0] = face_weight(perm_ref[0], hx[0][...] * inside[0])
    wx[nx] = face_weight(perm_ref[nx - 1], hx[1][...] * inside[1])
    low = jnp.concatenate([perm_ref[x, 0:1, :] for x in range(nx)], axis=0)
    high = jnp.concatenate([perm_ref[x, ny - 1 : ny, :] for x in range(nx)], axis=0)
    low = face_weight(low, hy[0][0:nx] * inside[2])
    high = face_weight(high, hy[1][0:nx] * inside[3])
    for x in range(nx):
        wy[x, 0:1, :] = low[x : x + 1]
        wy[x, ny : ny + 1, :] = high[x : x + 1]


def local_sources(boreholes, anchors, nx, ny, nz, total_y, total_z):
    cell = jnp.broadcast_to(boreholes, (boreholes.shape[0], nz))
    along_z = cell % total_z - anchors[2]
    along_y = (cell // total_z) % total_y - anchors[1]
    along_x = cell // (total_z * total_y) - anchors[0]
    inside = (along_x >= 0) & (along_x < nx) & (along_y >= 0) & (along_y < ny)
    matched = inside & (along_z == lanes(boreholes.shape[0]))
    return jnp.where(matched, along_x * ny + along_y, -1)


def inner_kernel(first, last, totals, *refs):
    refs = list(refs)
    take = lambda count: [refs.pop(0) for _ in range(count)]
    field, hzl, hzr = take(3)
    if first:
        perm, inside, anchors, boreholes = take(4)
    else:
        wx, wy, wzm, wzp = take(4)
    (out,) = take(1)
    if not last:
        (ends,) = take(1)
    if first:
        wx, wy, wzm, wzp = take(4)
    else:
        (total,) = take(1)
    (flux,) = take(1)
    nx, ny, columns, nz = field.shape
    if not last:
        ends[...] = jnp.zeros_like(ends)
    if first:
        inner_weights(perm, inside, (hzl, hzr), wx, wy, wzm, wzp)
        code = local_sources(boreholes[...], anchors, nx, ny, nz, totals[1], totals[2])
    else:
        total[...] = jnp.zeros_like(total)
    flux[...] = jnp.zeros_like(flux)
    lane = lanes(columns)

    def at_x(x, beside):
        block = lax.div(x, 4)
        beyond = arrived(hzl[block], hzr[block])
        beyond = pltpu.roll(beyond, lax.rem(128 - lax.rem(x, 4) * 32, 128), 1)
        center = field[x, 0]
        flux_y = None
        mine = jnp.zeros((columns, nz), F32)
        for y in range(ny):
            applied = LEAKAGE * center - flux[y]
            if beside is not None:
                flux_x = wx[x + 1, y : y + 1, :] * (center - beside[y])
                applied = applied + flux_x
                flux[y] = flux_x
            if flux_y is not None:
                applied = applied - flux_y
            if y + 1 < ny:
                following = field[x, y + 1]
                flux_y = wy[x, y + 1 : y + 2, :] * (center - following)
                applied = applied + flux_y
            edge = pltpu.roll(beyond, (128 - (2 * y + 1)) % 128, 1)
            after = jnp.where(lane == nz - 1, edge, pltpu.roll(center, nz - 1, 1))
            before = jnp.where(lane == 0, edge, pltpu.roll(center, 1, 1))
            applied = applied + wzp[x, y : y + 1, :] * (center - after)
            applied = applied + wzm[x, y : y + 1, :] * (center - before)
            if first:
                applied = jnp.where(code == x * ny + y, 1.0, 0.0) - applied
            out[x, y] = applied
            if not last:
                mine = packed_ends(applied, y, mine)
            center = following
        if not last:
            place_x(mine, x, ends, block, slice(None))
        if not first:
            left = split([jnp.concatenate([field[x, y] for y in range(ny)], axis=1)])
            right = split([jnp.concatenate([out[x, y] for y in range(ny)], axis=1)])
            total[...] += gram(left, jnp.concatenate([left, right], axis=0))

    def inner(x, carry):
        at_x(x, field.at[x + 1])
        return carry

    lax.fori_loop(0, nx - 1, inner, 0)
    at_x(jnp.int32(nx - 1), None)


def sides_kernel(first, last, *refs):
    refs = list(refs)
    take = lambda count: [refs.pop(0) for _ in range(count)]
    _, field, hxl, hxr, hyl, hyr = take(6)
    if not last:
        take(1)
    if first:
        take(2)
        perm, inside = take(2)
    else:
        wx, wy, total = take(3)
    if last:
        (earlier,) = take(1)
    (out,) = take(1)
    if not last:
        (ends,) = take(1)
    if first:
        wx, wy = take(2)
    else:
        (sums,) = take(1)
    if not last:
        xlo, xhi, ylo, yhi = take(4)
    nx, ny, columns, nz = field.shape
    lane = lanes(columns)
    if first:
        hx = (hxl.at[ny, 0:ny], hxr.at[ny, 0:ny])
        outer_weights(perm, inside, hx, (hyl.at[ny], hyr.at[ny]), wx, wy)

    added = None
    faces = (
        (hxl, [(0, y) for y in range(ny)], [(0, y) for y in range(ny)], wx),
        (hxr, [(nx - 1, y) for y in range(ny)], [(nx, y) for y in range(ny)], wx),
        (hyl, [(x, 0) for x in range(nx)], [(x, 0) for x in range(nx)], wy),
        (hyr, [(x, ny - 1) for x in range(nx)], [(x, ny) for x in range(nx)], wy),
    )
    for halo, rows, weight_rows, weight in faces:
        own, fluxes = [], []
        for place, ((x, y), (p, q)) in enumerate(zip(rows, weight_rows)):
            center = field[x, y]
            flux = weight[p, q : q + 1, :] * (center - halo[place])
            if first:
                out[x, y] -= flux
            else:
                out[x, y] += flux
                own.append(center)
                fluxes.append(flux)
        if not first:
            left = split([jnp.concatenate(own, axis=1)])
            right = split([jnp.concatenate(fluxes, axis=1)])
            part = gram(left, right)
            added = part if added is None else added + part
    if not last:
        for x in range(nx):
            tile = ends[x // 4]
            for y in range(ny):
                if x in (0, nx - 1) or y in (0, ny - 1):
                    tile = packed_ends(out[x, y], (x % 4) * 16 + y, tile)
            ends[x // 4] = tile
        for y in range(ny):
            xlo[y] = out[0, y]
            xhi[y] = out[nx - 1, y]
        for x in range(nx):
            ylo[x] = out[x, 0]
            yhi[x] = out[x, ny - 1]
    if not first:
        held = total[...]
        held = held[0:32] + held[32:64]
        held = held + pltpu.roll(held, 96, 1)
        held = jnp.where(lane < 32, held, pltpu.roll(held, 96, 1))
        fixed = added[0:32] + added[32:64]
        fixed = fixed[:, 0:32] + fixed[:, 32:64]
        fixed = jnp.concatenate([fixed, jnp.zeros((columns, 96), F32)], axis=1)
        held = jnp.where(lane < 32, held, held + pltpu.roll(fixed, 32, 1))
        if last:
            held = jnp.where(lane < 64, earlier[...], pltpu.roll(held, 64, 1))
        sums[...] = held


def split(fields):
    high = [field.astype(BF16) for field in fields]
    low = [(field - top.astype(F32)).astype(BF16) for field, top in zip(fields, high)]
    return jnp.concatenate(high + low, axis=0)


def gram(left, right):
    return lax.dot_general(left, right, (((1,), (1,)), ((), ())), preferred_element_type=F32)


def fold(products, fields):
    half = products.shape[0] // 2
    summed = products[:half] + products[half:]
    return summed[:, :half] + summed[:, half:]


def inner_part(field, halos, extra, first, last, totals):
    nx, ny, columns, nz = field.shape
    in_specs = [VMEM] * 3
    if first:
        in_specs += [VMEM, SMEM, SMEM, VMEM]
    else:
        in_specs += [VMEM] * 4
    out_shape = [shaped(nx, ny, columns, nz)]
    if not last:
        out_shape += [shaped(4, columns, nz)]
    if first:
        out_shape += [
            shaped(nx + 1, ny, nz),
            shaped(nx, ny + 8, nz),
            shaped(nx, ny, nz),
            shaped(nx, ny, nz),
        ]
    else:
        out_shape += [shaped(2 * columns, 4 * columns)]
    return pl.pallas_call(
        functools.partial(inner_kernel, first, last, totals),
        in_specs=in_specs,
        out_specs=[VMEM] * len(out_shape),
        out_shape=out_shape,
        scratch_shapes=[pltpu.VMEM((ny, columns, nz), F32)],
        compiler_params=params(),
        cost_estimate=pl.CostEstimate(
            flops=20 * field.size, bytes_accessed=6 * field.size * 4, transcendentals=0
        ),
        name="inner_first" if first else "inner_last" if last else "inner_next",
    )(field, *halos, *extra)


def sides_part(part, field, halos, ends, extra, first, last):
    nx, ny, columns, nz = field.shape
    operands = [part, field, *halos]
    if not last:
        operands += [ends]
    operands += extra
    in_specs = [VMEM] * len(operands)
    aliases = {0: 0}
    out_shape = [shaped(*part.shape)]
    if not last:
        aliases[6] = 1
        out_shape += [shaped(*ends.shape)]
    if first:
        in_specs[-1] = SMEM
        aliases[7] = 2
        aliases[8] = 3
        out_shape += [shaped(*extra[0].shape), shaped(*extra[1].shape)]
    else:
        out_shape += [shaped(columns, 128)]
    if not last:
        out_shape += [shaped(ny, columns, nz)] * 2 + [shaped(nx, columns, nz)] * 2
    return pl.pallas_call(
        functools.partial(sides_kernel, first, last),
        in_specs=in_specs,
        out_specs=[VMEM] * len(out_shape),
        out_shape=out_shape,
        input_output_aliases=aliases,
        compiler_params=params(),
        name="sides_first" if first else "sides_last" if last else "sides_next",
    )(*operands)


def exchanged(xlo, xhi, ylo, yhi, ends):
    ahead = lambda axis: [(i, (i + 1) % lax.axis_size(axis)) for i in range(lax.axis_size(axis))]
    back = lambda axis: [(j, i) for i, j in ahead(axis)]
    near = (
        lax.ppermute(ends, "layer", ahead("layer")),
        lax.ppermute(ends, "layer", back("layer")),
    )
    near, ylo, yhi = lax.optimization_barrier((near, ylo, yhi))
    far = (
        lax.ppermute(xhi, "strike", ahead("strike")),
        lax.ppermute(xlo, "strike", back("strike")),
        lax.ppermute(yhi, "dip", ahead("dip")),
        lax.ppermute(ylo, "dip", back("dip")),
    )
    return near, far


def dot(left, right, contract=(1, 0)):
    dims = (((contract[0],), (contract[1],)), ((), ()))
    return lax.dot_general(left, right, dims, precision=HIGHEST, preferred_element_type=F32)


def eliminate(tables):
    row = rows_of(32)
    for k in range(0, 32, 2):
        done = []
        for table in tables:
            one = jnp.broadcast_to(table[:, k : k + 1], table.shape)
            two = jnp.broadcast_to(table[:, k + 1 : k + 2], table.shape)
            a, b = one[k : k + 1], two[k : k + 1]
            c, d = one[k + 1 : k + 2], two[k + 1 : k + 2]
            scale = 1.0 / (a * d - b * c)
            upper, lower = table[k : k + 1], table[k + 1 : k + 2]
            first = (d * upper - b * lower) * scale
            second = (a * lower - c * upper) * scale
            rest = (table - one * first) - two * second
            done.append(jnp.where(row == k, first, jnp.where(row == k + 1, second, rest)))
        tables = done
    return tables


def solve_kernel(*refs):
    out_ref = refs[-1]
    sums = refs[0][...]
    for ref in refs[1:-1]:
        sums = sums + ref[...]
    lane = lanes(32)
    row = rows_of(32)
    unit = jnp.where(lane == row + 32, 1.0, 0.0)
    advance_table = jnp.where(lane < 32, pltpu.roll(sums, 96, 1), pltpu.roll(sums, 32, 1))
    norm_table = jnp.where(lane < 32, sums, unit)
    advance_table, norm_table = eliminate([advance_table, norm_table])
    norm = sums[:, 0:32]
    moment = sums[:, 32:64]
    square = sums[:, 64:96]
    cube = sums[:, 96:128]
    advance = advance_table[:, 32:64]
    inverse = norm_table[:, 32:64]
    turned = dot(square, advance)
    tripled = dot(dot(advance, cube, (0, 0)), advance)
    norm_next = dot(advance, turned, (0, 0)) - norm
    eye = jnp.where(lane[:, 0:32] == row[:, 0:32], 1.0, 0.0)
    mixing = eye + dot(inverse, norm_next)
    curvature = dot(mixing, dot(moment, mixing) - turned, (0, 0))
    curvature = curvature - dot(turned, mixing, (0, 0)) + tripled
    wide = jnp.concatenate([curvature, norm_next, jnp.zeros((32, 64), F32)], axis=1)
    (wide,) = eliminate([wide])
    later = wide[:, 32:64]
    taken = advance + dot(mixing, later)
    beyond = dot(advance, later)
    taken_t = taken.T
    beyond_t = beyond.T
    nothing = jnp.zeros((32, 32), F32)
    out_ref[0:32, :] = jnp.concatenate([taken_t, -beyond_t, nothing, nothing], axis=1)
    out_ref[32:64, :] = jnp.concatenate([nothing, -taken_t, beyond_t, nothing], axis=1)


def solve(parts):
    return pl.pallas_call(
        solve_kernel,
        in_specs=[VMEM] * len(parts),
        out_specs=VMEM,
        out_shape=shaped(64, 128),
        compiler_params=params(),
        name="solve_small",
    )(*parts)


def combine_kernel(
    mix_ref, guess_hbm, one_ref, two_ref, three_ref, solution_hbm, residual_hbm,
    guess, solution, residual, sem, guess_sem,
):
    nx, ny, columns, nz = one_ref.shape
    slots = solution.shape[0]

    def arriving(x):
        return pltpu.make_async_copy(guess_hbm.at[:, x], guess.at[x], guess_sem.at[x])

    def leaving(x):
        slot = lax.rem(x, slots)
        return (
            pltpu.make_async_copy(solution.at[slot], solution_hbm.at[:, x], sem.at[0, slot]),
            pltpu.make_async_copy(residual.at[slot], residual_hbm.at[:, x], sem.at[1, slot]),
        )

    for x in range(nx):
        arriving(x).start()
    mix = mix_ref[...]
    high = mix.astype(BF16)
    low = (mix - high.astype(F32)).astype(BF16)
    mixing = jnp.concatenate(
        [jnp.concatenate([high, high], axis=1), jnp.concatenate([low, low], axis=1)], axis=0
    )
    nothing = jnp.zeros((columns, 2 * nz), F32)

    def at_x(x, carry):
        slot = lax.rem(x, slots)

        @pl.when(x >= slots)
        def _():
            for copy in leaving(x - slots):
                copy.wait()

        arriving(x).wait()
        guess_rows = guess.at[x].reshape(columns * ny, nz)
        solution_rows = solution.at[slot].reshape(columns * ny, nz)
        residual_rows = residual.at[slot].reshape(columns * ny, nz)
        for y in range(0, ny, 2):
            fields = [
                jnp.concatenate([ref[x, y], ref[x, y + 1]], axis=1)
                for ref in (one_ref, two_ref, three_ref)
            ]
            halves = split(fields + [nothing])
            mixed = jnp.dot(mixing, halves, preferred_element_type=F32)
            mixed = mixed[0:64] + mixed[64:128]
            for step in range(2):
                rows = pl.ds(y + step, columns, stride=ny)
                part = mixed[:, step * nz : (step + 1) * nz]
                solution_rows[rows, :] = guess_rows[rows, :] + part[0:32]
                residual_rows[rows, :] = one_ref[x, y + step] + part[32:64]
        for copy in leaving(x):
            copy.start()
        return carry

    lax.fori_loop(0, nx, at_x, 0)
    for x in range(nx - slots, nx):
        for copy in leaving(jnp.int32(x)):
            copy.wait()


def combine(mix, guess, one, two, three):
    nx, ny, columns, nz = one.shape
    return pl.pallas_call(
        combine_kernel,
        in_specs=[VMEM, HBM, VMEM, VMEM, VMEM],
        out_specs=[HBM] * 2,
        out_shape=[jax.ShapeDtypeStruct((columns, nx, ny, nz), F32)] * 2,
        scratch_shapes=[
            pltpu.VMEM((nx, columns, ny, nz), F32),
            pltpu.VMEM((8, columns, ny, nz), F32),
            pltpu.VMEM((8, columns, ny, nz), F32),
            pltpu.SemaphoreType.DMA((2, 8)),
            pltpu.SemaphoreType.DMA((nx,)),
        ],
        compiler_params=pltpu.CompilerParams(vmem_limit_bytes=VMEM_LIMIT),
        name="combine_fields",
    )(mix, guess, one, two, three)


def swaps(axis, mask, stride=1):
    return [(i, i ^ (mask * stride)) for i in range(lax.axis_size(axis))]


def summed_but_last(values):
    groups = []
    for axis in AXES[::-1]:
        size, stride = lax.axis_size(axis), 1
        while size // stride > 4:
            values = values + lax.ppermute(values, axis, swaps(axis, 1, stride))
            stride *= 2
        groups.append((axis, stride))
    for place, (axis, stride) in enumerate(groups):
        others = [
            lax.ppermute(values, axis, swaps(axis, mask, stride))
            for mask in (1, 3, 2)
            if mask * stride < lax.axis_size(axis)
        ]
        if place + 1 < len(groups):
            for other in others:
                values = values + other
    return [values, *others]


def shards(perm_class, perm_table, boreholes, start_guess):
    columns, nx, ny, nz = start_guess.shape
    places = [lax.axis_index(axis) for axis in AXES]
    sizes = [lax.axis_size(axis) for axis in AXES]
    anchors = jnp.stack([place * size for place, size in zip(places, (nx, ny, nz))])
    totals = tuple(size * count for size, count in zip((nx, ny, nz), sizes))
    inside = []
    for place, size in zip(places, sizes):
        inside += [place > 0, place < size - 1]
    inside = jnp.stack(inside).astype(F32)

    perm_class, perm_table, start_guess = (
        pltpu.with_memory_space_constraint(held, pltpu.HBM)
        for held in (perm_class, perm_table, start_guess)
    )
    guess, perm, *faces = pack(perm_class, perm_table, start_guess)
    near, far = exchanged(*faces)
    extra = (perm, inside, anchors.astype(jnp.int32), boreholes[:, None])
    part, ends, wx, wy, *along_z = inner_part(guess, near, extra, True, False, totals)
    residual, ends, wx, wy, *faces = sides_part(
        part, guess, far, ends, [wx, wy, perm, inside], True, False
    )
    weights = (wx, wy, *along_z)
    near, far = exchanged(*faces, ends)
    part, ends, total = inner_part(residual, near, weights, False, False, totals)
    once, ends, sums, *faces = sides_part(
        part, residual, far, ends, [wx, wy, total], False, False
    )
    near, far = exchanged(*faces, ends)
    part, total = inner_part(once, near, weights, False, True, totals)
    twice, sums = sides_part(part, once, far, None, [wx, wy, total, sums], False, True)
    mix = solve(summed_but_last(sums))
    return tuple(combine(mix, start_guess, residual, once, twice))


def solution(mesh):
    placed = (P("strike", "dip", "layer"), P(), P(), P(None, "strike", "dip", "layer"))
    return jax.shard_map(
        shards,
        mesh=mesh,
        in_specs=placed,
        out_specs=(P(None, "strike", "dip", "layer"), P(None, "strike", "dip", "layer")),
        check_vma=False,
    )
```

```python
import functools

import jax
import jax.numpy as jnp
from jax import lax
from jax.experimental import pallas as pl
from jax.experimental.pallas import tpu as pltpu
from jax.sharding import PartitionSpec as P

LEAKAGE = 0.01
HIGHEST = lax.Precision.HIGHEST
F32 = jnp.float32
BF16 = jnp.bfloat16
VMEM_LIMIT = 24 * 1024 * 1024
AXES = ("strike", "dip", "layer")
VMEM = pl.BlockSpec(memory_space=pltpu.VMEM)
SMEM = pl.BlockSpec(memory_space=pltpu.SMEM)
HBM = pl.BlockSpec(memory_space=pltpu.HBM)


def params(**more):
    return pltpu.CompilerParams(vmem_limit_bytes=VMEM_LIMIT, **more)


def shaped(*shape):
    return pltpu.VMEM(shape, F32)


def lanes(rows):
    return lax.broadcasted_iota(jnp.int32, (rows, 128), 1)


def rows_of(count):
    return lax.broadcasted_iota(jnp.int32, (count, 128), 0)


def packed_ends(cells, y, into):
    turned = pltpu.roll(cells, 2 * y + 1, 1)
    lane = lanes(cells.shape[0])
    return jnp.where((lane == 2 * y) | (lane == 2 * y + 1), turned, into)


def place_x(tile, x, ref, plane, rows):
    turned = pltpu.roll(tile, (x % 4) * 32, 1)
    lane = lanes(tile.shape[0])
    mine = (lane // 32) == (x % 4)
    ref[plane, rows, :] = jnp.where(mine, turned, ref[plane, rows, :])


def pack_kernel(
    class_hbm, table_hbm, guess_hbm, field_hbm, perm_ref, xlo, xhi, ylo, yhi, ends_ref,
    classes, table, guess, field_ref, plane_sem, field_sem, class_sem, table_sem,
):
    columns, nx, ny, nz = guess_hbm.shape

    def plane(x):
        return pltpu.make_async_copy(guess_hbm.at[:, x], guess.at[x], plane_sem.at[x])

    def leaving(x):
        return pltpu.make_async_copy(field_ref.at[x], field_hbm.at[x], field_sem.at[x])

    class_copy = pltpu.make_async_copy(class_hbm, classes, class_sem)
    table_copy = pltpu.make_async_copy(table_hbm, table, table_sem)
    table_copy.start()
    class_copy.start()
    for x in range(nx):
        plane(x).start()
    ends_ref[...] = jnp.zeros_like(ends_ref)
    for ref in (xlo, xhi, ylo, yhi):
        ref[ny] = jnp.zeros((columns, nz), F32)
    table_copy.wait()
    class_copy.wait()
    lane = lanes(ny)
    row = rows_of(ny)

    def permeability(x):
        perm = jnp.zeros((ny, nz), F32)
        for level in range(table.shape[0]):
            perm = jnp.where(classes[x] == level, table[level], perm)
        perm_ref[x] = perm
        ylo[ny, pl.ds(x, 1), :] = perm[0:1]
        yhi[ny, pl.ds(x, 1), :] = perm[ny - 1 : ny]
        first = jnp.broadcast_to(perm[:, 0:1], (ny, nz))
        final = jnp.broadcast_to(perm[:, nz - 1 : nz], (ny, nz))
        both = jnp.where(lane == 2 * row, final, jnp.where(lane == 2 * row + 1, first, 0.0))
        edge = jnp.sum(both, axis=0, keepdims=True)
        return jnp.where((lanes(1) // 32) == x % 4, pltpu.roll(edge, (x % 4) * 32, 1), 0.0)

    def four(block, carry):
        edges = [permeability(4 * block + step) for step in range(4)]
        ends_ref[4, pl.ds(block, 1), :] = (edges[0] + edges[1]) + (edges[2] + edges[3])
        return carry

    lax.fori_loop(0, nx // 4, four, 0)
    xlo[ny, 0:ny, :] = perm_ref[0]
    xhi[ny, 0:ny, :] = perm_ref[nx - 1]

    def cells_of(pair, carry):
        for step in range(2):
            plane(2 * pair + step).wait()
        for step in range(2):
            x = 2 * pair + step
            flat = guess.at[x].reshape(columns * ny, nz)
            ends = jnp.zeros((columns, nz), F32)
            for y in range(ny):
                cells = flat[pl.ds(y, columns, stride=ny), :]
                field_ref[x, y] = cells
                ends = packed_ends(cells, y, ends)
                if y == 0:
                    ylo[x] = cells
                if y == ny - 1:
                    yhi[x] = cells
            place_x(ends, x, ends_ref, x // 4, slice(None))
            leaving(x).start()
        return carry

    lax.fori_loop(0, nx // 2, cells_of, 0)
    for y in range(ny):
        xlo[y] = field_ref[0, y]
        xhi[y] = field_ref[nx - 1, y]
    for x in range(nx):
        leaving(x).wait()


def pack(perm_class, perm_table, start_guess):
    columns, nx, ny, nz = start_guess.shape
    face = shaped(ny + 1, columns, nz)
    return pl.pallas_call(
        pack_kernel,
        in_specs=[HBM] * 3,
        out_specs=[HBM] + [VMEM] * 6,
        out_shape=[
            pltpu.HBM((nx, ny, columns, nz), F32),
            shaped(nx, ny, nz),
            face,
            face,
            shaped(nx + 1, columns, nz),
            shaped(nx + 1, columns, nz),
            shaped(5, columns, nz),
        ],
        scratch_shapes=[
            pltpu.VMEM((nx, ny, nz), jnp.int32),
            pltpu.SMEM(perm_table.shape, F32),
            pltpu.VMEM((nx, columns, ny, nz), F32),
            pltpu.VMEM((nx, ny, columns, nz), F32),
            pltpu.SemaphoreType.DMA((nx,)),
            pltpu.SemaphoreType.DMA((nx,)),
            pltpu.SemaphoreType.DMA(()),
            pltpu.SemaphoreType.DMA(()),
        ],
        compiler_params=pltpu.CompilerParams(vmem_limit_bytes=VMEM_LIMIT),
        name="pack_guess",
    )(perm_class, perm_table, start_guess)


def face_weight(center_k, beside_k):
    summed = center_k + beside_k
    divisor = jnp.where(summed > 0.0, summed, 1.0)
    return jnp.where(summed > 0.0, 2.0 * center_k * beside_k / divisor, 0.0)


def arrived(left, right, left_scale=None, right_scale=None):
    after = pltpu.roll(right, 127, 1)
    before = pltpu.roll(left, 1, 1)
    if left_scale is not None:
        after, before = after * right_scale, before * left_scale
    return jnp.where(lanes(left.shape[0]) % 2 == 0, after, before)


def inner_weights(perm_ref, inside, hz, wx, wy, wzm, wzp, wze):
    nx, ny, nz = perm_ref.shape
    lane = lanes(ny)
    row = rows_of(ny)

    def at_x(x):
        center = perm_ref[x]
        wx[x] = face_weight(center, perm_ref[jnp.maximum(x - 1, 0)])
        below = jnp.concatenate([center[:1], center[: ny - 1]], axis=0)
        wy[x, 0:ny, :] = face_weight(center, below)
        ends = arrived(
            hz[0][4, pl.ds(x // 4, 1), :], hz[1][4, pl.ds(x // 4, 1), :], inside[4:5], inside[5:6]
        )
        ends = jnp.broadcast_to(ends, (ny, nz))
        offset = (x % 4) * 32 + 2 * row
        after = jnp.sum(jnp.where(lane == offset, ends, 0.0), axis=1, keepdims=True)
        ahead = jnp.sum(jnp.where(lane == offset + 1, ends, 0.0), axis=1, keepdims=True)
        down = face_weight(center, jnp.where(lane == 0, ahead, pltpu.roll(center, 1, 1)))
        up = face_weight(center, jnp.where(lane == nz - 1, after, pltpu.roll(center, nz - 1, 1)))
        wzm[x] = down
        wzp[x] = up
        first = jnp.broadcast_to(down[:, 0:1], (ny, nz))
        final = jnp.broadcast_to(up[:, nz - 1 : nz], (ny, nz))
        both = jnp.where(lane == 2 * row, final, jnp.where(lane == 2 * row + 1, first, 0.0))
        return jnp.sum(both, axis=0, keepdims=True)

    def at_four(block, carry):
        edges = [at_x(4 * block + step) for step in range(4)]
        for step in range(4):
            wze[pl.ds(4 * block + step, 1), :] = edges[step]
        return carry

    lax.fori_loop(0, nx // 4, at_four, 0)


def outer_weights(perm_ref, inside, hx, hy, wx, wy):
    nx, ny, nz = perm_ref.shape
    wx[0] = face_weight(perm_ref[0], hx[0][...] * inside[0:1])
    wx[nx] = face_weight(perm_ref[nx - 1], hx[1][...] * inside[1:2])
    low = jnp.concatenate([perm_ref[x, 0:1, :] for x in range(nx)], axis=0)
    high = jnp.concatenate([perm_ref[x, ny - 1 : ny, :] for x in range(nx)], axis=0)
    low = face_weight(low, hy[0][0:nx] * inside[2:3])
    high = face_weight(high, hy[1][0:nx] * inside[3:4])
    for x in range(nx):
        wy[x, 0:1, :] = low[x : x + 1]
        wy[x, ny : ny + 1, :] = high[x : x + 1]


def local_sources(boreholes, anchors, nx, ny, nz, total_y, total_z):
    cell = jnp.broadcast_to(boreholes, (boreholes.shape[0], nz))
    along_z = cell % total_z - anchors[2]
    along_y = (cell // total_z) % total_y - anchors[1]
    along_x = cell // (total_z * total_y) - anchors[0]
    inside = (along_x >= 0) & (along_x < nx) & (along_y >= 0) & (along_y < ny)
    matched = inside & (along_z == lanes(boreholes.shape[0]))
    return jnp.where(matched, along_x * ny + along_y, -1)


def difference_matrix(matrix):
    size = matrix.shape[0] // 2
    source = lax.broadcasted_iota(jnp.int32, matrix.shape, 0) % size
    target = lax.broadcasted_iota(jnp.int32, matrix.shape, 1)
    beside = jnp.where(target < size, target + 1, target - size - 1)
    same = jnp.where(source == target % size, 1.0, 0.0)
    matrix[...] = (same - jnp.where(source == beside, 1.0, 0.0)).astype(BF16)


def first_kernel(
    away, hzl, hzr, perm, inside, code, out, ends, wx, wy, wzm, wzp, wze, flux, field, plane_sem
):
    nx, ny, columns, nz = field.shape

    def plane(x):
        return pltpu.make_async_copy(away.at[x], field.at[x], plane_sem.at[x])

    for x in range(nx):
        plane(x).start()
    ends[...] = jnp.zeros_like(ends)
    inner_weights(perm, inside, (hzl, hzr), wx, wy, wzm, wzp, wze)
    flux[...] = jnp.zeros_like(flux)
    plane(0).wait()

    def at_x(x, beside):
        block = x // 4
        beyond = arrived(hzl[block], hzr[block])
        beyond = pltpu.roll(beyond, (128 - (x % 4) * 32) % 128, 1)
        lane = lanes(columns)
        center = field[x, 0]
        flux_y = None
        mine = jnp.zeros((columns, nz), F32)
        for y in range(ny):
            applied = LEAKAGE * center - flux[y]
            if beside is not None:
                flux_x = wx[x + 1, y : y + 1, :] * (center - beside[y])
                applied = applied + flux_x
                flux[y] = flux_x
            if flux_y is not None:
                applied = applied - flux_y
            if y + 1 < ny:
                following = field[x, y + 1]
                flux_y = wy[x, y + 1 : y + 2, :] * (center - following)
                applied = applied + flux_y
            edge = pltpu.roll(beyond, (128 - (2 * y + 1)) % 128, 1)
            after = jnp.where(lane == nz - 1, edge, pltpu.roll(center, nz - 1, 1))
            before = jnp.where(lane == 0, edge, pltpu.roll(center, 1, 1))
            applied = applied + wzp[x, y : y + 1, :] * (center - after)
            applied = applied + wzm[x, y : y + 1, :] * (center - before)
            applied = jnp.where(code[...] == x * ny + y, 1.0, 0.0) - applied
            out[x, y] = applied
            mine = packed_ends(applied, y, mine)
            center = following
        place_x(mine, x, ends, block, slice(None))

    def inner(x, carry):
        plane(x + 1).wait()
        at_x(x, field.at[x + 1])
        return carry

    lax.fori_loop(0, nx - 1, inner, 0)
    at_x(nx - 1, None)


def inner_kernel(last, *refs):
    refs = list(refs)
    take = lambda count: [refs.pop(0) for _ in range(count)]
    field, hzl, hzr, wx, wy, wzm, wzp, wze, out = take(9)
    if not last:
        (ends,) = take(1)
    total, flux, matrix, even, odd, even_halves, odd_halves = take(7)
    nx, ny, columns, nz = field.shape
    if not last:
        ends[...] = jnp.zeros_like(ends)
    difference_matrix(matrix)
    total[...] = jnp.zeros_like(total)
    flux[...] = jnp.zeros_like(flux)

    def differences(x, across, halves):
        plane = field[x].reshape(ny * columns, nz)
        high = plane.astype(BF16)
        low = (plane - high.astype(F32)).astype(BF16)
        both = jnp.concatenate([high, low], axis=1)
        halves[...] = both
        across[...] = jnp.dot(both, matrix[...], preferred_element_type=F32)

    def products(x, halves):
        left = jnp.concatenate(
            [
                jnp.concatenate(
                    [halves[y * columns : (y + 1) * columns, half] for y in range(ny)], axis=1
                )
                for half in (slice(0, nz), slice(nz, 2 * nz))
            ],
            axis=0,
        )
        right = split([jnp.concatenate([out[x, y] for y in range(ny)], axis=1)])
        total[...] += gram(left, jnp.concatenate([left, right], axis=0))

    def stencil(x, across, beside):
        block = x // 4
        beyond = arrived(hzl[block], hzr[block])
        beyond = pltpu.roll(beyond, (128 - (x % 4) * 32) % 128, 1)
        beyond = beyond * wze[pl.ds(x, 1), :]
        lane = lanes(columns)
        outer = (lane == 0) | (lane == nz - 1)
        center = field[x, 0]
        flux_y = None
        mine = jnp.zeros((columns, nz), F32)
        for y in range(ny):
            rows = slice(y * columns, (y + 1) * columns)
            applied = LEAKAGE * center - flux[y]
            if beside is not None:
                flux_x = wx[x + 1, y : y + 1, :] * (center - beside[y])
                applied = applied + flux_x
                flux[y] = flux_x
            if flux_y is not None:
                applied = applied - flux_y
            if y + 1 < ny:
                following = field[x, y + 1]
                flux_y = wy[x, y + 1 : y + 2, :] * (center - following)
                applied = applied + flux_y
            applied = applied + wzp[x, y : y + 1, :] * across[rows, 0:nz]
            applied = applied + wzm[x, y : y + 1, :] * across[rows, nz : 2 * nz]
            edge = pltpu.roll(beyond, (128 - (2 * y + 1)) % 128, 1)
            applied = applied - jnp.where(outer, edge, 0.0)
            out[x, y] = applied
            if not last:
                mine = packed_ends(applied, y, mine)
            center = following
        if not last:
            place_x(mine, x, ends, block, slice(None))

    def step(x, here, there, halves):
        products(x - 1, halves)
        differences(x + 1, there, halves)
        stencil(x, here, field.at[x + 1])

    def pair(place, carry):
        step(2 * place + 1, odd, even, even_halves)
        step(2 * place + 2, even, odd, odd_halves)
        return carry

    differences(0, even, even_halves)
    differences(1, odd, odd_halves)
    stencil(0, even, field.at[1])
    lax.fori_loop(0, nx // 2 - 1, pair, 0)
    products(nx - 2, even_halves)
    stencil(nx - 1, odd, None)
    products(nx - 1, odd_halves)


def sides_kernel(first, last, *refs):
    refs = list(refs)
    take = lambda count: [refs.pop(0) for _ in range(count)]
    part = take(1)[0]
    if first:
        own_faces = take(4)
    else:
        (field,) = take(1)
    hxl, hxr, hyl, hyr = take(4)
    if not last:
        take(1)
    if first:
        take(2)
        perm, inside = take(2)
    else:
        wx, wy, total = take(3)
    if last:
        (earlier,) = take(1)
    (out,) = take(1)
    if not last:
        (ends,) = take(1)
    if first:
        wx, wy = take(2)
    else:
        (sums,) = take(1)
    if not last:
        xlo, xhi, ylo, yhi = take(4)
    nx, ny, columns, nz = part.shape
    lane = lanes(columns)
    if first:
        hx = (hxl.at[ny, 0:ny], hxr.at[ny, 0:ny])
        outer_weights(perm, inside, hx, (hyl.at[ny], hyr.at[ny]), wx, wy)

    added = None
    faces = (
        (hxl, [(0, y) for y in range(ny)], [(0, y) for y in range(ny)], wx),
        (hxr, [(nx - 1, y) for y in range(ny)], [(nx, y) for y in range(ny)], wx),
        (hyl, [(x, 0) for x in range(nx)], [(x, 0) for x in range(nx)], wy),
        (hyr, [(x, ny - 1) for x in range(nx)], [(x, ny) for x in range(nx)], wy),
    )
    for side, (halo, rows, weight_rows, weight) in enumerate(faces):
        own, fluxes = [], []
        for place, ((x, y), (p, q)) in enumerate(zip(rows, weight_rows)):
            center = own_faces[side][place] if first else field[x, y]
            flux = weight[p, q : q + 1, :] * (center - halo[place])
            if first:
                out[x, y] -= flux
            else:
                out[x, y] += flux
                own.append(center)
                fluxes.append(flux)
        if not first:
            left = split([jnp.concatenate(own, axis=1)])
            right = split([jnp.concatenate(fluxes, axis=1)])
            part = gram(left, right)
            added = part if added is None else added + part
    if not last:
        for x in range(nx):
            tile = ends[x // 4]
            for y in range(ny):
                if x in (0, nx - 1) or y in (0, ny - 1):
                    tile = packed_ends(out[x, y], (x % 4) * 16 + y, tile)
            ends[x // 4] = tile
        for y in range(ny):
            xlo[y] = out[0, y]
            xhi[y] = out[nx - 1, y]
        for x in range(nx):
            ylo[x] = out[x, 0]
            yhi[x] = out[x, ny - 1]
    if not first:
        held = total[...]
        held = held[0:32] + held[32:64]
        held = held + pltpu.roll(held, 96, 1)
        held = jnp.where(lane < 32, held, pltpu.roll(held, 96, 1))
        fixed = added[0:32] + added[32:64]
        fixed = fixed[:, 0:32] + fixed[:, 32:64]
        fixed = jnp.concatenate([fixed, jnp.zeros((columns, 96), F32)], axis=1)
        held = jnp.where(lane < 32, held, held + pltpu.roll(fixed, 32, 1))
        if last:
            held = jnp.where(lane < 64, earlier[...], pltpu.roll(held, 64, 1))
        sums[...] = held


def split(fields):
    high = [field.astype(BF16) for field in fields]
    low = [(field - top.astype(F32)).astype(BF16) for field, top in zip(fields, high)]
    return jnp.concatenate(high + low, axis=0)


def gram(left, right):
    return lax.dot_general(left, right, (((1,), (1,)), ((), ())), preferred_element_type=F32)


def fold(products, fields):
    half = products.shape[0] // 2
    summed = products[:half] + products[half:]
    return summed[:, :half] + summed[:, half:]


def inner_part(field, halos, extra, first, last):
    nx, ny, columns, nz = field.shape
    in_specs = [HBM if first else VMEM] + [VMEM] * (len(halos) + len(extra))
    scratch = [pltpu.VMEM((ny, columns, nz), F32)]
    out_shape = [shaped(nx, ny, columns, nz)]
    if not last:
        out_shape += [shaped(4, columns, nz)]
    if first:
        scratch += [pltpu.VMEM(field.shape, F32), pltpu.SemaphoreType.DMA((nx,))]
        out_shape += [
            shaped(nx + 1, ny, nz),
            shaped(nx, ny + 8, nz),
            shaped(nx, ny, nz),
            shaped(nx, ny, nz),
            shaped(nx, nz),
        ]
    else:
        scratch += [pltpu.VMEM((2 * nz, 2 * nz), BF16)]
        scratch += [pltpu.VMEM((ny * columns, 2 * nz), F32)] * 2
        scratch += [pltpu.VMEM((ny * columns, 2 * nz), BF16)] * 2
        out_shape += [shaped(2 * columns, 4 * columns)]
    return pl.pallas_call(
        first_kernel if first else functools.partial(inner_kernel, last),
        in_specs=in_specs,
        out_specs=[VMEM] * len(out_shape),
        out_shape=out_shape,
        scratch_shapes=scratch,
        compiler_params=params(),
        cost_estimate=pl.CostEstimate(
            flops=20 * field.size, bytes_accessed=6 * field.size * 4, transcendentals=0
        ),
        name="inner_first" if first else "inner_last" if last else "inner_next",
    )(field, *halos, *extra)


def sides_part(part, own, halos, ends, extra, first, last):
    nx, ny, columns, nz = part.shape
    operands = [part, *own, *halos]
    place = len(operands)
    if not last:
        operands += [ends]
    operands += extra
    in_specs = [VMEM] * len(operands)
    aliases = {0: 0}
    out_shape = [shaped(*part.shape)]
    if not last:
        aliases[place] = 1
        out_shape += [shaped(*ends.shape)]
    if first:
        aliases[place + 1] = 2
        aliases[place + 2] = 3
        out_shape += [shaped(*extra[0].shape), shaped(*extra[1].shape)]
    else:
        out_shape += [shaped(columns, 128)]
    if not last:
        out_shape += [shaped(ny, columns, nz)] * 2 + [shaped(nx, columns, nz)] * 2
    return pl.pallas_call(
        functools.partial(sides_kernel, first, last),
        in_specs=in_specs,
        out_specs=[VMEM] * len(out_shape),
        out_shape=out_shape,
        input_output_aliases=aliases,
        compiler_params=params(),
        name="sides_first" if first else "sides_last" if last else "sides_next",
    )(*operands)


def exchanged(xlo, xhi, ylo, yhi, ends):
    ahead = lambda axis: [(i, (i + 1) % lax.axis_size(axis)) for i in range(lax.axis_size(axis))]
    back = lambda axis: [(j, i) for i, j in ahead(axis)]
    near = (
        lax.ppermute(ends, "layer", ahead("layer")),
        lax.ppermute(ends, "layer", back("layer")),
    )
    near, ylo, yhi = lax.optimization_barrier((near, ylo, yhi))
    far = (
        lax.ppermute(xhi, "strike", ahead("strike")),
        lax.ppermute(xlo, "strike", back("strike")),
        lax.ppermute(yhi, "dip", ahead("dip")),
        lax.ppermute(ylo, "dip", back("dip")),
    )
    return near, far


def dot(left, right, contract=(1, 0)):
    dims = (((contract[0],), (contract[1],)), ((), ()))
    return lax.dot_general(left, right, dims, precision=HIGHEST, preferred_element_type=F32)


def eliminate(tables):
    row = rows_of(32)
    for k in range(0, 32, 2):
        done = []
        for table in tables:
            one = jnp.broadcast_to(table[:, k : k + 1], table.shape)
            two = jnp.broadcast_to(table[:, k + 1 : k + 2], table.shape)
            a, b = one[k : k + 1], two[k : k + 1]
            c, d = one[k + 1 : k + 2], two[k + 1 : k + 2]
            scale = 1.0 / (a * d - b * c)
            upper, lower = table[k : k + 1], table[k + 1 : k + 2]
            first = (d * upper - b * lower) * scale
            second = (a * lower - c * upper) * scale
            rest = (table - one * first) - two * second
            done.append(jnp.where(row == k, first, jnp.where(row == k + 1, second, rest)))
        tables = done
    return tables


def solve_kernel(*refs):
    out_ref = refs[-1]
    sums = refs[0][...]
    for ref in refs[1:-1]:
        sums = sums + ref[...]
    lane = lanes(32)
    row = rows_of(32)
    unit = jnp.where(lane == row + 32, 1.0, 0.0)
    advance_table = jnp.where(lane < 32, pltpu.roll(sums, 96, 1), pltpu.roll(sums, 32, 1))
    norm_table = jnp.where(lane < 32, sums, unit)
    advance_table, norm_table = eliminate([advance_table, norm_table])
    norm = sums[:, 0:32]
    moment = sums[:, 32:64]
    square = sums[:, 64:96]
    cube = sums[:, 96:128]
    advance = advance_table[:, 32:64]
    inverse = norm_table[:, 32:64]
    turned = dot(square, advance)
    tripled = dot(dot(advance, cube, (0, 0)), advance)
    norm_next = dot(advance, turned, (0, 0)) - norm
    eye = jnp.where(lane[:, 0:32] == row[:, 0:32], 1.0, 0.0)
    mixing = eye + dot(inverse, norm_next)
    curvature = dot(mixing, dot(moment, mixing) - turned, (0, 0))
    curvature = curvature - dot(turned, mixing, (0, 0)) + tripled
    wide = jnp.concatenate([curvature, norm_next, jnp.zeros((32, 64), F32)], axis=1)
    (wide,) = eliminate([wide])
    later = wide[:, 32:64]
    taken = advance + dot(mixing, later)
    beyond = dot(advance, later)
    taken_t = taken.T
    beyond_t = beyond.T
    nothing = jnp.zeros((32, 32), F32)
    out_ref[0:32, :] = jnp.concatenate([taken_t, -beyond_t, nothing, nothing], axis=1)
    out_ref[32:64, :] = jnp.concatenate([nothing, -taken_t, beyond_t, nothing], axis=1)


def solve(parts):
    return pl.pallas_call(
        solve_kernel,
        in_specs=[VMEM] * len(parts),
        out_specs=VMEM,
        out_shape=shaped(64, 128),
        compiler_params=params(),
        name="solve_small",
    )(*parts)


def combine_kernel(
    mix_ref, guess_hbm, one_ref, two_ref, three_ref, solution_hbm, residual_hbm,
    guess_ref, solution, residual, sem, guess_sem,
):
    nx, ny, columns, nz = guess_ref.shape
    slots = solution.shape[0]

    def arriving(x):
        return pltpu.make_async_copy(guess_hbm.at[x], guess_ref.at[x], guess_sem.at[x])

    for x in range(nx):
        arriving(x).start()
    mix = mix_ref[...]
    high = mix.astype(BF16)
    low = (mix - high.astype(F32)).astype(BF16)
    mixing = jnp.concatenate(
        [jnp.concatenate([high, high], axis=1), jnp.concatenate([low, low], axis=1)], axis=0
    )
    nothing = jnp.zeros((columns, 2 * nz), F32)

    def leaving(x):
        slot = lax.rem(x, slots)
        return (
            pltpu.make_async_copy(solution.at[slot], solution_hbm.at[:, x], sem.at[0, slot]),
            pltpu.make_async_copy(residual.at[slot], residual_hbm.at[:, x], sem.at[1, slot]),
        )

    def at_x(x, carry):
        slot = lax.rem(x, slots)

        @pl.when(x >= slots)
        def _():
            for copy in leaving(x - slots):
                copy.wait()

        arriving(x).wait()
        solution_rows = solution.at[slot].reshape(columns * ny, nz)
        residual_rows = residual.at[slot].reshape(columns * ny, nz)
        for y in range(0, ny, 2):
            fields = [
                jnp.concatenate([ref[x, y], ref[x, y + 1]], axis=1)
                for ref in (one_ref, two_ref, three_ref)
            ]
            halves = split(fields + [nothing])
            mixed = jnp.dot(mixing, halves, preferred_element_type=F32)
            mixed = mixed[0:64] + mixed[64:128]
            for step in range(2):
                rows = pl.ds(y + step, columns, stride=ny)
                part = mixed[:, step * nz : (step + 1) * nz]
                solution_rows[rows, :] = guess_ref[x, y + step] + part[0:32]
                residual_rows[rows, :] = one_ref[x, y + step] + part[32:64]
        for copy in leaving(x):
            copy.start()
        return carry

    lax.fori_loop(0, nx, at_x, 0)
    for x in range(nx - slots, nx):
        for copy in leaving(jnp.int32(x)):
            copy.wait()


def combine(mix, guess, one, two, three):
    nx, ny, columns, nz = guess.shape
    return pl.pallas_call(
        combine_kernel,
        in_specs=[VMEM, HBM] + [VMEM] * 3,
        out_specs=[HBM] * 2,
        out_shape=[jax.ShapeDtypeStruct((columns, nx, ny, nz), F32)] * 2,
        scratch_shapes=[
            pltpu.VMEM(guess.shape, F32),
            pltpu.VMEM((8, columns, ny, nz), F32),
            pltpu.VMEM((8, columns, ny, nz), F32),
            pltpu.SemaphoreType.DMA((2, 8)),
            pltpu.SemaphoreType.DMA((nx,)),
        ],
        compiler_params=params(),
        name="combine_fields",
    )(mix, guess, one, two, three)


def swaps(axis, mask, stride=1):
    return [(i, i ^ (mask * stride)) for i in range(lax.axis_size(axis))]


def summed_but_last(values):
    groups = []
    for axis in AXES[::-1]:
        size, stride = lax.axis_size(axis), 1
        while size // stride > 4:
            values = values + lax.ppermute(values, axis, swaps(axis, 1, stride))
            stride *= 2
        groups.append((axis, stride))
    for place, (axis, stride) in enumerate(groups):
        others = [
            lax.ppermute(values, axis, swaps(axis, mask, stride))
            for mask in (1, 3, 2)
            if mask * stride < lax.axis_size(axis)
        ]
        if place + 1 < len(groups):
            for other in others:
                values = values + other
    return [values, *others]


def shards(perm_class, perm_table, boreholes, start_guess):
    columns, nx, ny, nz = start_guess.shape
    places = [lax.axis_index(axis) for axis in AXES]
    sizes = [lax.axis_size(axis) for axis in AXES]
    anchors = [place * size for place, size in zip(places, (nx, ny, nz))]
    totals = tuple(size * count for size, count in zip((nx, ny, nz), sizes))
    inside = []
    for place, size in zip(places, sizes):
        inside += [place > 0, place < size - 1]
    inside = jnp.broadcast_to(jnp.stack(inside + inside[:2]).astype(F32)[:, None], (8, nz))

    in_hbm = [
        pltpu.with_memory_space_constraint(held, pltpu.HBM)
        for held in (perm_class, perm_table, start_guess)
    ]
    guess, perm, *faces = pack(*in_hbm)
    guess = pltpu.with_memory_space_constraint(guess, pltpu.HBM)
    near, far = exchanged(*faces)
    code = local_sources(boreholes[:, None], anchors, nx, ny, nz, totals[1], totals[2])
    extra = (perm, inside, code)
    part, ends, wx, wy, *along_z = inner_part(guess, near, extra, True, False)
    residual, ends, wx, wy, *faces = sides_part(
        part, faces[:4], far, ends, [wx, wy, perm, inside], True, False
    )
    weights = (wx, wy, *along_z)
    near, far = exchanged(*faces, ends)
    part, ends, total = inner_part(residual, near, weights, False, False)
    once, ends, sums, *faces = sides_part(
        part, [residual], far, ends, [wx, wy, total], False, False
    )
    near, far = exchanged(*faces, ends)
    part, total = inner_part(once, near, weights, False, True)
    twice, sums = sides_part(part, [once], far, None, [wx, wy, total, sums], False, True)
    mix = solve(summed_but_last(sums))
    return tuple(combine(mix, guess, residual, once, twice))


def solution(mesh):
    placed = (P("strike", "dip", "layer"), P(), P(), P(None, "strike", "dip", "layer"))
    return jax.shard_map(
        shards,
        mesh=mesh,
        in_specs=placed,
        out_specs=(P(None, "strike", "dip", "layer"), P(None, "strike", "dip", "layer")),
        check_vma=False,
    )
```

```python
import functools

import jax
import jax.numpy as jnp
from jax import lax
from jax.experimental import pallas as pl
from jax.experimental.pallas import tpu as pltpu
from jax.sharding import PartitionSpec as P

LEAKAGE = 0.01
HIGHEST = lax.Precision.HIGHEST
F32 = jnp.float32
BF16 = jnp.bfloat16
VMEM_LIMIT = 24 * 1024 * 1024
AXES = ("strike", "dip", "layer")
VMEM = pl.BlockSpec(memory_space=pltpu.VMEM)
SMEM = pl.BlockSpec(memory_space=pltpu.SMEM)
HBM = pl.BlockSpec(memory_space=pltpu.HBM)


def params(**more):
    return pltpu.CompilerParams(vmem_limit_bytes=VMEM_LIMIT, **more)


def shaped(*shape):
    return pltpu.VMEM(shape, F32)


def lanes(rows):
    return lax.broadcasted_iota(jnp.int32, (rows, 128), 1)


def rows_of(count):
    return lax.broadcasted_iota(jnp.int32, (count, 128), 0)


def packed_ends(cells, y, into):
    turned = pltpu.roll(cells, 2 * y + 1, 1)
    lane = lanes(cells.shape[0])
    return jnp.where((lane == 2 * y) | (lane == 2 * y + 1), turned, into)


def place_x(tile, x, ref, plane, rows):
    turned = pltpu.roll(tile, (x % 4) * 32, 1)
    lane = lanes(tile.shape[0])
    mine = (lane // 32) == (x % 4)
    ref[plane, rows, :] = jnp.where(mine, turned, ref[plane, rows, :])


def pack_kernel(
    class_hbm, table_hbm, guess_hbm, field_hbm, perm_ref, xlo, xhi, ylo, yhi, ends_ref,
    classes, table, guess, field_ref, plane_sem, field_sem, class_sem, table_sem,
):
    columns, nx, ny, nz = guess_hbm.shape

    def plane(x):
        return pltpu.make_async_copy(guess_hbm.at[:, x], guess.at[x], plane_sem.at[x])

    def leaving(x):
        return pltpu.make_async_copy(field_ref.at[x], field_hbm.at[x], field_sem.at[x])

    class_copy = pltpu.make_async_copy(class_hbm, classes, class_sem)
    table_copy = pltpu.make_async_copy(table_hbm, table, table_sem)
    table_copy.start()
    class_copy.start()
    for x in range(nx):
        plane(x).start()
    ends_ref[...] = jnp.zeros_like(ends_ref)
    for ref in (xlo, xhi, ylo, yhi):
        ref[ny] = jnp.zeros((columns, nz), F32)
    table_copy.wait()
    class_copy.wait()
    lane = lanes(ny)
    row = rows_of(ny)

    def permeability(x):
        perm = jnp.zeros((ny, nz), F32)
        for level in range(table.shape[0]):
            perm = jnp.where(classes[x] == level, table[level], perm)
        perm_ref[x] = perm
        ylo[ny, pl.ds(x, 1), :] = perm[0:1]
        yhi[ny, pl.ds(x, 1), :] = perm[ny - 1 : ny]
        first = jnp.broadcast_to(perm[:, 0:1], (ny, nz))
        final = jnp.broadcast_to(perm[:, nz - 1 : nz], (ny, nz))
        both = jnp.where(lane == 2 * row, final, jnp.where(lane == 2 * row + 1, first, 0.0))
        edge = jnp.sum(both, axis=0, keepdims=True)
        return jnp.where((lanes(1) // 32) == x % 4, pltpu.roll(edge, (x % 4) * 32, 1), 0.0)

    def four(block, carry):
        edges = [permeability(4 * block + step) for step in range(4)]
        ends_ref[4, pl.ds(block, 1), :] = (edges[0] + edges[1]) + (edges[2] + edges[3])
        return carry

    lax.fori_loop(0, nx // 4, four, 0)
    xlo[ny, 0:ny, :] = perm_ref[0]
    xhi[ny, 0:ny, :] = perm_ref[nx - 1]

    def cells_of(pair, carry):
        for step in range(2):
            plane(2 * pair + step).wait()
        for step in range(2):
            x = 2 * pair + step
            flat = guess.at[x].reshape(columns * ny, nz)
            ends = jnp.zeros((columns, nz), F32)
            for y in range(ny):
                cells = flat[pl.ds(y, columns, stride=ny), :]
                field_ref[x, y] = cells
                ends = packed_ends(cells, y, ends)
                if y == 0:
                    ylo[x] = cells
                if y == ny - 1:
                    yhi[x] = cells
            place_x(ends, x, ends_ref, x // 4, slice(None))
            leaving(x).start()
        return carry

    lax.fori_loop(0, nx // 2, cells_of, 0)
    for y in range(ny):
        xlo[y] = field_ref[0, y]
        xhi[y] = field_ref[nx - 1, y]
    for x in range(nx):
        leaving(x).wait()


def pack(perm_class, perm_table, start_guess):
    columns, nx, ny, nz = start_guess.shape
    face = shaped(ny + 1, columns, nz)
    return pl.pallas_call(
        pack_kernel,
        in_specs=[HBM] * 3,
        out_specs=[HBM] + [VMEM] * 6,
        out_shape=[
            pltpu.HBM((nx, ny, columns, nz), F32),
            shaped(nx, ny, nz),
            face,
            face,
            shaped(nx + 1, columns, nz),
            shaped(nx + 1, columns, nz),
            shaped(5, columns, nz),
        ],
        scratch_shapes=[
            pltpu.VMEM((nx, ny, nz), jnp.int32),
            pltpu.SMEM(perm_table.shape, F32),
            pltpu.VMEM((nx, columns, ny, nz), F32),
            pltpu.VMEM((nx, ny, columns, nz), F32),
            pltpu.SemaphoreType.DMA((nx,)),
            pltpu.SemaphoreType.DMA((nx,)),
            pltpu.SemaphoreType.DMA(()),
            pltpu.SemaphoreType.DMA(()),
        ],
        compiler_params=pltpu.CompilerParams(vmem_limit_bytes=VMEM_LIMIT),
        name="pack_guess",
    )(perm_class, perm_table, start_guess)


def face_weight(center_k, beside_k):
    summed = center_k + beside_k
    divisor = jnp.where(summed > 0.0, summed, 1.0)
    return jnp.where(summed > 0.0, 2.0 * center_k * beside_k / divisor, 0.0)


def arrived(left, right, left_scale=None, right_scale=None):
    after = pltpu.roll(right, 127, 1)
    before = pltpu.roll(left, 1, 1)
    if left_scale is not None:
        after, before = after * right_scale, before * left_scale
    return jnp.where(lanes(left.shape[0]) % 2 == 0, after, before)


def inner_weights(perm_ref, inside, hz, wx, wy, wzm, wzp, wze):
    nx, ny, nz = perm_ref.shape
    lane = lanes(ny)
    row = rows_of(ny)

    def at_x(x):
        center = perm_ref[x]
        wx[x] = face_weight(center, perm_ref[jnp.maximum(x - 1, 0)])
        below = jnp.concatenate([center[:1], center[: ny - 1]], axis=0)
        wy[x, 0:ny, :] = face_weight(center, below)
        ends = arrived(
            hz[0][4, pl.ds(x // 4, 1), :], hz[1][4, pl.ds(x // 4, 1), :], inside[4:5], inside[5:6]
        )
        ends = jnp.broadcast_to(ends, (ny, nz))
        offset = (x % 4) * 32 + 2 * row
        after = jnp.sum(jnp.where(lane == offset, ends, 0.0), axis=1, keepdims=True)
        ahead = jnp.sum(jnp.where(lane == offset + 1, ends, 0.0), axis=1, keepdims=True)
        down = face_weight(center, jnp.where(lane == 0, ahead, pltpu.roll(center, 1, 1)))
        up = face_weight(center, jnp.where(lane == nz - 1, after, pltpu.roll(center, nz - 1, 1)))
        wzm[x] = down
        wzp[x] = up
        first = jnp.broadcast_to(down[:, 0:1], (ny, nz))
        final = jnp.broadcast_to(up[:, nz - 1 : nz], (ny, nz))
        both = jnp.where(lane == 2 * row, final, jnp.where(lane == 2 * row + 1, first, 0.0))
        return jnp.sum(both, axis=0, keepdims=True)

    def at_four(block, carry):
        edges = [at_x(4 * block + step) for step in range(4)]
        for step in range(4):
            wze[pl.ds(4 * block + step, 1), :] = edges[step]
        return carry

    lax.fori_loop(0, nx // 4, at_four, 0)


def outer_weights(perm_ref, inside, hx, hy, wx, wy):
    nx, ny, nz = perm_ref.shape
    wx[0] = face_weight(perm_ref[0], hx[0][...] * inside[0:1])
    wx[nx] = face_weight(perm_ref[nx - 1], hx[1][...] * inside[1:2])
    low = jnp.concatenate([perm_ref[x, 0:1, :] for x in range(nx)], axis=0)
    high = jnp.concatenate([perm_ref[x, ny - 1 : ny, :] for x in range(nx)], axis=0)
    low = face_weight(low, hy[0][0:nx] * inside[2:3])
    high = face_weight(high, hy[1][0:nx] * inside[3:4])
    for x in range(nx):
        wy[x, 0:1, :] = low[x : x + 1]
        wy[x, ny : ny + 1, :] = high[x : x + 1]


def local_sources(boreholes, anchors, nx, ny, nz, total_y, total_z):
    cell = jnp.broadcast_to(boreholes, (boreholes.shape[0], nz))
    along_z = cell % total_z - anchors[2]
    along_y = (cell // total_z) % total_y - anchors[1]
    along_x = cell // (total_z * total_y) - anchors[0]
    inside = (along_x >= 0) & (along_x < nx) & (along_y >= 0) & (along_y < ny)
    matched = inside & (along_z == lanes(boreholes.shape[0]))
    return jnp.where(matched, along_x * ny + along_y, -1)


def difference_matrix(matrix):
    size = matrix.shape[0] // 2
    source = lax.broadcasted_iota(jnp.int32, matrix.shape, 0) % size
    target = lax.broadcasted_iota(jnp.int32, matrix.shape, 1)
    beside = jnp.where(target < size, target + 1, target - size - 1)
    same = jnp.where(source == target % size, 1.0, 0.0)
    matrix[...] = (same - jnp.where(source == beside, 1.0, 0.0)).astype(BF16)


def first_kernel(
    away, hzl, hzr, perm, inside, code, out, ends, wx, wy, wzm, wzp, wze, flux, field, plane_sem
):
    nx, ny, columns, nz = field.shape

    def plane(x):
        return pltpu.make_async_copy(away.at[x], field.at[x], plane_sem.at[x])

    for x in range(nx):
        plane(x).start()
    ends[...] = jnp.zeros_like(ends)
    inner_weights(perm, inside, (hzl, hzr), wx, wy, wzm, wzp, wze)
    flux[...] = jnp.zeros_like(flux)
    plane(0).wait()

    def at_x(x, beside):
        block = x // 4
        beyond = arrived(hzl[block], hzr[block])
        beyond = pltpu.roll(beyond, (128 - (x % 4) * 32) % 128, 1)
        lane = lanes(columns)
        center = field[x, 0]
        flux_y = None
        mine = jnp.zeros((columns, nz), F32)
        for y in range(ny):
            applied = LEAKAGE * center - flux[y]
            if beside is not None:
                flux_x = wx[x + 1, y : y + 1, :] * (center - beside[y])
                applied = applied + flux_x
                flux[y] = flux_x
            if flux_y is not None:
                applied = applied - flux_y
            if y + 1 < ny:
                following = field[x, y + 1]
                flux_y = wy[x, y + 1 : y + 2, :] * (center - following)
                applied = applied + flux_y
            edge = pltpu.roll(beyond, (128 - (2 * y + 1)) % 128, 1)
            after = jnp.where(lane == nz - 1, edge, pltpu.roll(center, nz - 1, 1))
            before = jnp.where(lane == 0, edge, pltpu.roll(center, 1, 1))
            applied = applied + wzp[x, y : y + 1, :] * (center - after)
            applied = applied + wzm[x, y : y + 1, :] * (center - before)
            applied = jnp.where(code[...] == x * ny + y, 1.0, 0.0) - applied
            out[x, y] = applied
            mine = packed_ends(applied, y, mine)
            center = following
        place_x(mine, x, ends, block, slice(None))

    def inner(x, carry):
        plane(x + 1).wait()
        at_x(x, field.at[x + 1])
        return carry

    lax.fori_loop(0, nx - 1, inner, 0)
    at_x(nx - 1, None)


def inner_kernel(last, *refs):
    refs = list(refs)
    take = lambda count: [refs.pop(0) for _ in range(count)]
    field, hzl, hzr, wx, wy, wzm, wzp, wze, out = take(9)
    if not last:
        (ends,) = take(1)
    total, flux, matrix, even, odd, even_halves, odd_halves = take(7)
    nx, ny, columns, nz = field.shape
    if not last:
        ends[...] = jnp.zeros_like(ends)
    difference_matrix(matrix)
    total[...] = jnp.zeros_like(total)
    flux[...] = jnp.zeros_like(flux)

    def differences(x, across, halves):
        plane = field[x].reshape(ny * columns, nz)
        high = plane.astype(BF16)
        low = (plane - high.astype(F32)).astype(BF16)
        both = jnp.concatenate([high, low], axis=1)
        halves[...] = both
        across[...] = jnp.dot(both, matrix[...], preferred_element_type=F32)

    def products(x, halves):
        left = jnp.concatenate(
            [
                jnp.concatenate(
                    [halves[y * columns : (y + 1) * columns, half] for y in range(ny)], axis=1
                )
                for half in (slice(0, nz), slice(nz, 2 * nz))
            ],
            axis=0,
        )
        right = split([jnp.concatenate([out[x, y] for y in range(ny)], axis=1)])
        total[...] += gram(left, jnp.concatenate([left, right], axis=0))

    def stencil(x, across, beside):
        block = x // 4
        beyond = arrived(hzl[block], hzr[block])
        beyond = pltpu.roll(beyond, (128 - (x % 4) * 32) % 128, 1)
        beyond = beyond * wze[pl.ds(x, 1), :]
        lane = lanes(columns)
        outer = (lane == 0) | (lane == nz - 1)
        center = field[x, 0]
        flux_y = None
        mine = jnp.zeros((columns, nz), F32)
        for y in range(ny):
            rows = slice(y * columns, (y + 1) * columns)
            applied = LEAKAGE * center - flux[y]
            if beside is not None:
                flux_x = wx[x + 1, y : y + 1, :] * (center - beside[y])
                applied = applied + flux_x
                flux[y] = flux_x
            if flux_y is not None:
                applied = applied - flux_y
            if y + 1 < ny:
                following = field[x, y + 1]
                flux_y = wy[x, y + 1 : y + 2, :] * (center - following)
                applied = applied + flux_y
            applied = applied + wzp[x, y : y + 1, :] * across[rows, 0:nz]
            applied = applied + wzm[x, y : y + 1, :] * across[rows, nz : 2 * nz]
            edge = pltpu.roll(beyond, (128 - (2 * y + 1)) % 128, 1)
            applied = applied - jnp.where(outer, edge, 0.0)
            out[x, y] = applied
            if not last:
                mine = packed_ends(applied, y, mine)
            center = following
        if not last:
            place_x(mine, x, ends, block, slice(None))

    def step(x, here, there, halves):
        products(x - 1, halves)
        differences(x + 1, there, halves)
        stencil(x, here, field.at[x + 1])

    def pair(place, carry):
        step(2 * place + 1, odd, even, even_halves)
        step(2 * place + 2, even, odd, odd_halves)
        return carry

    differences(0, even, even_halves)
    differences(1, odd, odd_halves)
    stencil(0, even, field.at[1])
    lax.fori_loop(0, nx // 2 - 1, pair, 0)
    products(nx - 2, even_halves)
    stencil(nx - 1, odd, None)
    products(nx - 1, odd_halves)


def sides_kernel(first, last, *refs):
    refs = list(refs)
    take = lambda count: [refs.pop(0) for _ in range(count)]
    part = take(1)[0]
    if first:
        own_faces = take(4)
    else:
        (field,) = take(1)
    hxl, hxr, hyl, hyr = take(4)
    if not last:
        take(1)
    if first:
        take(2)
        perm, inside = take(2)
    else:
        wx, wy, total = take(3)
    if last:
        (earlier,) = take(1)
    (out,) = take(1)
    if not last:
        (ends,) = take(1)
    if first:
        wx, wy = take(2)
    else:
        (sums,) = take(1)
    if not last:
        xlo, xhi, ylo, yhi = take(4)
    nx, ny, columns, nz = part.shape
    lane = lanes(columns)
    if first:
        hx = (hxl.at[ny, 0:ny], hxr.at[ny, 0:ny])
        outer_weights(perm, inside, hx, (hyl.at[ny], hyr.at[ny]), wx, wy)

    added = None
    faces = (
        (hxl, [(0, y) for y in range(ny)], [(0, y) for y in range(ny)], wx),
        (hxr, [(nx - 1, y) for y in range(ny)], [(nx, y) for y in range(ny)], wx),
        (hyl, [(x, 0) for x in range(nx)], [(x, 0) for x in range(nx)], wy),
        (hyr, [(x, ny - 1) for x in range(nx)], [(x, ny) for x in range(nx)], wy),
    )
    for side, (halo, rows, weight_rows, weight) in enumerate(faces):
        own, fluxes = [], []
        for place, ((x, y), (p, q)) in enumerate(zip(rows, weight_rows)):
            center = own_faces[side][place] if first else field[x, y]
            flux = weight[p, q : q + 1, :] * (center - halo[place])
            if first:
                out[x, y] -= flux
            else:
                out[x, y] += flux
                own.append(center)
                fluxes.append(flux)
        if not first:
            left = split([jnp.concatenate(own, axis=1)])
            right = split([jnp.concatenate(fluxes, axis=1)])
            part = gram(left, right)
            added = part if added is None else added + part
    if not last:
        for x in range(nx):
            tile = ends[x // 4]
            for y in range(ny):
                if x in (0, nx - 1) or y in (0, ny - 1):
                    tile = packed_ends(out[x, y], (x % 4) * 16 + y, tile)
            ends[x // 4] = tile
        for y in range(ny):
            xlo[y] = out[0, y]
            xhi[y] = out[nx - 1, y]
        for x in range(nx):
            ylo[x] = out[x, 0]
            yhi[x] = out[x, ny - 1]
    if not first:
        held = total[...]
        held = held[0:32] + held[32:64]
        held = held + pltpu.roll(held, 96, 1)
        held = jnp.where(lane < 32, held, pltpu.roll(held, 96, 1))
        fixed = added[0:32] + added[32:64]
        fixed = fixed[:, 0:32] + fixed[:, 32:64]
        fixed = jnp.concatenate([fixed, jnp.zeros((columns, 96), F32)], axis=1)
        held = jnp.where(lane < 32, held, held + pltpu.roll(fixed, 32, 1))
        if last:
            held = jnp.where(lane < 64, earlier[...], pltpu.roll(held, 64, 1))
        sums[...] = held


def split(fields):
    high = [field.astype(BF16) for field in fields]
    low = [(field - top.astype(F32)).astype(BF16) for field, top in zip(fields, high)]
    return jnp.concatenate(high + low, axis=0)


def gram(left, right):
    return lax.dot_general(left, right, (((1,), (1,)), ((), ())), preferred_element_type=F32)


def fold(products, fields):
    half = products.shape[0] // 2
    summed = products[:half] + products[half:]
    return summed[:, :half] + summed[:, half:]


def inner_part(field, halos, extra, first, last):
    nx, ny, columns, nz = field.shape
    in_specs = [HBM if first else VMEM] + [VMEM] * (len(halos) + len(extra))
    scratch = [pltpu.VMEM((ny, columns, nz), F32)]
    out_shape = [shaped(nx, ny, columns, nz)]
    if not last:
        out_shape += [shaped(4, columns, nz)]
    if first:
        scratch += [pltpu.VMEM(field.shape, F32), pltpu.SemaphoreType.DMA((nx,))]
        out_shape += [
            shaped(nx + 1, ny, nz),
            shaped(nx, ny + 8, nz),
            shaped(nx, ny, nz),
            shaped(nx, ny, nz),
            shaped(nx, nz),
        ]
    else:
        scratch += [pltpu.VMEM((2 * nz, 2 * nz), BF16)]
        scratch += [pltpu.VMEM((ny * columns, 2 * nz), F32)] * 2
        scratch += [pltpu.VMEM((ny * columns, 2 * nz), BF16)] * 2
        out_shape += [shaped(2 * columns, 4 * columns)]
    return pl.pallas_call(
        first_kernel if first else functools.partial(inner_kernel, last),
        in_specs=in_specs,
        out_specs=[VMEM] * len(out_shape),
        out_shape=out_shape,
        scratch_shapes=scratch,
        compiler_params=params(),
        cost_estimate=pl.CostEstimate(
            flops=20 * field.size, bytes_accessed=6 * field.size * 4, transcendentals=0
        ),
        name="inner_first" if first else "inner_last" if last else "inner_next",
    )(field, *halos, *extra)


def sides_part(part, own, halos, ends, extra, first, last):
    nx, ny, columns, nz = part.shape
    operands = [part, *own, *halos]
    place = len(operands)
    if not last:
        operands += [ends]
    operands += extra
    in_specs = [VMEM] * len(operands)
    aliases = {0: 0}
    out_shape = [shaped(*part.shape)]
    if not last:
        aliases[place] = 1
        out_shape += [shaped(*ends.shape)]
    if first:
        aliases[place + 1] = 2
        aliases[place + 2] = 3
        out_shape += [shaped(*extra[0].shape), shaped(*extra[1].shape)]
    else:
        out_shape += [shaped(columns, 128)]
    if not last:
        out_shape += [shaped(ny, columns, nz)] * 2 + [shaped(nx, columns, nz)] * 2
    return pl.pallas_call(
        functools.partial(sides_kernel, first, last),
        in_specs=in_specs,
        out_specs=[VMEM] * len(out_shape),
        out_shape=out_shape,
        input_output_aliases=aliases,
        compiler_params=params(),
        name="sides_first" if first else "sides_last" if last else "sides_next",
    )(*operands)


def exchanged(xlo, xhi, ylo, yhi, ends):
    ahead = lambda axis: [(i, (i + 1) % lax.axis_size(axis)) for i in range(lax.axis_size(axis))]
    back = lambda axis: [(j, i) for i, j in ahead(axis)]
    near = (
        lax.ppermute(ends, "layer", ahead("layer")),
        lax.ppermute(ends, "layer", back("layer")),
    )
    near, ylo, yhi = lax.optimization_barrier((near, ylo, yhi))
    far = (
        lax.ppermute(xhi, "strike", ahead("strike")),
        lax.ppermute(xlo, "strike", back("strike")),
        lax.ppermute(yhi, "dip", ahead("dip")),
        lax.ppermute(ylo, "dip", back("dip")),
    )
    return near, far


def dot(left, right, contract=(1, 0)):
    dims = (((contract[0],), (contract[1],)), ((), ()))
    return lax.dot_general(left, right, dims, precision=HIGHEST, preferred_element_type=F32)


def eliminate(tables):
    row = rows_of(32)
    for k in range(0, 32, 2):
        done = []
        for table in tables:
            one = jnp.broadcast_to(table[:, k : k + 1], table.shape)
            two = jnp.broadcast_to(table[:, k + 1 : k + 2], table.shape)
            a, b = one[k : k + 1], two[k : k + 1]
            c, d = one[k + 1 : k + 2], two[k + 1 : k + 2]
            scale = 1.0 / (a * d - b * c)
            upper, lower = table[k : k + 1], table[k + 1 : k + 2]
            first = (d * upper - b * lower) * scale
            second = (a * lower - c * upper) * scale
            rest = (table - one * first) - two * second
            done.append(jnp.where(row == k, first, jnp.where(row == k + 1, second, rest)))
        tables = done
    return tables


def solve_kernel(*refs):
    out_ref = refs[-1]
    sums = refs[0][...]
    for ref in refs[1:-1]:
        sums = sums + ref[...]
    lane = lanes(32)
    row = rows_of(32)
    table = jnp.where(lane < 32, pltpu.roll(sums, 96, 1), pltpu.roll(sums, 32, 1))
    table = jnp.where(lane < 64, table, jnp.where(lane == row + 64, 1.0, 0.0))
    (table,) = eliminate([table])
    norm = sums[:, 0:32]
    square = sums[:, 64:96]
    cube = sums[:, 96:128]
    advance = table[:, 32:64]
    inverse = table[:, 64:96]
    advance_t = advance.T
    turned = dot(square, advance)
    tripled = dot(advance, dot(cube, advance), (0, 0))
    mixing = dot(inverse, turned)
    norm_next = dot(advance, turned, (0, 0)) - norm
    curvature = tripled - dot(turned, mixing, (0, 0))
    wide = jnp.concatenate([curvature, norm_next, jnp.zeros((32, 64), F32)], axis=1)
    (wide,) = eliminate([wide])
    later = wide[:, 32:64]
    taken_t = advance_t + dot(later, mixing, (0, 1))
    beyond_t = dot(later, advance, (0, 1))
    nothing = jnp.zeros((32, 32), F32)
    out_ref[0:32, :] = jnp.concatenate([taken_t, -beyond_t, nothing, nothing], axis=1)
    out_ref[32:64, :] = jnp.concatenate([nothing, -taken_t, beyond_t, nothing], axis=1)


def solve(parts):
    return pl.pallas_call(
        solve_kernel,
        in_specs=[VMEM] * len(parts),
        out_specs=VMEM,
        out_shape=shaped(64, 128),
        compiler_params=params(),
        name="solve_small",
    )(*parts)


def combine_kernel(
    mix_ref, guess_hbm, one_ref, two_ref, three_ref, solution_hbm, residual_hbm,
    guess_ref, solution, residual, sem, guess_sem,
):
    nx, ny, columns, nz = guess_ref.shape
    slots = solution.shape[0]

    def arriving(x):
        return pltpu.make_async_copy(guess_hbm.at[x], guess_ref.at[x], guess_sem.at[x])

    for x in range(nx):
        arriving(x).start()
    mix = mix_ref[...]
    high = mix.astype(BF16)
    low = (mix - high.astype(F32)).astype(BF16)
    mixing = jnp.concatenate(
        [
            jnp.concatenate([half[:, : 3 * columns], half[:, : 3 * columns]], axis=1)
            for half in (high, low)
        ],
        axis=0,
    )

    def leaving(x):
        slot = x % slots
        copies = []
        for place, (held, away) in enumerate(((solution, solution_hbm), (residual, residual_hbm))):
            for half in range(ny // 8):
                copies.append(
                    pltpu.make_async_copy(
                        held.at[slot, half],
                        away.at[:, x, 8 * half : 8 * half + 8],
                        sem.at[place, half, slot],
                    )
                )
        return copies

    mix = mix_ref[...]
    high = mix.astype(BF16)
    low = (mix - high.astype(F32)).astype(BF16)
    mixing = jnp.concatenate(
        [
            jnp.concatenate([half[:, : 3 * columns], half[:, : 3 * columns]], axis=1)
            for half in (high, low)
        ],
        axis=0,
    )

    def at_pair(pair, carry):
        @pl.when(2 * pair >= slots)
        def _():
            for step in range(2):
                for copy in leaving(2 * pair + step - slots):
                    copy.wait()

        for step in range(2):
            arriving(2 * pair + step).wait()
        for step in range(2):
            x = 2 * pair + step
            slot = lax.rem(x, slots)
            solution_rows = solution.at[slot].reshape(columns * ny, nz)
            residual_rows = residual.at[slot].reshape(columns * ny, nz)
            for y in range(0, ny, 2):
                fields = [
                    jnp.concatenate([ref[x, y], ref[x, y + 1]], axis=1)
                    for ref in (one_ref, two_ref, three_ref)
                ]
                mixed = jnp.dot(mixing, split(fields), preferred_element_type=F32)
                mixed = mixed[0:64] + mixed[64:128]
                for z in range(2):
                    own = y + z
                    rows = pl.ds((own // 8) * 8 * columns + own % 8, columns, stride=8)
                    part = mixed[:, z * nz : (z + 1) * nz]
                    solution_rows[rows, :] = guess_ref[x, own] + part[0:32]
                    residual_rows[rows, :] = one_ref[x, own] + part[32:64]
        for step in range(2):
            for copy in leaving(2 * pair + step):
                copy.start()
        return carry

    lax.fori_loop(0, nx // 2, at_pair, 0)
    for x in range(nx - slots, nx):
        for copy in leaving(x):
            copy.wait()


def combine(mix, guess, one, two, three):
    nx, ny, columns, nz = guess.shape
    return pl.pallas_call(
        combine_kernel,
        in_specs=[VMEM, HBM] + [VMEM] * 3,
        out_specs=[HBM] * 2,
        out_shape=[jax.ShapeDtypeStruct((columns, nx, ny, nz), F32)] * 2,
        scratch_shapes=[
            pltpu.VMEM(guess.shape, F32),
            pltpu.VMEM((8, ny // 8, columns, 8, nz), F32),
            pltpu.VMEM((8, ny // 8, columns, 8, nz), F32),
            pltpu.SemaphoreType.DMA((2, ny // 8, 8)),
            pltpu.SemaphoreType.DMA((nx,)),
        ],
        compiler_params=params(),
        name="combine_fields",
    )(mix, guess, one, two, three)


def swaps(axis, mask, stride=1):
    return [(i, i ^ (mask * stride)) for i in range(lax.axis_size(axis))]


def summed_but_last(values):
    groups = []
    for axis in AXES[::-1]:
        size, stride = lax.axis_size(axis), 1
        while size // stride > 4:
            values = values + lax.ppermute(values, axis, swaps(axis, 1, stride))
            stride *= 2
        groups.append((axis, stride))
    for place, (axis, stride) in enumerate(groups):
        others = [
            lax.ppermute(values, axis, swaps(axis, mask, stride))
            for mask in (1, 3, 2)
            if mask * stride < lax.axis_size(axis)
        ]
        if place + 1 < len(groups):
            for other in others:
                values = values + other
    return [values, *others]


def shards(perm_class, perm_table, boreholes, start_guess):
    columns, nx, ny, nz = start_guess.shape
    places = [lax.axis_index(axis) for axis in AXES]
    sizes = [lax.axis_size(axis) for axis in AXES]
    anchors = [place * size for place, size in zip(places, (nx, ny, nz))]
    totals = tuple(size * count for size, count in zip((nx, ny, nz), sizes))
    inside = []
    for place, size in zip(places, sizes):
        inside += [place > 0, place < size - 1]
    inside = jnp.broadcast_to(jnp.stack(inside + inside[:2]).astype(F32)[:, None], (8, nz))

    in_hbm = [
        pltpu.with_memory_space_constraint(held, pltpu.HBM)
        for held in (perm_class, perm_table, start_guess)
    ]
    guess, perm, *faces = pack(*in_hbm)
    guess = pltpu.with_memory_space_constraint(guess, pltpu.HBM)
    near, far = exchanged(*faces)
    code = local_sources(boreholes[:, None], anchors, nx, ny, nz, totals[1], totals[2])
    extra = (perm, inside, code)
    part, ends, wx, wy, *along_z = inner_part(guess, near, extra, True, False)
    residual, ends, wx, wy, *faces = sides_part(
        part, faces[:4], far, ends, [wx, wy, perm, inside], True, False
    )
    weights = (wx, wy, *along_z)
    near, far = exchanged(*faces, ends)
    part, ends, total = inner_part(residual, near, weights, False, False)
    once, ends, sums, *faces = sides_part(
        part, [residual], far, ends, [wx, wy, total], False, False
    )
    near, far = exchanged(*faces, ends)
    part, total = inner_part(once, near, weights, False, True)
    twice, sums = sides_part(part, [once], far, None, [wx, wy, total, sums], False, True)
    mix = solve(summed_but_last(sums))
    return tuple(combine(mix, guess, residual, once, twice))


def solution(mesh):
    placed = (P("strike", "dip", "layer"), P(), P(), P(None, "strike", "dip", "layer"))
    return jax.shard_map(
        shards,
        mesh=mesh,
        in_specs=placed,
        out_specs=(P(None, "strike", "dip", "layer"), P(None, "strike", "dip", "layer")),
        check_vma=False,
    )
```

```python
import functools

import jax
import jax.numpy as jnp
from jax import lax
from jax.experimental import pallas as pl
from jax.experimental.pallas import tpu as pltpu
from jax.sharding import PartitionSpec as P

LEAKAGE = 0.01
HIGHEST = lax.Precision.HIGHEST
F32 = jnp.float32
BF16 = jnp.bfloat16
VMEM_LIMIT = 24 * 1024 * 1024
AXES = ("strike", "dip", "layer")
VMEM = pl.BlockSpec(memory_space=pltpu.VMEM)
SMEM = pl.BlockSpec(memory_space=pltpu.SMEM)
HBM = pl.BlockSpec(memory_space=pltpu.HBM)


def params(**more):
    return pltpu.CompilerParams(vmem_limit_bytes=VMEM_LIMIT, **more)


def shaped(*shape):
    return pltpu.VMEM(shape, F32)


def lanes(rows):
    return lax.broadcasted_iota(jnp.int32, (rows, 128), 1)


def rows_of(count):
    return lax.broadcasted_iota(jnp.int32, (count, 128), 0)


def packed_ends(cells, y, into):
    turned = pltpu.roll(cells, 2 * y + 1, 1)
    lane = lanes(cells.shape[0])
    return jnp.where((lane == 2 * y) | (lane == 2 * y + 1), turned, into)


def place_x(tile, x, ref, plane, rows):
    turned = pltpu.roll(tile, (x % 4) * 32, 1)
    lane = lanes(tile.shape[0])
    mine = (lane // 32) == (x % 4)
    ref[plane, rows, :] = jnp.where(mine, turned, ref[plane, rows, :])


def pack_kernel(
    class_hbm, table_hbm, guess_hbm, field_hbm, perm_ref, xlo, xhi, ylo, yhi, ends_ref,
    classes, table, guess, field_ref, plane_sem, field_sem, class_sem, table_sem,
):
    columns, nx, ny, nz = guess_hbm.shape

    def plane(x):
        return pltpu.make_async_copy(guess_hbm.at[:, x], guess.at[x], plane_sem.at[x])

    def leaving(x):
        return pltpu.make_async_copy(field_ref.at[x], field_hbm.at[x], field_sem.at[x])

    class_copy = pltpu.make_async_copy(class_hbm, classes, class_sem)
    table_copy = pltpu.make_async_copy(table_hbm, table, table_sem)
    table_copy.start()
    class_copy.start()
    for x in range(nx):
        plane(x).start()
    ends_ref[...] = jnp.zeros_like(ends_ref)
    for ref in (xlo, xhi, ylo, yhi):
        ref[ny] = jnp.zeros((columns, nz), F32)
    table_copy.wait()
    class_copy.wait()
    lane = lanes(ny)
    row = rows_of(ny)

    def permeability(x):
        perm = jnp.zeros((ny, nz), F32)
        for level in range(table.shape[0]):
            perm = jnp.where(classes[x] == level, table[level], perm)
        perm_ref[x] = perm
        ylo[ny, pl.ds(x, 1), :] = perm[0:1]
        yhi[ny, pl.ds(x, 1), :] = perm[ny - 1 : ny]
        first = jnp.broadcast_to(perm[:, 0:1], (ny, nz))
        final = jnp.broadcast_to(perm[:, nz - 1 : nz], (ny, nz))
        both = jnp.where(lane == 2 * row, final, jnp.where(lane == 2 * row + 1, first, 0.0))
        edge = jnp.sum(both, axis=0, keepdims=True)
        return jnp.where((lanes(1) // 32) == x % 4, pltpu.roll(edge, (x % 4) * 32, 1), 0.0)

    def four(block, carry):
        edges = [permeability(4 * block + step) for step in range(4)]
        ends_ref[4, pl.ds(block, 1), :] = (edges[0] + edges[1]) + (edges[2] + edges[3])
        return carry

    lax.fori_loop(0, nx // 4, four, 0)
    xlo[ny, 0:ny, :] = perm_ref[0]
    xhi[ny, 0:ny, :] = perm_ref[nx - 1]

    def cells_of(pair, carry):
        for step in range(2):
            plane(2 * pair + step).wait()
        for step in range(2):
            x = 2 * pair + step
            flat = guess.at[x].reshape(columns * ny, nz)
            ends = jnp.zeros((columns, nz), F32)
            for y in range(ny):
                cells = flat[pl.ds(y, columns, stride=ny), :]
                field_ref[x, y] = cells
                ends = packed_ends(cells, y, ends)
                if y == 0:
                    ylo[x] = cells
                if y == ny - 1:
                    yhi[x] = cells
            place_x(ends, x, ends_ref, x // 4, slice(None))
            leaving(x).start()
        return carry

    lax.fori_loop(0, nx // 2, cells_of, 0)
    for y in range(ny):
        xlo[y] = field_ref[0, y]
        xhi[y] = field_ref[nx - 1, y]
    for x in range(nx):
        leaving(x).wait()


def pack(perm_class, perm_table, start_guess):
    columns, nx, ny, nz = start_guess.shape
    face = shaped(ny + 1, columns, nz)
    return pl.pallas_call(
        pack_kernel,
        in_specs=[HBM] * 3,
        out_specs=[HBM] + [VMEM] * 6,
        out_shape=[
            pltpu.HBM((nx, ny, columns, nz), F32),
            shaped(nx, ny, nz),
            face,
            face,
            shaped(nx + 1, columns, nz),
            shaped(nx + 1, columns, nz),
            shaped(5, columns, nz),
        ],
        scratch_shapes=[
            pltpu.VMEM((nx, ny, nz), jnp.int32),
            pltpu.SMEM(perm_table.shape, F32),
            pltpu.VMEM((nx, columns, ny, nz), F32),
            pltpu.VMEM((nx, ny, columns, nz), F32),
            pltpu.SemaphoreType.DMA((nx,)),
            pltpu.SemaphoreType.DMA((nx,)),
            pltpu.SemaphoreType.DMA(()),
            pltpu.SemaphoreType.DMA(()),
        ],
        compiler_params=pltpu.CompilerParams(vmem_limit_bytes=VMEM_LIMIT),
        name="pack_guess",
    )(perm_class, perm_table, start_guess)


def face_weight(center_k, beside_k):
    summed = center_k + beside_k
    divisor = jnp.where(summed > 0.0, summed, 1.0)
    return jnp.where(summed > 0.0, 2.0 * center_k * beside_k / divisor, 0.0)


def arrived(left, right, left_scale=None, right_scale=None):
    after = pltpu.roll(right, 127, 1)
    before = pltpu.roll(left, 1, 1)
    if left_scale is not None:
        after, before = after * right_scale, before * left_scale
    return jnp.where(lanes(left.shape[0]) % 2 == 0, after, before)


def inner_weights(perm_ref, inside, hz, wx, wy, wzm, wzp, wze):
    nx, ny, nz = perm_ref.shape
    lane = lanes(ny)
    row = rows_of(ny)

    def at_x(x):
        center = perm_ref[x]
        wx[x] = face_weight(center, perm_ref[jnp.maximum(x - 1, 0)])
        below = jnp.concatenate([center[:1], center[: ny - 1]], axis=0)
        wy[x, 0:ny, :] = face_weight(center, below)
        ends = arrived(
            hz[0][4, pl.ds(x // 4, 1), :], hz[1][4, pl.ds(x // 4, 1), :], inside[4:5], inside[5:6]
        )
        ends = jnp.broadcast_to(ends, (ny, nz))
        offset = (x % 4) * 32 + 2 * row
        after = jnp.sum(jnp.where(lane == offset, ends, 0.0), axis=1, keepdims=True)
        ahead = jnp.sum(jnp.where(lane == offset + 1, ends, 0.0), axis=1, keepdims=True)
        down = face_weight(center, jnp.where(lane == 0, ahead, pltpu.roll(center, 1, 1)))
        up = face_weight(center, jnp.where(lane == nz - 1, after, pltpu.roll(center, nz - 1, 1)))
        wzm[x] = down
        wzp[x] = up
        first = jnp.broadcast_to(down[:, 0:1], (ny, nz))
        final = jnp.broadcast_to(up[:, nz - 1 : nz], (ny, nz))
        both = jnp.where(lane == 2 * row, final, jnp.where(lane == 2 * row + 1, first, 0.0))
        return jnp.sum(both, axis=0, keepdims=True)

    def at_four(block, carry):
        edges = [at_x(4 * block + step) for step in range(4)]
        for step in range(4):
            wze[pl.ds(4 * block + step, 1), :] = edges[step]
        return carry

    lax.fori_loop(0, nx // 4, at_four, 0)


def outer_weights(perm_ref, inside, hx, hy, wx, wy):
    nx, ny, nz = perm_ref.shape
    wx[0] = face_weight(perm_ref[0], hx[0][...] * inside[0:1])
    wx[nx] = face_weight(perm_ref[nx - 1], hx[1][...] * inside[1:2])
    low = jnp.concatenate([perm_ref[x, 0:1, :] for x in range(nx)], axis=0)
    high = jnp.concatenate([perm_ref[x, ny - 1 : ny, :] for x in range(nx)], axis=0)
    low = face_weight(low, hy[0][0:nx] * inside[2:3])
    high = face_weight(high, hy[1][0:nx] * inside[3:4])
    for x in range(nx):
        wy[x, 0:1, :] = low[x : x + 1]
        wy[x, ny : ny + 1, :] = high[x : x + 1]


def local_sources(boreholes, anchors, nx, ny, nz, total_y, total_z):
    cell = jnp.broadcast_to(boreholes, (boreholes.shape[0], nz))
    along_z = cell % total_z - anchors[2]
    along_y = (cell // total_z) % total_y - anchors[1]
    along_x = cell // (total_z * total_y) - anchors[0]
    inside = (along_x >= 0) & (along_x < nx) & (along_y >= 0) & (along_y < ny)
    matched = inside & (along_z == lanes(boreholes.shape[0]))
    return jnp.where(matched, along_x * ny + along_y, -1)


def difference_matrix(matrix):
    size = matrix.shape[0] // 2
    source = lax.broadcasted_iota(jnp.int32, matrix.shape, 0) % size
    target = lax.broadcasted_iota(jnp.int32, matrix.shape, 1)
    beside = jnp.where(target < size, target + 1, target - size - 1)
    same = jnp.where(source == target % size, 1.0, 0.0)
    matrix[...] = (same - jnp.where(source == beside, 1.0, 0.0)).astype(BF16)


def first_kernel(
    away, hzl, hzr, perm, inside, code, out, ends, wx, wy, wzm, wzp, wze, flux, field, plane_sem
):
    nx, ny, columns, nz = field.shape

    def plane(x):
        return pltpu.make_async_copy(away.at[x], field.at[x], plane_sem.at[x])

    for x in range(nx):
        plane(x).start()
    ends[...] = jnp.zeros_like(ends)
    inner_weights(perm, inside, (hzl, hzr), wx, wy, wzm, wzp, wze)
    flux[...] = jnp.zeros_like(flux)
    plane(0).wait()

    def at_x(x, beside):
        block = x // 4
        beyond = arrived(hzl[block], hzr[block])
        beyond = pltpu.roll(beyond, (128 - (x % 4) * 32) % 128, 1)
        lane = lanes(columns)
        center = field[x, 0]
        flux_y = None
        mine = jnp.zeros((columns, nz), F32)
        for y in range(ny):
            applied = LEAKAGE * center - flux[y]
            if beside is not None:
                flux_x = wx[x + 1, y : y + 1, :] * (center - beside[y])
                applied = applied + flux_x
                flux[y] = flux_x
            if flux_y is not None:
                applied = applied - flux_y
            if y + 1 < ny:
                following = field[x, y + 1]
                flux_y = wy[x, y + 1 : y + 2, :] * (center - following)
                applied = applied + flux_y
            edge = pltpu.roll(beyond, (128 - (2 * y + 1)) % 128, 1)
            after = jnp.where(lane == nz - 1, edge, pltpu.roll(center, nz - 1, 1))
            before = jnp.where(lane == 0, edge, pltpu.roll(center, 1, 1))
            applied = applied + wzp[x, y : y + 1, :] * (center - after)
            applied = applied + wzm[x, y : y + 1, :] * (center - before)
            applied = jnp.where(code[...] == x * ny + y, 1.0, 0.0) - applied
            out[x, y] = applied
            mine = packed_ends(applied, y, mine)
            center = following
        place_x(mine, x, ends, block, slice(None))

    def inner(x, carry):
        plane(x + 1).wait()
        at_x(x, field.at[x + 1])
        return carry

    lax.fori_loop(0, nx - 1, inner, 0)
    at_x(nx - 1, None)


def inner_kernel(last, *refs):
    refs = list(refs)
    take = lambda count: [refs.pop(0) for _ in range(count)]
    field, hzl, hzr, wx, wy, wzm, wzp, wze, out = take(9)
    if not last:
        (ends,) = take(1)
    total, flux, matrix, even, odd, even_halves, odd_halves = take(7)
    nx, ny, columns, nz = field.shape
    if not last:
        ends[...] = jnp.zeros_like(ends)
    difference_matrix(matrix)
    total[...] = jnp.zeros_like(total)
    flux[...] = jnp.zeros_like(flux)

    def differences(x, across, halves):
        plane = field[x].reshape(ny * columns, nz)
        high = plane.astype(BF16)
        low = (plane - high.astype(F32)).astype(BF16)
        both = jnp.concatenate([high, low], axis=1)
        halves[...] = both
        across[...] = jnp.dot(both, matrix[...], preferred_element_type=F32)

    def products(x, halves):
        left = jnp.concatenate(
            [
                jnp.concatenate(
                    [halves[y * columns : (y + 1) * columns, half] for y in range(ny)], axis=1
                )
                for half in (slice(0, nz), slice(nz, 2 * nz))
            ],
            axis=0,
        )
        right = split([jnp.concatenate([out[x, y] for y in range(ny)], axis=1)])
        total[...] += gram(left, jnp.concatenate([left, right], axis=0))

    def stencil(x, across, beside):
        block = x // 4
        beyond = arrived(hzl[block], hzr[block])
        beyond = pltpu.roll(beyond, (128 - (x % 4) * 32) % 128, 1)
        beyond = beyond * wze[pl.ds(x, 1), :]
        lane = lanes(columns)
        outer = (lane == 0) | (lane == nz - 1)
        center = field[x, 0]
        flux_y = None
        mine = jnp.zeros((columns, nz), F32)
        for y in range(ny):
            rows = slice(y * columns, (y + 1) * columns)
            applied = LEAKAGE * center - flux[y]
            if beside is not None:
                flux_x = wx[x + 1, y : y + 1, :] * (center - beside[y])
                applied = applied + flux_x
                flux[y] = flux_x
            if flux_y is not None:
                applied = applied - flux_y
            if y + 1 < ny:
                following = field[x, y + 1]
                flux_y = wy[x, y + 1 : y + 2, :] * (center - following)
                applied = applied + flux_y
            applied = applied + wzp[x, y : y + 1, :] * across[rows, 0:nz]
            applied = applied + wzm[x, y : y + 1, :] * across[rows, nz : 2 * nz]
            edge = pltpu.roll(beyond, (128 - (2 * y + 1)) % 128, 1)
            applied = applied - jnp.where(outer, edge, 0.0)
            out[x, y] = applied
            if not last:
                mine = packed_ends(applied, y, mine)
            center = following
        if not last:
            place_x(mine, x, ends, block, slice(None))

    def step(x, here, there, halves):
        products(x - 1, halves)
        differences(x + 1, there, halves)
        stencil(x, here, field.at[x + 1])

    def pair(place, carry):
        step(2 * place + 1, odd, even, even_halves)
        step(2 * place + 2, even, odd, odd_halves)
        return carry

    differences(0, even, even_halves)
    differences(1, odd, odd_halves)
    stencil(0, even, field.at[1])
    lax.fori_loop(0, nx // 2 - 1, pair, 0)
    products(nx - 2, even_halves)
    stencil(nx - 1, odd, None)
    products(nx - 1, odd_halves)


def sides_kernel(first, last, *refs):
    refs = list(refs)
    take = lambda count: [refs.pop(0) for _ in range(count)]
    part = take(1)[0]
    if first:
        own_faces = take(4)
    else:
        (field,) = take(1)
    hxl, hxr, hyl, hyr = take(4)
    if not last:
        take(1)
    if first:
        take(2)
        perm, inside = take(2)
    else:
        wx, wy, total = take(3)
    if last:
        (earlier,) = take(1)
    (out,) = take(1)
    if not last:
        (ends,) = take(1)
    if first:
        wx, wy = take(2)
    else:
        (sums,) = take(1)
    if not last:
        xlo, xhi, ylo, yhi = take(4)
    nx, ny, columns, nz = part.shape
    lane = lanes(columns)
    if first:
        hx = (hxl.at[ny, 0:ny], hxr.at[ny, 0:ny])
        outer_weights(perm, inside, hx, (hyl.at[ny], hyr.at[ny]), wx, wy)

    added = None
    faces = (
        (hxl, [(0, y) for y in range(ny)], [(0, y) for y in range(ny)], wx),
        (hxr, [(nx - 1, y) for y in range(ny)], [(nx, y) for y in range(ny)], wx),
        (hyl, [(x, 0) for x in range(nx)], [(x, 0) for x in range(nx)], wy),
        (hyr, [(x, ny - 1) for x in range(nx)], [(x, ny) for x in range(nx)], wy),
    )
    for side, (halo, rows, weight_rows, weight) in enumerate(faces):
        own, fluxes = [], []
        for place, ((x, y), (p, q)) in enumerate(zip(rows, weight_rows)):
            center = own_faces[side][place] if first else field[x, y]
            flux = weight[p, q : q + 1, :] * (center - halo[place])
            if first:
                out[x, y] -= flux
            else:
                out[x, y] += flux
                own.append(center)
                fluxes.append(flux)
        if not first:
            left = split([jnp.concatenate(own, axis=1)])
            right = split([jnp.concatenate(fluxes, axis=1)])
            part = gram(left, right)
            added = part if added is None else added + part
    if not last:
        for x in range(nx):
            tile = ends[x // 4]
            for y in range(ny):
                if x in (0, nx - 1) or y in (0, ny - 1):
                    tile = packed_ends(out[x, y], (x % 4) * 16 + y, tile)
            ends[x // 4] = tile
        for y in range(ny):
            xlo[y] = out[0, y]
            xhi[y] = out[nx - 1, y]
        for x in range(nx):
            ylo[x] = out[x, 0]
            yhi[x] = out[x, ny - 1]
    if not first:
        held = total[...]
        held = held[0:32] + held[32:64]
        held = held + pltpu.roll(held, 96, 1)
        held = jnp.where(lane < 32, held, pltpu.roll(held, 96, 1))
        fixed = added[0:32] + added[32:64]
        fixed = fixed[:, 0:32] + fixed[:, 32:64]
        fixed = jnp.concatenate([fixed, jnp.zeros((columns, 96), F32)], axis=1)
        held = jnp.where(lane < 32, held, held + pltpu.roll(fixed, 32, 1))
        if last:
            held = jnp.where(lane < 64, earlier[...], pltpu.roll(held, 64, 1))
        sums[...] = held


def split(fields):
    high = [field.astype(BF16) for field in fields]
    low = [(field - top.astype(F32)).astype(BF16) for field, top in zip(fields, high)]
    return jnp.concatenate(high + low, axis=0)


def gram(left, right):
    return lax.dot_general(left, right, (((1,), (1,)), ((), ())), preferred_element_type=F32)


def fold(products, fields):
    half = products.shape[0] // 2
    summed = products[:half] + products[half:]
    return summed[:, :half] + summed[:, half:]


def inner_part(field, halos, extra, first, last):
    nx, ny, columns, nz = field.shape
    in_specs = [HBM if first else VMEM] + [VMEM] * (len(halos) + len(extra))
    scratch = [pltpu.VMEM((ny, columns, nz), F32)]
    out_shape = [shaped(nx, ny, columns, nz)]
    if not last:
        out_shape += [shaped(4, columns, nz)]
    if first:
        scratch += [pltpu.VMEM(field.shape, F32), pltpu.SemaphoreType.DMA((nx,))]
        out_shape += [
            shaped(nx + 1, ny, nz),
            shaped(nx, ny + 8, nz),
            shaped(nx, ny, nz),
            shaped(nx, ny, nz),
            shaped(nx, nz),
        ]
    else:
        scratch += [pltpu.VMEM((2 * nz, 2 * nz), BF16)]
        scratch += [pltpu.VMEM((ny * columns, 2 * nz), F32)] * 2
        scratch += [pltpu.VMEM((ny * columns, 2 * nz), BF16)] * 2
        out_shape += [shaped(2 * columns, 4 * columns)]
    return pl.pallas_call(
        first_kernel if first else functools.partial(inner_kernel, last),
        in_specs=in_specs,
        out_specs=[VMEM] * len(out_shape),
        out_shape=out_shape,
        scratch_shapes=scratch,
        compiler_params=params(),
        cost_estimate=pl.CostEstimate(
            flops=20 * field.size, bytes_accessed=6 * field.size * 4, transcendentals=0
        ),
        name="inner_first" if first else "inner_last" if last else "inner_next",
    )(field, *halos, *extra)


def sides_part(part, own, halos, ends, extra, first, last):
    nx, ny, columns, nz = part.shape
    operands = [part, *own, *halos]
    place = len(operands)
    if not last:
        operands += [ends]
    operands += extra
    in_specs = [VMEM] * len(operands)
    aliases = {0: 0}
    out_shape = [shaped(*part.shape)]
    if not last:
        aliases[place] = 1
        out_shape += [shaped(*ends.shape)]
    if first:
        aliases[place + 1] = 2
        aliases[place + 2] = 3
        out_shape += [shaped(*extra[0].shape), shaped(*extra[1].shape)]
    else:
        out_shape += [shaped(columns, 128)]
    if not last:
        out_shape += [shaped(ny, columns, nz)] * 2 + [shaped(nx, columns, nz)] * 2
    return pl.pallas_call(
        functools.partial(sides_kernel, first, last),
        in_specs=in_specs,
        out_specs=[VMEM] * len(out_shape),
        out_shape=out_shape,
        input_output_aliases=aliases,
        compiler_params=params(),
        name="sides_first" if first else "sides_last" if last else "sides_next",
    )(*operands)


def exchanged(xlo, xhi, ylo, yhi, ends):
    ahead = lambda axis: [(i, (i + 1) % lax.axis_size(axis)) for i in range(lax.axis_size(axis))]
    back = lambda axis: [(j, i) for i, j in ahead(axis)]
    near = (
        lax.ppermute(ends, "layer", ahead("layer")),
        lax.ppermute(ends, "layer", back("layer")),
    )
    near, ylo = lax.optimization_barrier((near, ylo))
    far = (
        lax.ppermute(xhi, "strike", ahead("strike")),
        lax.ppermute(xlo, "strike", back("strike")),
        lax.ppermute(yhi, "dip", ahead("dip")),
        lax.ppermute(ylo, "dip", back("dip")),
    )
    return near, far


def dot(left, right, contract=(1, 0)):
    dims = (((contract[0],), (contract[1],)), ((), ()))
    return lax.dot_general(left, right, dims, precision=HIGHEST, preferred_element_type=F32)


def eliminate(tables):
    row = rows_of(32)
    for k in range(0, 32, 2):
        done = []
        for table in tables:
            one = jnp.broadcast_to(table[:, k : k + 1], table.shape)
            two = jnp.broadcast_to(table[:, k + 1 : k + 2], table.shape)
            a, b = one[k : k + 1], two[k : k + 1]
            c, d = one[k + 1 : k + 2], two[k + 1 : k + 2]
            scale = 1.0 / (a * d - b * c)
            upper, lower = table[k : k + 1], table[k + 1 : k + 2]
            first = (d * upper - b * lower) * scale
            second = (a * lower - c * upper) * scale
            rest = (table - one * first) - two * second
            done.append(jnp.where(row == k, first, jnp.where(row == k + 1, second, rest)))
        tables = done
    return tables


def solve_kernel(*refs):
    out_ref = refs[-1]
    sums = refs[0][...]
    for ref in refs[1:-1]:
        sums = sums + ref[...]
    lane = lanes(32)
    row = rows_of(32)
    table = jnp.where(lane < 32, pltpu.roll(sums, 96, 1), pltpu.roll(sums, 32, 1))
    table = jnp.where(lane < 64, table, jnp.where(lane == row + 64, 1.0, 0.0))
    (table,) = eliminate([table])
    norm = sums[:, 0:32]
    square = sums[:, 64:96]
    cube = sums[:, 96:128]
    advance = table[:, 32:64]
    inverse = table[:, 64:96]
    advance_t = advance.T
    turned = dot(square, advance)
    tripled = dot(advance, dot(cube, advance), (0, 0))
    mixing = dot(inverse, turned)
    norm_next = dot(advance, turned, (0, 0)) - norm
    curvature = tripled - dot(turned, mixing, (0, 0))
    wide = jnp.concatenate([curvature, norm_next, jnp.zeros((32, 64), F32)], axis=1)
    (wide,) = eliminate([wide])
    later = wide[:, 32:64]
    taken_t = advance_t + dot(later, mixing, (0, 1))
    beyond_t = dot(later, advance, (0, 1))
    nothing = jnp.zeros((32, 32), F32)
    out_ref[0:32, :] = jnp.concatenate([taken_t, -beyond_t, nothing, nothing], axis=1)
    out_ref[32:64, :] = jnp.concatenate([nothing, -taken_t, beyond_t, nothing], axis=1)


def solve(parts):
    return pl.pallas_call(
        solve_kernel,
        in_specs=[VMEM] * len(parts),
        out_specs=VMEM,
        out_shape=shaped(64, 128),
        compiler_params=params(),
        name="solve_small",
    )(*parts)


def combine_kernel(
    mix_ref, guess_hbm, one_ref, two_ref, three_ref, solution_hbm, residual_hbm,
    guess_ref, solution, residual, sem, guess_sem,
):
    nx, ny, columns, nz = guess_ref.shape
    slots = solution.shape[0]

    def arriving(x):
        return pltpu.make_async_copy(guess_hbm.at[x], guess_ref.at[x], guess_sem.at[x])

    for x in range(nx):
        arriving(x).start()
    mix = mix_ref[...]
    high = mix.astype(BF16)
    low = (mix - high.astype(F32)).astype(BF16)
    mixing = jnp.concatenate(
        [
            jnp.concatenate([half[:, : 3 * columns], half[:, : 3 * columns]], axis=1)
            for half in (high, low)
        ],
        axis=0,
    )

    def leaving(x):
        slot = x % slots
        copies = []
        for place, (held, away) in enumerate(((solution, solution_hbm), (residual, residual_hbm))):
            for half in range(ny // 8):
                copies.append(
                    pltpu.make_async_copy(
                        held.at[slot, half],
                        away.at[:, x, 8 * half : 8 * half + 8],
                        sem.at[place, half, slot],
                    )
                )
        return copies

    mix = mix_ref[...]
    high = mix.astype(BF16)
    low = (mix - high.astype(F32)).astype(BF16)
    mixing = jnp.concatenate(
        [
            jnp.concatenate([half[:, : 3 * columns], half[:, : 3 * columns]], axis=1)
            for half in (high, low)
        ],
        axis=0,
    )

    def at_pair(pair, carry):
        @pl.when(2 * pair >= slots)
        def _():
            for step in range(2):
                for copy in leaving(2 * pair + step - slots):
                    copy.wait()

        for step in range(2):
            arriving(2 * pair + step).wait()
        for step in range(2):
            x = 2 * pair + step
            slot = lax.rem(x, slots)
            solution_rows = solution.at[slot].reshape(columns * ny, nz)
            residual_rows = residual.at[slot].reshape(columns * ny, nz)
            for y in range(0, ny, 2):
                fields = [
                    jnp.concatenate([ref[x, y], ref[x, y + 1]], axis=1)
                    for ref in (one_ref, two_ref, three_ref)
                ]
                mixed = jnp.dot(mixing, split(fields), preferred_element_type=F32)
                mixed = mixed[0:64] + mixed[64:128]
                for z in range(2):
                    own = y + z
                    rows = pl.ds((own // 8) * 8 * columns + own % 8, columns, stride=8)
                    part = mixed[:, z * nz : (z + 1) * nz]
                    solution_rows[rows, :] = guess_ref[x, own] + part[0:32]
                    residual_rows[rows, :] = one_ref[x, own] + part[32:64]
        for step in range(2):
            for copy in leaving(2 * pair + step):
                copy.start()
        return carry

    lax.fori_loop(0, nx // 2, at_pair, 0)
    for x in range(nx - slots, nx):
        for copy in leaving(x):
            copy.wait()


def combine(mix, guess, one, two, three):
    nx, ny, columns, nz = guess.shape
    return pl.pallas_call(
        combine_kernel,
        in_specs=[VMEM, HBM] + [VMEM] * 3,
        out_specs=[HBM] * 2,
        out_shape=[jax.ShapeDtypeStruct((columns, nx, ny, nz), F32)] * 2,
        scratch_shapes=[
            pltpu.VMEM(guess.shape, F32),
            pltpu.VMEM((8, ny // 8, columns, 8, nz), F32),
            pltpu.VMEM((8, ny // 8, columns, 8, nz), F32),
            pltpu.SemaphoreType.DMA((2, ny // 8, 8)),
            pltpu.SemaphoreType.DMA((nx,)),
        ],
        compiler_params=params(),
        name="combine_fields",
    )(mix, guess, one, two, three)


def swaps(axis, mask, stride=1):
    return [(i, i ^ (mask * stride)) for i in range(lax.axis_size(axis))]


def summed_but_last(values):
    groups = []
    for axis in AXES[::-1]:
        size, stride = lax.axis_size(axis), 1
        while size // stride > 4:
            values = values + lax.ppermute(values, axis, swaps(axis, 1, stride))
            stride *= 2
        groups.append((axis, stride))
    for place, (axis, stride) in enumerate(groups):
        others = [
            lax.ppermute(values, axis, swaps(axis, mask, stride))
            for mask in (1, 3, 2)
            if mask * stride < lax.axis_size(axis)
        ]
        if place + 1 < len(groups):
            for other in others:
                values = values + other
    return [values, *others]


def shards(perm_class, perm_table, boreholes, start_guess):
    columns, nx, ny, nz = start_guess.shape
    places = [lax.axis_index(axis) for axis in AXES]
    sizes = [lax.axis_size(axis) for axis in AXES]
    anchors = [place * size for place, size in zip(places, (nx, ny, nz))]
    totals = tuple(size * count for size, count in zip((nx, ny, nz), sizes))
    inside = []
    for place, size in zip(places, sizes):
        inside += [place > 0, place < size - 1]
    inside = jnp.broadcast_to(jnp.stack(inside + inside[:2]).astype(F32)[:, None], (8, nz))

    in_hbm = [
        pltpu.with_memory_space_constraint(held, pltpu.HBM)
        for held in (perm_class, perm_table, start_guess)
    ]
    guess, perm, *faces = pack(*in_hbm)
    guess = pltpu.with_memory_space_constraint(guess, pltpu.HBM)
    near, far = exchanged(*faces)
    code = local_sources(boreholes[:, None], anchors, nx, ny, nz, totals[1], totals[2])
    extra = (perm, inside, code)
    part, ends, wx, wy, *along_z = inner_part(guess, near, extra, True, False)
    residual, ends, wx, wy, *faces = sides_part(
        part, faces[:4], far, ends, [wx, wy, perm, inside], True, False
    )
    weights = (wx, wy, *along_z)
    near, far = exchanged(*faces, ends)
    part, ends, total = inner_part(residual, near, weights, False, False)
    once, ends, sums, *faces = sides_part(
        part, [residual], far, ends, [wx, wy, total], False, False
    )
    near, far = exchanged(*faces, ends)
    part, total = inner_part(once, near, weights, False, True)
    twice, sums = sides_part(part, [once], far, None, [wx, wy, total, sums], False, True)
    mix = solve(summed_but_last(sums))
    return tuple(combine(mix, guess, residual, once, twice))


def solution(mesh):
    placed = (P("strike", "dip", "layer"), P(), P(), P(None, "strike", "dip", "layer"))
    return jax.shard_map(
        shards,
        mesh=mesh,
        in_specs=placed,
        out_specs=(P(None, "strike", "dip", "layer"), P(None, "strike", "dip", "layer")),
        check_vma=False,
    )
```

```python
import functools

import jax
import jax.numpy as jnp
from jax import lax
from jax.experimental import pallas as pl
from jax.experimental.pallas import tpu as pltpu
from jax.sharding import PartitionSpec as P

LEAKAGE = 0.01
HIGHEST = lax.Precision.HIGHEST
F32 = jnp.float32
BF16 = jnp.bfloat16
VMEM_LIMIT = 24 * 1024 * 1024
AXES = ("strike", "dip", "layer")
VMEM = pl.BlockSpec(memory_space=pltpu.VMEM)
SMEM = pl.BlockSpec(memory_space=pltpu.SMEM)
HBM = pl.BlockSpec(memory_space=pltpu.HBM)


def params(**more):
    return pltpu.CompilerParams(vmem_limit_bytes=VMEM_LIMIT, **more)


def shaped(*shape):
    return pltpu.VMEM(shape, F32)


def lanes(rows):
    return lax.broadcasted_iota(jnp.int32, (rows, 128), 1)


def rows_of(count):
    return lax.broadcasted_iota(jnp.int32, (count, 128), 0)


def packed_ends(cells, y, into):
    turned = pltpu.roll(cells, 2 * y + 1, 1)
    lane = lanes(cells.shape[0])
    return jnp.where((lane == 2 * y) | (lane == 2 * y + 1), turned, into)


def place_x(tile, x, ref, plane, rows):
    turned = pltpu.roll(tile, (x % 4) * 32, 1)
    lane = lanes(tile.shape[0])
    mine = (lane // 32) == (x % 4)
    ref[plane, rows, :] = jnp.where(mine, turned, ref[plane, rows, :])


def pack_kernel(
    class_hbm, table_hbm, guess_hbm, field_hbm, perm_ref, xlo, xhi, ylo, yhi, ends_ref,
    classes, table, guess, field_ref, plane_sem, field_sem, class_sem, table_sem,
):
    columns, nx, ny, nz = guess_hbm.shape

    def plane(x):
        return pltpu.make_async_copy(guess_hbm.at[:, x], guess.at[x], plane_sem.at[x])

    def leaving(x):
        return pltpu.make_async_copy(field_ref.at[x], field_hbm.at[x], field_sem.at[x])

    class_copy = pltpu.make_async_copy(class_hbm, classes, class_sem)
    table_copy = pltpu.make_async_copy(table_hbm, table, table_sem)
    table_copy.start()
    class_copy.start()
    for x in range(nx):
        plane(x).start()
    ends_ref[...] = jnp.zeros_like(ends_ref)
    for ref in (xlo, xhi, ylo, yhi):
        ref[ny] = jnp.zeros((columns, nz), F32)
    table_copy.wait()
    class_copy.wait()
    lane = lanes(ny)
    row = rows_of(ny)

    def permeability(x):
        perm = jnp.zeros((ny, nz), F32)
        for level in range(table.shape[0]):
            perm = jnp.where(classes[x] == level, table[level], perm)
        perm_ref[x] = perm
        ylo[ny, pl.ds(x, 1), :] = perm[0:1]
        yhi[ny, pl.ds(x, 1), :] = perm[ny - 1 : ny]
        first = jnp.broadcast_to(perm[:, 0:1], (ny, nz))
        final = jnp.broadcast_to(perm[:, nz - 1 : nz], (ny, nz))
        both = jnp.where(lane == 2 * row, final, jnp.where(lane == 2 * row + 1, first, 0.0))
        edge = jnp.sum(both, axis=0, keepdims=True)
        return jnp.where((lanes(1) // 32) == x % 4, pltpu.roll(edge, (x % 4) * 32, 1), 0.0)

    def four(block, carry):
        edges = [permeability(4 * block + step) for step in range(4)]
        ends_ref[4, pl.ds(block, 1), :] = (edges[0] + edges[1]) + (edges[2] + edges[3])
        return carry

    lax.fori_loop(0, nx // 4, four, 0)
    xlo[ny, 0:ny, :] = perm_ref[0]
    xhi[ny, 0:ny, :] = perm_ref[nx - 1]

    def cells_of(pair, carry):
        for step in range(2):
            plane(2 * pair + step).wait()
        for step in range(2):
            x = 2 * pair + step
            flat = guess.at[x].reshape(columns * ny, nz)
            ends = jnp.zeros((columns, nz), F32)
            for y in range(ny):
                cells = flat[pl.ds(y, columns, stride=ny), :]
                field_ref[x, y] = cells
                ends = packed_ends(cells, y, ends)
                if y == 0:
                    ylo[x] = cells
                if y == ny - 1:
                    yhi[x] = cells
            place_x(ends, x, ends_ref, x // 4, slice(None))
            leaving(x).start()
        return carry

    lax.fori_loop(0, nx // 2, cells_of, 0)
    for y in range(ny):
        xlo[y] = field_ref[0, y]
        xhi[y] = field_ref[nx - 1, y]
    for x in range(nx):
        leaving(x).wait()


def pack(perm_class, perm_table, start_guess):
    columns, nx, ny, nz = start_guess.shape
    face = shaped(ny + 1, columns, nz)
    return pl.pallas_call(
        pack_kernel,
        in_specs=[HBM] * 3,
        out_specs=[HBM] + [VMEM] * 6,
        out_shape=[
            pltpu.HBM((nx, ny, columns, nz), F32),
            shaped(nx, ny, nz),
            face,
            face,
            shaped(nx + 1, columns, nz),
            shaped(nx + 1, columns, nz),
            shaped(5, columns, nz),
        ],
        scratch_shapes=[
            pltpu.VMEM((nx, ny, nz), jnp.int32),
            pltpu.SMEM(perm_table.shape, F32),
            pltpu.VMEM((nx, columns, ny, nz), F32),
            pltpu.VMEM((nx, ny, columns, nz), F32),
            pltpu.SemaphoreType.DMA((nx,)),
            pltpu.SemaphoreType.DMA((nx,)),
            pltpu.SemaphoreType.DMA(()),
            pltpu.SemaphoreType.DMA(()),
        ],
        compiler_params=pltpu.CompilerParams(vmem_limit_bytes=VMEM_LIMIT),
        name="pack_guess",
    )(perm_class, perm_table, start_guess)


def face_weight(center_k, beside_k):
    summed = center_k + beside_k
    divisor = jnp.where(summed > 0.0, summed, 1.0)
    return jnp.where(summed > 0.0, 2.0 * center_k * beside_k / divisor, 0.0)


def arrived(left, right, left_scale=None, right_scale=None):
    after = pltpu.roll(right, 127, 1)
    before = pltpu.roll(left, 1, 1)
    if left_scale is not None:
        after, before = after * right_scale, before * left_scale
    return jnp.where(lanes(left.shape[0]) % 2 == 0, after, before)


def inner_weights(perm_ref, inside, hz, wx, wy, wzm, wzp, wze):
    nx, ny, nz = perm_ref.shape
    lane = lanes(ny)
    row = rows_of(ny)

    def at_x(x):
        center = perm_ref[x]
        wx[x] = face_weight(center, perm_ref[jnp.maximum(x - 1, 0)])
        below = jnp.concatenate([center[:1], center[: ny - 1]], axis=0)
        wy[x, 0:ny, :] = face_weight(center, below)
        ends = arrived(
            hz[0][4, pl.ds(x // 4, 1), :], hz[1][4, pl.ds(x // 4, 1), :], inside[4:5], inside[5:6]
        )
        ends = jnp.broadcast_to(ends, (ny, nz))
        offset = (x % 4) * 32 + 2 * row
        after = jnp.sum(jnp.where(lane == offset, ends, 0.0), axis=1, keepdims=True)
        ahead = jnp.sum(jnp.where(lane == offset + 1, ends, 0.0), axis=1, keepdims=True)
        down = face_weight(center, jnp.where(lane == 0, ahead, pltpu.roll(center, 1, 1)))
        up = face_weight(center, jnp.where(lane == nz - 1, after, pltpu.roll(center, nz - 1, 1)))
        wzm[x] = down
        wzp[x] = up
        first = jnp.broadcast_to(down[:, 0:1], (ny, nz))
        final = jnp.broadcast_to(up[:, nz - 1 : nz], (ny, nz))
        both = jnp.where(lane == 2 * row, final, jnp.where(lane == 2 * row + 1, first, 0.0))
        return jnp.sum(both, axis=0, keepdims=True)

    def at_four(block, carry):
        edges = [at_x(4 * block + step) for step in range(4)]
        for step in range(4):
            wze[pl.ds(4 * block + step, 1), :] = edges[step]
        return carry

    lax.fori_loop(0, nx // 4, at_four, 0)


def outer_weights(perm_ref, inside, hx, hy, wx, wy):
    nx, ny, nz = perm_ref.shape
    wx[0] = face_weight(perm_ref[0], hx[0][...] * inside[0:1])
    wx[nx] = face_weight(perm_ref[nx - 1], hx[1][...] * inside[1:2])
    low = jnp.concatenate([perm_ref[x, 0:1, :] for x in range(nx)], axis=0)
    high = jnp.concatenate([perm_ref[x, ny - 1 : ny, :] for x in range(nx)], axis=0)
    low = face_weight(low, hy[0][0:nx] * inside[2:3])
    high = face_weight(high, hy[1][0:nx] * inside[3:4])
    for x in range(nx):
        wy[x, 0:1, :] = low[x : x + 1]
        wy[x, ny : ny + 1, :] = high[x : x + 1]


def local_sources(boreholes, anchors, nx, ny, nz, total_y, total_z):
    cell = jnp.broadcast_to(boreholes, (boreholes.shape[0], nz))
    along_z = cell % total_z - anchors[2]
    along_y = (cell // total_z) % total_y - anchors[1]
    along_x = cell // (total_z * total_y) - anchors[0]
    inside = (along_x >= 0) & (along_x < nx) & (along_y >= 0) & (along_y < ny)
    matched = inside & (along_z == lanes(boreholes.shape[0]))
    return jnp.where(matched, along_x * ny + along_y, -1)


def difference_matrix(matrix):
    size = matrix.shape[0] // 2
    source = lax.broadcasted_iota(jnp.int32, matrix.shape, 0) % size
    target = lax.broadcasted_iota(jnp.int32, matrix.shape, 1)
    beside = jnp.where(target < size, target + 1, target - size - 1)
    same = jnp.where(source == target % size, 1.0, 0.0)
    matrix[...] = (same - jnp.where(source == beside, 1.0, 0.0)).astype(BF16)


def first_kernel(
    away, hzl, hzr, perm, inside, code, out, ends, wx, wy, wzm, wzp, wze, flux, field, plane_sem
):
    nx, ny, columns, nz = field.shape

    def plane(x):
        return pltpu.make_async_copy(away.at[x], field.at[x], plane_sem.at[x])

    for x in range(nx):
        plane(x).start()
    ends[...] = jnp.zeros_like(ends)
    inner_weights(perm, inside, (hzl, hzr), wx, wy, wzm, wzp, wze)
    flux[...] = jnp.zeros_like(flux)
    plane(0).wait()

    def at_x(x, beside):
        block = x // 4
        beyond = arrived(hzl[block], hzr[block])
        beyond = pltpu.roll(beyond, (128 - (x % 4) * 32) % 128, 1)
        lane = lanes(columns)
        center = field[x, 0]
        flux_y = None
        mine = jnp.zeros((columns, nz), F32)
        for y in range(ny):
            applied = LEAKAGE * center - flux[y]
            if beside is not None:
                flux_x = wx[x + 1, y : y + 1, :] * (center - beside[y])
                applied = applied + flux_x
                flux[y] = flux_x
            if flux_y is not None:
                applied = applied - flux_y
            if y + 1 < ny:
                following = field[x, y + 1]
                flux_y = wy[x, y + 1 : y + 2, :] * (center - following)
                applied = applied + flux_y
            edge = pltpu.roll(beyond, (128 - (2 * y + 1)) % 128, 1)
            after = jnp.where(lane == nz - 1, edge, pltpu.roll(center, nz - 1, 1))
            before = jnp.where(lane == 0, edge, pltpu.roll(center, 1, 1))
            applied = applied + wzp[x, y : y + 1, :] * (center - after)
            applied = applied + wzm[x, y : y + 1, :] * (center - before)
            applied = jnp.where(code[...] == x * ny + y, 1.0, 0.0) - applied
            out[x, y] = applied
            mine = packed_ends(applied, y, mine)
            center = following
        place_x(mine, x, ends, block, slice(None))

    def inner(x, carry):
        plane(x + 1).wait()
        at_x(x, field.at[x + 1])
        return carry

    lax.fori_loop(0, nx - 1, inner, 0)
    at_x(nx - 1, None)


def inner_kernel(last, *refs):
    refs = list(refs)
    take = lambda count: [refs.pop(0) for _ in range(count)]
    field, hzl, hzr, wx, wy, wzm, wzp, wze, out = take(9)
    if not last:
        (ends,) = take(1)
    total, flux, matrix, even, odd, even_halves, odd_halves = take(7)
    nx, ny, columns, nz = field.shape
    if not last:
        ends[...] = jnp.zeros_like(ends)
    difference_matrix(matrix)
    total[...] = jnp.zeros_like(total)
    flux[...] = jnp.zeros_like(flux)

    def differences(x, across, halves):
        plane = field[x].reshape(ny * columns, nz)
        high = plane.astype(BF16)
        low = (plane - high.astype(F32)).astype(BF16)
        both = jnp.concatenate([high, low], axis=1)
        halves[...] = both
        across[...] = jnp.dot(both, matrix[...], preferred_element_type=F32)

    def products(x, halves):
        left = jnp.concatenate(
            [
                jnp.concatenate(
                    [halves[y * columns : (y + 1) * columns, half] for y in range(ny)], axis=1
                )
                for half in (slice(0, nz), slice(nz, 2 * nz))
            ],
            axis=0,
        )
        right = split([jnp.concatenate([out[x, y] for y in range(ny)], axis=1)])
        total[...] += gram(left, jnp.concatenate([left, right], axis=0))

    def stencil(x, across, beside):
        block = x // 4
        beyond = arrived(hzl[block], hzr[block])
        beyond = pltpu.roll(beyond, (128 - (x % 4) * 32) % 128, 1)
        beyond = beyond * wze[pl.ds(x, 1), :]
        lane = lanes(columns)
        outer = (lane == 0) | (lane == nz - 1)
        center = field[x, 0]
        flux_y = None
        mine = jnp.zeros((columns, nz), F32)
        for y in range(ny):
            rows = slice(y * columns, (y + 1) * columns)
            applied = LEAKAGE * center - flux[y]
            if beside is not None:
                flux_x = wx[x + 1, y : y + 1, :] * (center - beside[y])
                applied = applied + flux_x
                flux[y] = flux_x
            if flux_y is not None:
                applied = applied - flux_y
            if y + 1 < ny:
                following = field[x, y + 1]
                flux_y = wy[x, y + 1 : y + 2, :] * (center - following)
                applied = applied + flux_y
            applied = applied + wzp[x, y : y + 1, :] * across[rows, 0:nz]
            applied = applied + wzm[x, y : y + 1, :] * across[rows, nz : 2 * nz]
            edge = pltpu.roll(beyond, (128 - (2 * y + 1)) % 128, 1)
            applied = applied - jnp.where(outer, edge, 0.0)
            out[x, y] = applied
            if not last:
                mine = packed_ends(applied, y, mine)
            center = following
        if not last:
            place_x(mine, x, ends, block, slice(None))

    def step(x, here, there, halves):
        products(x - 1, halves)
        differences(x + 1, there, halves)
        stencil(x, here, field.at[x + 1])

    def pair(place, carry):
        step(2 * place + 1, odd, even, even_halves)
        step(2 * place + 2, even, odd, odd_halves)
        return carry

    differences(0, even, even_halves)
    differences(1, odd, odd_halves)
    stencil(0, even, field.at[1])
    lax.fori_loop(0, nx // 2 - 1, pair, 0)
    products(nx - 2, even_halves)
    stencil(nx - 1, odd, None)
    products(nx - 1, odd_halves)


def sides_kernel(first, last, *refs):
    refs = list(refs)
    take = lambda count: [refs.pop(0) for _ in range(count)]
    part = take(1)[0]
    if first:
        own_faces = take(4)
    else:
        (field,) = take(1)
    hxl, hxr, hyl, hyr = take(4)
    if not last:
        take(1)
    if first:
        take(2)
        perm, inside = take(2)
    else:
        wx, wy, total = take(3)
    if last:
        (earlier,) = take(1)
    (out,) = take(1)
    if not last:
        (ends,) = take(1)
    if first:
        wx, wy = take(2)
    else:
        (sums,) = take(1)
    if not last:
        xlo, xhi, ylo, yhi = take(4)
    nx, ny, columns, nz = part.shape
    lane = lanes(columns)
    if first:
        hx = (hxl.at[ny, 0:ny], hxr.at[ny, 0:ny])
        outer_weights(perm, inside, hx, (hyl.at[ny], hyr.at[ny]), wx, wy)

    added = None
    faces = (
        (hxl, [(0, y) for y in range(ny)], [(0, y) for y in range(ny)], wx),
        (hxr, [(nx - 1, y) for y in range(ny)], [(nx, y) for y in range(ny)], wx),
        (hyl, [(x, 0) for x in range(nx)], [(x, 0) for x in range(nx)], wy),
        (hyr, [(x, ny - 1) for x in range(nx)], [(x, ny) for x in range(nx)], wy),
    )
    for side, (halo, rows, weight_rows, weight) in enumerate(faces):
        own, fluxes = [], []
        for place, ((x, y), (p, q)) in enumerate(zip(rows, weight_rows)):
            center = own_faces[side][place] if first else field[x, y]
            flux = weight[p, q : q + 1, :] * (center - halo[place])
            if first:
                out[x, y] -= flux
            else:
                out[x, y] += flux
                own.append(center)
                fluxes.append(flux)
        if not first:
            left = split([jnp.concatenate(own, axis=1)])
            right = split([jnp.concatenate(fluxes, axis=1)])
            part = gram(left, right)
            added = part if added is None else added + part
    if not last:
        for x in range(nx):
            tile = ends[x // 4]
            for y in range(ny):
                if x in (0, nx - 1) or y in (0, ny - 1):
                    tile = packed_ends(out[x, y], (x % 4) * 16 + y, tile)
            ends[x // 4] = tile
        for y in range(ny):
            xlo[y] = out[0, y]
            xhi[y] = out[nx - 1, y]
        for x in range(nx):
            ylo[x] = out[x, 0]
            yhi[x] = out[x, ny - 1]
    if not first:
        held = total[...]
        held = held[0:32] + held[32:64]
        held = held + pltpu.roll(held, 96, 1)
        held = jnp.where(lane < 32, held, pltpu.roll(held, 96, 1))
        fixed = added[0:32] + added[32:64]
        fixed = fixed[:, 0:32] + fixed[:, 32:64]
        fixed = jnp.concatenate([fixed, jnp.zeros((columns, 96), F32)], axis=1)
        held = jnp.where(lane < 32, held, held + pltpu.roll(fixed, 32, 1))
        if last:
            held = jnp.where(lane < 64, earlier[...], pltpu.roll(held, 64, 1))
        sums[...] = held


def split(fields):
    high = [field.astype(BF16) for field in fields]
    low = [(field - top.astype(F32)).astype(BF16) for field, top in zip(fields, high)]
    return jnp.concatenate(high + low, axis=0)


def gram(left, right):
    return lax.dot_general(left, right, (((1,), (1,)), ((), ())), preferred_element_type=F32)


def fold(products, fields):
    half = products.shape[0] // 2
    summed = products[:half] + products[half:]
    return summed[:, :half] + summed[:, half:]


def inner_part(field, halos, extra, first, last):
    nx, ny, columns, nz = field.shape
    in_specs = [HBM if first else VMEM] + [VMEM] * (len(halos) + len(extra))
    scratch = [pltpu.VMEM((ny, columns, nz), F32)]
    out_shape = [shaped(nx, ny, columns, nz)]
    if not last:
        out_shape += [shaped(4, columns, nz)]
    if first:
        scratch += [pltpu.VMEM(field.shape, F32), pltpu.SemaphoreType.DMA((nx,))]
        out_shape += [
            shaped(nx + 1, ny, nz),
            shaped(nx, ny + 8, nz),
            shaped(nx, ny, nz),
            shaped(nx, ny, nz),
            shaped(nx, nz),
        ]
    else:
        scratch += [pltpu.VMEM((2 * nz, 2 * nz), BF16)]
        scratch += [pltpu.VMEM((ny * columns, 2 * nz), F32)] * 2
        scratch += [pltpu.VMEM((ny * columns, 2 * nz), BF16)] * 2
        out_shape += [shaped(2 * columns, 4 * columns)]
    return pl.pallas_call(
        first_kernel if first else functools.partial(inner_kernel, last),
        in_specs=in_specs,
        out_specs=[VMEM] * len(out_shape),
        out_shape=out_shape,
        scratch_shapes=scratch,
        compiler_params=params(),
        cost_estimate=pl.CostEstimate(
            flops=20 * field.size, bytes_accessed=6 * field.size * 4, transcendentals=0
        ),
        name="inner_first" if first else "inner_last" if last else "inner_next",
    )(field, *halos, *extra)


def sides_part(part, own, halos, ends, extra, first, last):
    nx, ny, columns, nz = part.shape
    operands = [part, *own, *halos]
    place = len(operands)
    if not last:
        operands += [ends]
    operands += extra
    in_specs = [VMEM] * len(operands)
    aliases = {0: 0}
    out_shape = [shaped(*part.shape)]
    if not last:
        aliases[place] = 1
        out_shape += [shaped(*ends.shape)]
    if first:
        aliases[place + 1] = 2
        aliases[place + 2] = 3
        out_shape += [shaped(*extra[0].shape), shaped(*extra[1].shape)]
    else:
        out_shape += [shaped(columns, 128)]
    if not last:
        out_shape += [shaped(ny, columns, nz)] * 2 + [shaped(nx, columns, nz)] * 2
    return pl.pallas_call(
        functools.partial(sides_kernel, first, last),
        in_specs=in_specs,
        out_specs=[VMEM] * len(out_shape),
        out_shape=out_shape,
        input_output_aliases=aliases,
        compiler_params=params(),
        name="sides_first" if first else "sides_last" if last else "sides_next",
    )(*operands)


def exchanged(xlo, xhi, ylo, yhi, ends):
    ahead = lambda axis: [(i, (i + 1) % lax.axis_size(axis)) for i in range(lax.axis_size(axis))]
    back = lambda axis: [(j, i) for i, j in ahead(axis)]
    near = (
        lax.ppermute(ends, "layer", ahead("layer")),
        lax.ppermute(ends, "layer", back("layer")),
    )
    near, yhi = lax.optimization_barrier((near, yhi))
    far = (
        lax.ppermute(xhi, "strike", ahead("strike")),
        lax.ppermute(xlo, "strike", back("strike")),
        lax.ppermute(yhi, "dip", ahead("dip")),
        lax.ppermute(ylo, "dip", back("dip")),
    )
    return near, far


def dot(left, right, contract=(1, 0)):
    dims = (((contract[0],), (contract[1],)), ((), ()))
    return lax.dot_general(left, right, dims, precision=HIGHEST, preferred_element_type=F32)


def eliminate(tables):
    row = rows_of(32)
    for k in range(0, 32, 2):
        done = []
        for table in tables:
            one = jnp.broadcast_to(table[:, k : k + 1], table.shape)
            two = jnp.broadcast_to(table[:, k + 1 : k + 2], table.shape)
            a, b = one[k : k + 1], two[k : k + 1]
            c, d = one[k + 1 : k + 2], two[k + 1 : k + 2]
            scale = 1.0 / (a * d - b * c)
            upper, lower = table[k : k + 1], table[k + 1 : k + 2]
            first = (d * upper - b * lower) * scale
            second = (a * lower - c * upper) * scale
            rest = (table - one * first) - two * second
            done.append(jnp.where(row == k, first, jnp.where(row == k + 1, second, rest)))
        tables = done
    return tables


def solve_kernel(*refs):
    out_ref = refs[-1]
    sums = refs[0][...]
    for ref in refs[1:-1]:
        sums = sums + ref[...]
    lane = lanes(32)
    row = rows_of(32)
    table = jnp.where(lane < 32, pltpu.roll(sums, 96, 1), pltpu.roll(sums, 32, 1))
    table = jnp.where(lane < 64, table, jnp.where(lane == row + 64, 1.0, 0.0))
    (table,) = eliminate([table])
    norm = sums[:, 0:32]
    square = sums[:, 64:96]
    cube = sums[:, 96:128]
    advance = table[:, 32:64]
    inverse = table[:, 64:96]
    advance_t = advance.T
    turned = dot(square, advance)
    tripled = dot(advance, dot(cube, advance), (0, 0))
    mixing = dot(inverse, turned)
    norm_next = dot(advance, turned, (0, 0)) - norm
    curvature = tripled - dot(turned, mixing, (0, 0))
    wide = jnp.concatenate([curvature, norm_next, jnp.zeros((32, 64), F32)], axis=1)
    (wide,) = eliminate([wide])
    later = wide[:, 32:64]
    taken_t = advance_t + dot(later, mixing, (0, 1))
    beyond_t = dot(later, advance, (0, 1))
    nothing = jnp.zeros((32, 32), F32)
    out_ref[0:32, :] = jnp.concatenate([taken_t, -beyond_t, nothing, nothing], axis=1)
    out_ref[32:64, :] = jnp.concatenate([nothing, -taken_t, beyond_t, nothing], axis=1)


def solve(parts):
    return pl.pallas_call(
        solve_kernel,
        in_specs=[VMEM] * len(parts),
        out_specs=VMEM,
        out_shape=shaped(64, 128),
        compiler_params=params(),
        name="solve_small",
    )(*parts)


def combine_kernel(
    mix_ref, guess_hbm, one_ref, two_ref, three_ref, solution_hbm, residual_hbm,
    guess_ref, solution, residual, sem, guess_sem,
):
    nx, ny, columns, nz = guess_ref.shape
    slots = solution.shape[0]

    def arriving(x):
        return pltpu.make_async_copy(guess_hbm.at[x], guess_ref.at[x], guess_sem.at[x])

    for x in range(nx):
        arriving(x).start()
    mix = mix_ref[...]
    high = mix.astype(BF16)
    low = (mix - high.astype(F32)).astype(BF16)
    mixing = jnp.concatenate(
        [
            jnp.concatenate([half[:, : 3 * columns], half[:, : 3 * columns]], axis=1)
            for half in (high, low)
        ],
        axis=0,
    )

    def leaving(x):
        slot = x % slots
        copies = []
        for place, (held, away) in enumerate(((solution, solution_hbm), (residual, residual_hbm))):
            for half in range(ny // 8):
                copies.append(
                    pltpu.make_async_copy(
                        held.at[slot, half],
                        away.at[:, x, 8 * half : 8 * half + 8],
                        sem.at[place, half, slot],
                    )
                )
        return copies

    mix = mix_ref[...]
    high = mix.astype(BF16)
    low = (mix - high.astype(F32)).astype(BF16)
    mixing = jnp.concatenate(
        [
            jnp.concatenate([half[:, : 3 * columns], half[:, : 3 * columns]], axis=1)
            for half in (high, low)
        ],
        axis=0,
    )

    def at_pair(pair, carry):
        @pl.when(2 * pair >= slots)
        def _():
            for step in range(2):
                for copy in leaving(2 * pair + step - slots):
                    copy.wait()

        for step in range(2):
            arriving(2 * pair + step).wait()
        for step in range(2):
            x = 2 * pair + step
            slot = lax.rem(x, slots)
            solution_rows = solution.at[slot].reshape(columns * ny, nz)
            residual_rows = residual.at[slot].reshape(columns * ny, nz)
            for y in range(0, ny, 2):
                fields = [
                    jnp.concatenate([ref[x, y], ref[x, y + 1]], axis=1)
                    for ref in (one_ref, two_ref, three_ref)
                ]
                mixed = jnp.dot(mixing, split(fields), preferred_element_type=F32)
                mixed = mixed[0:64] + mixed[64:128]
                for z in range(2):
                    own = y + z
                    rows = pl.ds((own // 8) * 8 * columns + own % 8, columns, stride=8)
                    part = mixed[:, z * nz : (z + 1) * nz]
                    solution_rows[rows, :] = guess_ref[x, own] + part[0:32]
                    residual_rows[rows, :] = one_ref[x, own] + part[32:64]
        for step in range(2):
            for copy in leaving(2 * pair + step):
                copy.start()
        return carry

    lax.fori_loop(0, nx // 2, at_pair, 0)
    for x in range(nx - slots, nx):
        for copy in leaving(x):
            copy.wait()


def combine(mix, guess, one, two, three):
    nx, ny, columns, nz = guess.shape
    return pl.pallas_call(
        combine_kernel,
        in_specs=[VMEM, HBM] + [VMEM] * 3,
        out_specs=[HBM] * 2,
        out_shape=[jax.ShapeDtypeStruct((columns, nx, ny, nz), F32)] * 2,
        scratch_shapes=[
            pltpu.VMEM(guess.shape, F32),
            pltpu.VMEM((8, ny // 8, columns, 8, nz), F32),
            pltpu.VMEM((8, ny // 8, columns, 8, nz), F32),
            pltpu.SemaphoreType.DMA((2, ny // 8, 8)),
            pltpu.SemaphoreType.DMA((nx,)),
        ],
        compiler_params=params(),
        name="combine_fields",
    )(mix, guess, one, two, three)


def swaps(axis, mask, stride=1):
    return [(i, i ^ (mask * stride)) for i in range(lax.axis_size(axis))]


def summed_but_last(values):
    groups = []
    for axis in AXES[::-1]:
        size, stride = lax.axis_size(axis), 1
        while size // stride > 4:
            values = values + lax.ppermute(values, axis, swaps(axis, 1, stride))
            stride *= 2
        groups.append((axis, stride))
    for place, (axis, stride) in enumerate(groups):
        others = [
            lax.ppermute(values, axis, swaps(axis, mask, stride))
            for mask in (1, 3, 2)
            if mask * stride < lax.axis_size(axis)
        ]
        if place + 1 < len(groups):
            for other in others:
                values = values + other
    return [values, *others]


def shards(perm_class, perm_table, boreholes, start_guess):
    columns, nx, ny, nz = start_guess.shape
    places = [lax.axis_index(axis) for axis in AXES]
    sizes = [lax.axis_size(axis) for axis in AXES]
    anchors = [place * size for place, size in zip(places, (nx, ny, nz))]
    totals = tuple(size * count for size, count in zip((nx, ny, nz), sizes))
    inside = []
    for place, size in zip(places, sizes):
        inside += [place > 0, place < size - 1]
    inside = jnp.broadcast_to(jnp.stack(inside + inside[:2]).astype(F32)[:, None], (8, nz))

    in_hbm = [
        pltpu.with_memory_space_constraint(held, pltpu.HBM)
        for held in (perm_class, perm_table, start_guess)
    ]
    guess, perm, *faces = pack(*in_hbm)
    guess = pltpu.with_memory_space_constraint(guess, pltpu.HBM)
    near, far = exchanged(*faces)
    code = local_sources(boreholes[:, None], anchors, nx, ny, nz, totals[1], totals[2])
    extra = (perm, inside, code)
    part, ends, wx, wy, *along_z = inner_part(guess, near, extra, True, False)
    residual, ends, wx, wy, *faces = sides_part(
        part, faces[:4], far, ends, [wx, wy, perm, inside], True, False
    )
    weights = (wx, wy, *along_z)
    near, far = exchanged(*faces, ends)
    part, ends, total = inner_part(residual, near, weights, False, False)
    once, ends, sums, *faces = sides_part(
        part, [residual], far, ends, [wx, wy, total], False, False
    )
    near, far = exchanged(*faces, ends)
    part, total = inner_part(once, near, weights, False, True)
    twice, sums = sides_part(part, [once], far, None, [wx, wy, total, sums], False, True)
    mix = solve(summed_but_last(sums))
    return tuple(combine(mix, guess, residual, once, twice))


def solution(mesh):
    placed = (P("strike", "dip", "layer"), P(), P(), P(None, "strike", "dip", "layer"))
    return jax.shard_map(
        shards,
        mesh=mesh,
        in_specs=placed,
        out_specs=(P(None, "strike", "dip", "layer"), P(None, "strike", "dip", "layer")),
        check_vma=False,
    )
```

```python
import functools

import jax
import jax.numpy as jnp
from jax import lax
from jax.experimental import pallas as pl
from jax.experimental.pallas import tpu as pltpu
from jax.sharding import PartitionSpec as P

LEAKAGE = 0.01
HIGHEST = lax.Precision.HIGHEST
F32 = jnp.float32
BF16 = jnp.bfloat16
VMEM_LIMIT = 24 * 1024 * 1024
AXES = ("strike", "dip", "layer")
VMEM = pl.BlockSpec(memory_space=pltpu.VMEM)
SMEM = pl.BlockSpec(memory_space=pltpu.SMEM)
HBM = pl.BlockSpec(memory_space=pltpu.HBM)


def params(**more):
    return pltpu.CompilerParams(vmem_limit_bytes=VMEM_LIMIT, **more)


def shaped(*shape):
    return pltpu.VMEM(shape, F32)


def lanes(rows):
    return lax.broadcasted_iota(jnp.int32, (rows, 128), 1)


def rows_of(count):
    return lax.broadcasted_iota(jnp.int32, (count, 128), 0)


def packed_ends(cells, y, into):
    turned = pltpu.roll(cells, 2 * y + 1, 1)
    lane = lanes(cells.shape[0])
    return jnp.where((lane == 2 * y) | (lane == 2 * y + 1), turned, into)


def place_x(tile, x, ref, plane, rows):
    turned = pltpu.roll(tile, (x % 4) * 32, 1)
    lane = lanes(tile.shape[0])
    mine = (lane // 32) == (x % 4)
    ref[plane, rows, :] = jnp.where(mine, turned, ref[plane, rows, :])


def pack_kernel(
    class_hbm, table_hbm, guess_hbm, field_hbm, perm_ref, xlo, xhi, ylo, yhi, ends_ref,
    classes, table, guess, field_ref, plane_sem, field_sem, class_sem, table_sem,
):
    columns, nx, ny, nz = guess_hbm.shape

    def plane(x):
        return pltpu.make_async_copy(guess_hbm.at[:, x], guess.at[x], plane_sem.at[x])

    def leaving(x):
        return pltpu.make_async_copy(field_ref.at[x], field_hbm.at[x], field_sem.at[x])

    class_copy = pltpu.make_async_copy(class_hbm, classes, class_sem)
    table_copy = pltpu.make_async_copy(table_hbm, table, table_sem)
    for x in range(nx):
        plane(x).start()
    table_copy.start()
    class_copy.start()
    ends_ref[...] = jnp.zeros_like(ends_ref)
    for ref in (xlo, xhi, ylo, yhi):
        ref[ny] = jnp.zeros((columns, nz), F32)
    lane = lanes(ny)
    row = rows_of(ny)

    def permeability(x):
        perm = jnp.zeros((ny, nz), F32)
        for level in range(table.shape[0]):
            perm = jnp.where(classes[x] == level, table[level], perm)
        perm_ref[x] = perm
        ylo[ny, pl.ds(x, 1), :] = perm[0:1]
        yhi[ny, pl.ds(x, 1), :] = perm[ny - 1 : ny]
        first = jnp.broadcast_to(perm[:, 0:1], (ny, nz))
        final = jnp.broadcast_to(perm[:, nz - 1 : nz], (ny, nz))
        both = jnp.where(lane == 2 * row, final, jnp.where(lane == 2 * row + 1, first, 0.0))
        edge = jnp.sum(both, axis=0, keepdims=True)
        return jnp.where((lanes(1) // 32) == x % 4, pltpu.roll(edge, (x % 4) * 32, 1), 0.0)

    def four(block, carry):
        edges = [permeability(4 * block + step) for step in range(4)]
        ends_ref[4, pl.ds(block, 1), :] = (edges[0] + edges[1]) + (edges[2] + edges[3])
        return carry

    def cells_of(pair, carry):
        for step in range(2):
            plane(2 * pair + step).wait()
        for step in range(2):
            x = 2 * pair + step
            flat = guess.at[x].reshape(columns * ny, nz)
            ends = jnp.zeros((columns, nz), F32)
            for y in range(ny):
                cells = flat[pl.ds(y, columns, stride=ny), :]
                field_ref[x, y] = cells
                ends = packed_ends(cells, y, ends)
                if y == 0:
                    ylo[x] = cells
                if y == ny - 1:
                    yhi[x] = cells
            place_x(ends, x, ends_ref, x // 4, slice(None))
            leaving(x).start()
        return carry

    lax.fori_loop(0, nx // 2, cells_of, 0)
    table_copy.wait()
    class_copy.wait()
    lax.fori_loop(0, nx // 4, four, 0)
    xlo[ny, 0:ny, :] = perm_ref[0]
    xhi[ny, 0:ny, :] = perm_ref[nx - 1]
    for y in range(ny):
        xlo[y] = field_ref[0, y]
        xhi[y] = field_ref[nx - 1, y]
    for x in range(nx):
        leaving(x).wait()


def pack(perm_class, perm_table, start_guess):
    columns, nx, ny, nz = start_guess.shape
    face = shaped(ny + 1, columns, nz)
    return pl.pallas_call(
        pack_kernel,
        in_specs=[HBM] * 3,
        out_specs=[HBM] + [VMEM] * 6,
        out_shape=[
            pltpu.HBM((nx, ny, columns, nz), F32),
            shaped(nx, ny, nz),
            face,
            face,
            shaped(nx + 1, columns, nz),
            shaped(nx + 1, columns, nz),
            shaped(5, columns, nz),
        ],
        scratch_shapes=[
            pltpu.VMEM((nx, ny, nz), jnp.int32),
            pltpu.SMEM(perm_table.shape, F32),
            pltpu.VMEM((nx, columns, ny, nz), F32),
            pltpu.VMEM((nx, ny, columns, nz), F32),
            pltpu.SemaphoreType.DMA((nx,)),
            pltpu.SemaphoreType.DMA((nx,)),
            pltpu.SemaphoreType.DMA(()),
            pltpu.SemaphoreType.DMA(()),
        ],
        compiler_params=pltpu.CompilerParams(vmem_limit_bytes=VMEM_LIMIT),
        name="pack_guess",
    )(perm_class, perm_table, start_guess)


def face_weight(center_k, beside_k):
    summed = center_k + beside_k
    divisor = jnp.where(summed > 0.0, summed, 1.0)
    return jnp.where(summed > 0.0, 2.0 * center_k * beside_k / divisor, 0.0)


def arrived(left, right, left_scale=None, right_scale=None):
    after = pltpu.roll(right, 127, 1)
    before = pltpu.roll(left, 1, 1)
    if left_scale is not None:
        after, before = after * right_scale, before * left_scale
    return jnp.where(lanes(left.shape[0]) % 2 == 0, after, before)


def inner_weights(perm_ref, inside, hz, wx, wy, wzm, wzp, wze):
    nx, ny, nz = perm_ref.shape
    lane = lanes(ny)
    row = rows_of(ny)

    def at_x(x):
        center = perm_ref[x]
        wx[x] = face_weight(center, perm_ref[jnp.maximum(x - 1, 0)])
        below = jnp.concatenate([center[:1], center[: ny - 1]], axis=0)
        wy[x, 0:ny, :] = face_weight(center, below)
        ends = arrived(
            hz[0][4, pl.ds(x // 4, 1), :], hz[1][4, pl.ds(x // 4, 1), :], inside[4:5], inside[5:6]
        )
        ends = jnp.broadcast_to(ends, (ny, nz))
        offset = (x % 4) * 32 + 2 * row
        after = jnp.sum(jnp.where(lane == offset, ends, 0.0), axis=1, keepdims=True)
        ahead = jnp.sum(jnp.where(lane == offset + 1, ends, 0.0), axis=1, keepdims=True)
        down = face_weight(center, jnp.where(lane == 0, ahead, pltpu.roll(center, 1, 1)))
        up = face_weight(center, jnp.where(lane == nz - 1, after, pltpu.roll(center, nz - 1, 1)))
        wzm[x] = down
        wzp[x] = up
        first = jnp.broadcast_to(down[:, 0:1], (ny, nz))
        final = jnp.broadcast_to(up[:, nz - 1 : nz], (ny, nz))
        both = jnp.where(lane == 2 * row, final, jnp.where(lane == 2 * row + 1, first, 0.0))
        return jnp.sum(both, axis=0, keepdims=True)

    def at_four(block, carry):
        edges = [at_x(4 * block + step) for step in range(4)]
        for step in range(4):
            wze[pl.ds(4 * block + step, 1), :] = edges[step]
        return carry

    lax.fori_loop(0, nx // 4, at_four, 0)


def outer_weights(perm_ref, inside, hx, hy, wx, wy):
    nx, ny, nz = perm_ref.shape
    wx[0] = face_weight(perm_ref[0], hx[0][...] * inside[0:1])
    wx[nx] = face_weight(perm_ref[nx - 1], hx[1][...] * inside[1:2])
    low = jnp.concatenate([perm_ref[x, 0:1, :] for x in range(nx)], axis=0)
    high = jnp.concatenate([perm_ref[x, ny - 1 : ny, :] for x in range(nx)], axis=0)
    low = face_weight(low, hy[0][0:nx] * inside[2:3])
    high = face_weight(high, hy[1][0:nx] * inside[3:4])
    for x in range(nx):
        wy[x, 0:1, :] = low[x : x + 1]
        wy[x, ny : ny + 1, :] = high[x : x + 1]


def local_sources(boreholes, anchors, nx, ny, nz, total_y, total_z):
    cell = jnp.broadcast_to(boreholes, (boreholes.shape[0], nz))
    along_z = cell % total_z - anchors[2]
    along_y = (cell // total_z) % total_y - anchors[1]
    along_x = cell // (total_z * total_y) - anchors[0]
    inside = (along_x >= 0) & (along_x < nx) & (along_y >= 0) & (along_y < ny)
    matched = inside & (along_z == lanes(boreholes.shape[0]))
    return jnp.where(matched, along_x * ny + along_y, -1)


def difference_matrix(matrix):
    size = matrix.shape[0] // 2
    source = lax.broadcasted_iota(jnp.int32, matrix.shape, 0) % size
    target = lax.broadcasted_iota(jnp.int32, matrix.shape, 1)
    beside = jnp.where(target < size, target + 1, target - size - 1)
    same = jnp.where(source == target % size, 1.0, 0.0)
    matrix[...] = (same - jnp.where(source == beside, 1.0, 0.0)).astype(BF16)


def first_kernel(
    away, hzl, hzr, perm, inside, code, out, ends, wx, wy, wzm, wzp, wze, flux, field, plane_sem
):
    nx, ny, columns, nz = field.shape

    def plane(x):
        return pltpu.make_async_copy(away.at[x], field.at[x], plane_sem.at[x])

    for x in range(nx):
        plane(x).start()
    ends[...] = jnp.zeros_like(ends)
    inner_weights(perm, inside, (hzl, hzr), wx, wy, wzm, wzp, wze)
    flux[...] = jnp.zeros_like(flux)
    plane(0).wait()

    def at_x(x, beside):
        block = x // 4
        beyond = arrived(hzl[block], hzr[block])
        beyond = pltpu.roll(beyond, (128 - (x % 4) * 32) % 128, 1)
        lane = lanes(columns)
        center = field[x, 0]
        flux_y = None
        mine = jnp.zeros((columns, nz), F32)
        for y in range(ny):
            applied = LEAKAGE * center - flux[y]
            if beside is not None:
                flux_x = wx[x + 1, y : y + 1, :] * (center - beside[y])
                applied = applied + flux_x
                flux[y] = flux_x
            if flux_y is not None:
                applied = applied - flux_y
            if y + 1 < ny:
                following = field[x, y + 1]
                flux_y = wy[x, y + 1 : y + 2, :] * (center - following)
                applied = applied + flux_y
            edge = pltpu.roll(beyond, (128 - (2 * y + 1)) % 128, 1)
            after = jnp.where(lane == nz - 1, edge, pltpu.roll(center, nz - 1, 1))
            before = jnp.where(lane == 0, edge, pltpu.roll(center, 1, 1))
            applied = applied + wzp[x, y : y + 1, :] * (center - after)
            applied = applied + wzm[x, y : y + 1, :] * (center - before)
            applied = jnp.where(code[...] == x * ny + y, 1.0, 0.0) - applied
            out[x, y] = applied
            mine = packed_ends(applied, y, mine)
            center = following
        place_x(mine, x, ends, block, slice(None))

    def inner(x, carry):
        plane(x + 1).wait()
        at_x(x, field.at[x + 1])
        return carry

    lax.fori_loop(0, nx - 1, inner, 0)
    at_x(nx - 1, None)


def inner_kernel(last, *refs):
    refs = list(refs)
    take = lambda count: [refs.pop(0) for _ in range(count)]
    field, hzl, hzr, wx, wy, wzm, wzp, wze, out = take(9)
    if not last:
        (ends,) = take(1)
    total, flux, matrix, even, odd, even_halves, odd_halves = take(7)
    nx, ny, columns, nz = field.shape
    if not last:
        ends[...] = jnp.zeros_like(ends)
    difference_matrix(matrix)
    total[...] = jnp.zeros_like(total)
    flux[...] = jnp.zeros_like(flux)

    def differences(x, across, halves):
        plane = field[x].reshape(ny * columns, nz)
        high = plane.astype(BF16)
        low = (plane - high.astype(F32)).astype(BF16)
        both = jnp.concatenate([high, low], axis=1)
        halves[...] = both
        across[...] = jnp.dot(both, matrix[...], preferred_element_type=F32)

    def products(x, halves):
        left = jnp.concatenate(
            [
                jnp.concatenate(
                    [halves[y * columns : (y + 1) * columns, half] for y in range(ny)], axis=1
                )
                for half in (slice(0, nz), slice(nz, 2 * nz))
            ],
            axis=0,
        )
        right = split([jnp.concatenate([out[x, y] for y in range(ny)], axis=1)])
        total[...] += gram(left, jnp.concatenate([left, right], axis=0))

    def stencil(x, across, beside):
        block = x // 4
        beyond = arrived(hzl[block], hzr[block])
        beyond = pltpu.roll(beyond, (128 - (x % 4) * 32) % 128, 1)
        beyond = beyond * wze[pl.ds(x, 1), :]
        lane = lanes(columns)
        outer = (lane == 0) | (lane == nz - 1)
        center = field[x, 0]
        flux_y = None
        mine = jnp.zeros((columns, nz), F32)
        for y in range(ny):
            rows = slice(y * columns, (y + 1) * columns)
            applied = LEAKAGE * center - flux[y]
            if beside is not None:
                flux_x = wx[x + 1, y : y + 1, :] * (center - beside[y])
                applied = applied + flux_x
                flux[y] = flux_x
            if flux_y is not None:
                applied = applied - flux_y
            if y + 1 < ny:
                following = field[x, y + 1]
                flux_y = wy[x, y + 1 : y + 2, :] * (center - following)
                applied = applied + flux_y
            applied = applied + wzp[x, y : y + 1, :] * across[rows, 0:nz]
            applied = applied + wzm[x, y : y + 1, :] * across[rows, nz : 2 * nz]
            edge = pltpu.roll(beyond, (128 - (2 * y + 1)) % 128, 1)
            applied = applied - jnp.where(outer, edge, 0.0)
            out[x, y] = applied
            if not last:
                mine = packed_ends(applied, y, mine)
            center = following
        if not last:
            place_x(mine, x, ends, block, slice(None))

    def step(x, here, there, halves):
        products(x - 1, halves)
        differences(x + 1, there, halves)
        stencil(x, here, field.at[x + 1])

    def pair(place, carry):
        step(2 * place + 1, odd, even, even_halves)
        step(2 * place + 2, even, odd, odd_halves)
        return carry

    differences(0, even, even_halves)
    differences(1, odd, odd_halves)
    stencil(0, even, field.at[1])
    lax.fori_loop(0, nx // 2 - 1, pair, 0)
    products(nx - 2, even_halves)
    stencil(nx - 1, odd, None)
    products(nx - 1, odd_halves)


def sides_kernel(first, last, *refs):
    refs = list(refs)
    take = lambda count: [refs.pop(0) for _ in range(count)]
    part = take(1)[0]
    if first:
        own_faces = take(4)
    else:
        (field,) = take(1)
    hxl, hxr, hyl, hyr = take(4)
    if not last:
        take(1)
    if first:
        take(2)
        perm, inside = take(2)
    else:
        wx, wy, total = take(3)
    if last:
        (earlier,) = take(1)
    (out,) = take(1)
    if not last:
        (ends,) = take(1)
    if first:
        wx, wy = take(2)
    else:
        (sums,) = take(1)
    if not last:
        xlo, xhi, ylo, yhi = take(4)
    nx, ny, columns, nz = part.shape
    lane = lanes(columns)
    if first:
        hx = (hxl.at[ny, 0:ny], hxr.at[ny, 0:ny])
        outer_weights(perm, inside, hx, (hyl.at[ny], hyr.at[ny]), wx, wy)

    added = None
    faces = (
        (hxl, [(0, y) for y in range(ny)], [(0, y) for y in range(ny)], wx),
        (hxr, [(nx - 1, y) for y in range(ny)], [(nx, y) for y in range(ny)], wx),
        (hyl, [(x, 0) for x in range(nx)], [(x, 0) for x in range(nx)], wy),
        (hyr, [(x, ny - 1) for x in range(nx)], [(x, ny) for x in range(nx)], wy),
    )
    for side, (halo, rows, weight_rows, weight) in enumerate(faces):
        own, fluxes = [], []
        for place, ((x, y), (p, q)) in enumerate(zip(rows, weight_rows)):
            center = own_faces[side][place] if first else field[x, y]
            flux = weight[p, q : q + 1, :] * (center - halo[place])
            if first:
                out[x, y] -= flux
            else:
                out[x, y] += flux
                own.append(center)
                fluxes.append(flux)
        if not first:
            left = split([jnp.concatenate(own, axis=1)])
            right = split([jnp.concatenate(fluxes, axis=1)])
            part = gram(left, right)
            added = part if added is None else added + part
    if not last:
        for x in range(nx):
            tile = ends[x // 4]
            for y in range(ny):
                if x in (0, nx - 1) or y in (0, ny - 1):
                    tile = packed_ends(out[x, y], (x % 4) * 16 + y, tile)
            ends[x // 4] = tile
        for y in range(ny):
            xlo[y] = out[0, y]
            xhi[y] = out[nx - 1, y]
        for x in range(nx):
            ylo[x] = out[x, 0]
            yhi[x] = out[x, ny - 1]
    if not first:
        held = total[...]
        held = held[0:32] + held[32:64]
        held = held + pltpu.roll(held, 96, 1)
        held = jnp.where(lane < 32, held, pltpu.roll(held, 96, 1))
        fixed = added[0:32] + added[32:64]
        fixed = fixed[:, 0:32] + fixed[:, 32:64]
        fixed = jnp.concatenate([fixed, jnp.zeros((columns, 96), F32)], axis=1)
        held = jnp.where(lane < 32, held, held + pltpu.roll(fixed, 32, 1))
        if last:
            held = jnp.where(lane < 64, earlier[...], pltpu.roll(held, 64, 1))
        sums[...] = held


def split(fields):
    high = [field.astype(BF16) for field in fields]
    low = [(field - top.astype(F32)).astype(BF16) for field, top in zip(fields, high)]
    return jnp.concatenate(high + low, axis=0)


def gram(left, right):
    return lax.dot_general(left, right, (((1,), (1,)), ((), ())), preferred_element_type=F32)


def fold(products, fields):
    half = products.shape[0] // 2
    summed = products[:half] + products[half:]
    return summed[:, :half] + summed[:, half:]


def inner_part(field, halos, extra, first, last):
    nx, ny, columns, nz = field.shape
    in_specs = [HBM if first else VMEM] + [VMEM] * (len(halos) + len(extra))
    scratch = [pltpu.VMEM((ny, columns, nz), F32)]
    out_shape = [shaped(nx, ny, columns, nz)]
    if not last:
        out_shape += [shaped(4, columns, nz)]
    if first:
        scratch += [pltpu.VMEM(field.shape, F32), pltpu.SemaphoreType.DMA((nx,))]
        out_shape += [
            shaped(nx + 1, ny, nz),
            shaped(nx, ny + 8, nz),
            shaped(nx, ny, nz),
            shaped(nx, ny, nz),
            shaped(nx, nz),
        ]
    else:
        scratch += [pltpu.VMEM((2 * nz, 2 * nz), BF16)]
        scratch += [pltpu.VMEM((ny * columns, 2 * nz), F32)] * 2
        scratch += [pltpu.VMEM((ny * columns, 2 * nz), BF16)] * 2
        out_shape += [shaped(2 * columns, 4 * columns)]
    return pl.pallas_call(
        first_kernel if first else functools.partial(inner_kernel, last),
        in_specs=in_specs,
        out_specs=[VMEM] * len(out_shape),
        out_shape=out_shape,
        scratch_shapes=scratch,
        compiler_params=params(),
        cost_estimate=pl.CostEstimate(
            flops=20 * field.size, bytes_accessed=6 * field.size * 4, transcendentals=0
        ),
        name="inner_first" if first else "inner_last" if last else "inner_next",
    )(field, *halos, *extra)


def sides_part(part, own, halos, ends, extra, first, last):
    nx, ny, columns, nz = part.shape
    operands = [part, *own, *halos]
    place = len(operands)
    if not last:
        operands += [ends]
    operands += extra
    in_specs = [VMEM] * len(operands)
    aliases = {0: 0}
    out_shape = [shaped(*part.shape)]
    if not last:
        aliases[place] = 1
        out_shape += [shaped(*ends.shape)]
    if first:
        aliases[place + 1] = 2
        aliases[place + 2] = 3
        out_shape += [shaped(*extra[0].shape), shaped(*extra[1].shape)]
    else:
        out_shape += [shaped(columns, 128)]
    if not last:
        out_shape += [shaped(ny, columns, nz)] * 2 + [shaped(nx, columns, nz)] * 2
    return pl.pallas_call(
        functools.partial(sides_kernel, first, last),
        in_specs=in_specs,
        out_specs=[VMEM] * len(out_shape),
        out_shape=out_shape,
        input_output_aliases=aliases,
        compiler_params=params(),
        name="sides_first" if first else "sides_last" if last else "sides_next",
    )(*operands)


def exchanged(xlo, xhi, ylo, yhi, ends):
    ahead = lambda axis: [(i, (i + 1) % lax.axis_size(axis)) for i in range(lax.axis_size(axis))]
    back = lambda axis: [(j, i) for i, j in ahead(axis)]
    near = (
        lax.ppermute(ends, "layer", ahead("layer")),
        lax.ppermute(ends, "layer", back("layer")),
    )
    near, yhi = lax.optimization_barrier((near, yhi))
    far = (
        lax.ppermute(xhi, "strike", ahead("strike")),
        lax.ppermute(xlo, "strike", back("strike")),
        lax.ppermute(yhi, "dip", ahead("dip")),
        lax.ppermute(ylo, "dip", back("dip")),
    )
    return near, far


def dot(left, right, contract=(1, 0)):
    dims = (((contract[0],), (contract[1],)), ((), ()))
    return lax.dot_general(left, right, dims, precision=HIGHEST, preferred_element_type=F32)


def eliminate(tables):
    row = rows_of(32)
    for k in range(0, 32, 2):
        done = []
        for table in tables:
            one = jnp.broadcast_to(table[:, k : k + 1], table.shape)
            two = jnp.broadcast_to(table[:, k + 1 : k + 2], table.shape)
            a, b = one[k : k + 1], two[k : k + 1]
            c, d = one[k + 1 : k + 2], two[k + 1 : k + 2]
            scale = 1.0 / (a * d - b * c)
            upper, lower = table[k : k + 1], table[k + 1 : k + 2]
            first = (d * upper - b * lower) * scale
            second = (a * lower - c * upper) * scale
            rest = (table - one * first) - two * second
            done.append(jnp.where(row == k, first, jnp.where(row == k + 1, second, rest)))
        tables = done
    return tables


def solve_kernel(*refs):
    out_ref = refs[-1]
    sums = refs[0][...]
    for ref in refs[1:-1]:
        sums = sums + ref[...]
    lane = lanes(32)
    row = rows_of(32)
    table = jnp.where(lane < 32, pltpu.roll(sums, 96, 1), pltpu.roll(sums, 32, 1))
    table = jnp.where(lane < 64, table, jnp.where(lane == row + 64, 1.0, 0.0))
    (table,) = eliminate([table])
    norm = sums[:, 0:32]
    square = sums[:, 64:96]
    cube = sums[:, 96:128]
    advance = table[:, 32:64]
    inverse = table[:, 64:96]
    advance_t = advance.T
    turned = dot(square, advance)
    tripled = dot(advance, dot(cube, advance), (0, 0))
    mixing = dot(inverse, turned)
    norm_next = dot(advance, turned, (0, 0)) - norm
    curvature = tripled - dot(turned, mixing, (0, 0))
    wide = jnp.concatenate([curvature, norm_next, jnp.zeros((32, 64), F32)], axis=1)
    (wide,) = eliminate([wide])
    later = wide[:, 32:64]
    taken_t = advance_t + dot(later, mixing, (0, 1))
    beyond_t = dot(later, advance, (0, 1))
    nothing = jnp.zeros((32, 32), F32)
    out_ref[0:32, :] = jnp.concatenate([taken_t, -beyond_t, nothing, nothing], axis=1)
    out_ref[32:64, :] = jnp.concatenate([nothing, -taken_t, beyond_t, nothing], axis=1)


def solve(parts):
    return pl.pallas_call(
        solve_kernel,
        in_specs=[VMEM] * len(parts),
        out_specs=VMEM,
        out_shape=shaped(64, 128),
        compiler_params=params(),
        name="solve_small",
    )(*parts)


def combine_kernel(
    mix_ref, guess_ref, one_ref, two_ref, three_ref, solution_hbm, residual_hbm,
    solution, residual, sem,
):
    nx, ny, columns, nz = guess_ref.shape
    slots = solution.shape[0]

    mix = mix_ref[...]
    high = mix.astype(BF16)
    low = (mix - high.astype(F32)).astype(BF16)
    mixing = jnp.concatenate(
        [
            jnp.concatenate([half[:, : 3 * columns], half[:, : 3 * columns]], axis=1)
            for half in (high, low)
        ],
        axis=0,
    )

    def leaving(x):
        slot = x % slots
        copies = []
        for place, (held, away) in enumerate(((solution, solution_hbm), (residual, residual_hbm))):
            for half in range(ny // 8):
                copies.append(
                    pltpu.make_async_copy(
                        held.at[slot, half],
                        away.at[:, x, 8 * half : 8 * half + 8],
                        sem.at[place, half, slot],
                    )
                )
        return copies

    mix = mix_ref[...]
    high = mix.astype(BF16)
    low = (mix - high.astype(F32)).astype(BF16)
    mixing = jnp.concatenate(
        [
            jnp.concatenate([half[:, : 3 * columns], half[:, : 3 * columns]], axis=1)
            for half in (high, low)
        ],
        axis=0,
    )

    def at_pair(pair, carry):
        @pl.when(2 * pair >= slots)
        def _():
            for step in range(2):
                for copy in leaving(2 * pair + step - slots):
                    copy.wait()

        for step in range(2):
            x = 2 * pair + step
            slot = lax.rem(x, slots)
            solution_rows = solution.at[slot].reshape(columns * ny, nz)
            residual_rows = residual.at[slot].reshape(columns * ny, nz)
            for y in range(0, ny, 2):
                fields = [
                    jnp.concatenate([ref[x, y], ref[x, y + 1]], axis=1)
                    for ref in (one_ref, two_ref, three_ref)
                ]
                mixed = jnp.dot(mixing, split(fields), preferred_element_type=F32)
                mixed = mixed[0:64] + mixed[64:128]
                for z in range(2):
                    own = y + z
                    rows = pl.ds((own // 8) * 8 * columns + own % 8, columns, stride=8)
                    part = mixed[:, z * nz : (z + 1) * nz]
                    solution_rows[rows, :] = guess_ref[x, own] + part[0:32]
                    residual_rows[rows, :] = one_ref[x, own] + part[32:64]
        for step in range(2):
            for copy in leaving(2 * pair + step):
                copy.start()
        return carry

    lax.fori_loop(0, nx // 2, at_pair, 0)
    for x in range(nx - slots, nx):
        for copy in leaving(x):
            copy.wait()


def combine(mix, guess, one, two, three):
    nx, ny, columns, nz = guess.shape
    return pl.pallas_call(
        combine_kernel,
        in_specs=[VMEM] * 5,
        out_specs=[HBM] * 2,
        out_shape=[jax.ShapeDtypeStruct((columns, nx, ny, nz), F32)] * 2,
        scratch_shapes=[
            pltpu.VMEM((8, ny // 8, columns, 8, nz), F32),
            pltpu.VMEM((8, ny // 8, columns, 8, nz), F32),
            pltpu.SemaphoreType.DMA((2, ny // 8, 8)),
        ],
        compiler_params=params(),
        name="combine_fields",
    )(mix, guess, one, two, three)


def swaps(axis, mask, stride=1):
    return [(i, i ^ (mask * stride)) for i in range(lax.axis_size(axis))]


def summed_but_last(values):
    groups = []
    for axis in AXES[::-1]:
        size, stride = lax.axis_size(axis), 1
        while size // stride > 4:
            values = values + lax.ppermute(values, axis, swaps(axis, 1, stride))
            stride *= 2
        groups.append((axis, stride))
    for place, (axis, stride) in enumerate(groups):
        others = [
            lax.ppermute(values, axis, swaps(axis, mask, stride))
            for mask in (1, 3, 2)
            if mask * stride < lax.axis_size(axis)
        ]
        if place + 1 < len(groups):
            for other in others:
                values = values + other
    return [values, *others]


def shards(perm_class, perm_table, boreholes, start_guess):
    columns, nx, ny, nz = start_guess.shape
    places = [lax.axis_index(axis) for axis in AXES]
    sizes = [lax.axis_size(axis) for axis in AXES]
    anchors = [place * size for place, size in zip(places, (nx, ny, nz))]
    totals = tuple(size * count for size, count in zip((nx, ny, nz), sizes))
    inside = []
    for place, size in zip(places, sizes):
        inside += [place > 0, place < size - 1]
    inside = jnp.broadcast_to(jnp.stack(inside + inside[:2]).astype(F32)[:, None], (8, nz))

    in_hbm = [
        pltpu.with_memory_space_constraint(held, pltpu.HBM)
        for held in (perm_class, perm_table, start_guess)
    ]
    guess, perm, *faces = pack(*in_hbm)
    guess = pltpu.with_memory_space_constraint(guess, pltpu.HBM)
    near, far = exchanged(*faces)
    code = local_sources(boreholes[:, None], anchors, nx, ny, nz, totals[1], totals[2])
    extra = (perm, inside, code)
    part, ends, wx, wy, *along_z = inner_part(guess, near, extra, True, False)
    residual, ends, wx, wy, *faces = sides_part(
        part, faces[:4], far, ends, [wx, wy, perm, inside], True, False
    )
    weights = (wx, wy, *along_z)
    near, far = exchanged(*faces, ends)
    part, ends, total = inner_part(residual, near, weights, False, False)
    once, ends, sums, *faces = sides_part(
        part, [residual], far, ends, [wx, wy, total], False, False
    )
    near, far = exchanged(*faces, ends)
    part, total = inner_part(once, near, weights, False, True)
    twice, sums = sides_part(part, [once], far, None, [wx, wy, total, sums], False, True)
    mix = solve(summed_but_last(sums))
    guess = pltpu.with_memory_space_constraint(guess, pltpu.VMEM)
    return tuple(combine(mix, guess, residual, once, twice))


def solution(mesh):
    placed = (P("strike", "dip", "layer"), P(), P(), P(None, "strike", "dip", "layer"))
    return jax.shard_map(
        shards,
        mesh=mesh,
        in_specs=placed,
        out_specs=(P(None, "strike", "dip", "layer"), P(None, "strike", "dip", "layer")),
        check_vma=False,
    )
```

```python
import functools

import jax
import jax.numpy as jnp
from jax import lax
from jax.experimental import pallas as pl
from jax.experimental.pallas import tpu as pltpu
from jax.sharding import PartitionSpec as P

LEAKAGE = 0.01
HIGHEST = lax.Precision.HIGHEST
F32 = jnp.float32
BF16 = jnp.bfloat16
VMEM_LIMIT = 24 * 1024 * 1024
AXES = ("strike", "dip", "layer")
VMEM = pl.BlockSpec(memory_space=pltpu.VMEM)
SMEM = pl.BlockSpec(memory_space=pltpu.SMEM)
HBM = pl.BlockSpec(memory_space=pltpu.HBM)


def params(**more):
    return pltpu.CompilerParams(vmem_limit_bytes=VMEM_LIMIT, **more)


def shaped(*shape):
    return pltpu.VMEM(shape, F32)


def lanes(rows):
    return lax.broadcasted_iota(jnp.int32, (rows, 128), 1)


def rows_of(count):
    return lax.broadcasted_iota(jnp.int32, (count, 128), 0)


def packed_ends(cells, y, into):
    turned = pltpu.roll(cells, 2 * y + 1, 1)
    lane = lanes(cells.shape[0])
    return jnp.where((lane == 2 * y) | (lane == 2 * y + 1), turned, into)


def place_x(tile, x, ref, plane, rows):
    turned = pltpu.roll(tile, (x % 4) * 32, 1)
    lane = lanes(tile.shape[0])
    mine = (lane // 32) == (x % 4)
    ref[plane, rows, :] = jnp.where(mine, turned, ref[plane, rows, :])


def pack_kernel(
    class_hbm, table_hbm, guess_hbm, field_hbm, perm_ref, xlo, xhi, ylo, yhi, ends_ref,
    classes, table, guess, field_ref, plane_sem, field_sem, class_sem, table_sem,
):
    columns, nx, ny, nz = guess_hbm.shape

    def plane(x):
        return pltpu.make_async_copy(
            guess_hbm.at[:, x], guess.at[x, 0:columns], plane_sem.at[x]
        )

    def leaving(x):
        return pltpu.make_async_copy(field_ref.at[x], field_hbm.at[x], field_sem.at[x])

    class_copy = pltpu.make_async_copy(class_hbm, classes, class_sem)
    table_copy = pltpu.make_async_copy(table_hbm, table, table_sem)
    for x in range(nx):
        plane(x).start()
    table_copy.start()
    class_copy.start()
    ends_ref[...] = jnp.zeros_like(ends_ref)
    for ref in (xlo, xhi, ylo, yhi):
        ref[ny] = jnp.zeros((columns, nz), F32)
    lane = lanes(ny)
    row = rows_of(ny)

    def permeability(x):
        perm = jnp.zeros((ny, nz), F32)
        for level in range(table.shape[0]):
            perm = jnp.where(classes[x] == level, table[level], perm)
        perm_ref[x] = perm
        ylo[ny, pl.ds(x, 1), :] = perm[0:1]
        yhi[ny, pl.ds(x, 1), :] = perm[ny - 1 : ny]
        first = jnp.broadcast_to(perm[:, 0:1], (ny, nz))
        final = jnp.broadcast_to(perm[:, nz - 1 : nz], (ny, nz))
        both = jnp.where(lane == 2 * row, final, jnp.where(lane == 2 * row + 1, first, 0.0))
        edge = jnp.sum(both, axis=0, keepdims=True)
        return jnp.where((lanes(1) // 32) == x % 4, pltpu.roll(edge, (x % 4) * 32, 1), 0.0)

    def four(block, carry):
        edges = [permeability(4 * block + step) for step in range(4)]
        ends_ref[4, pl.ds(block, 1), :] = (edges[0] + edges[1]) + (edges[2] + edges[3])
        return carry

    def cells_of(pair, carry):
        for step in range(2):
            plane(2 * pair + step).wait()
        for step in range(2):
            x = 2 * pair + step
            flat = guess.at[x].reshape((columns + 1) * ny, nz)
            ends = jnp.zeros((columns, nz), F32)
            for y in range(ny):
                cells = flat[pl.ds(y, columns, stride=ny), :]
                field_ref[x, y] = cells
                ends = packed_ends(cells, y, ends)
                if y == 0:
                    ylo[x] = cells
                if y == ny - 1:
                    yhi[x] = cells
            place_x(ends, x, ends_ref, x // 4, slice(None))
            leaving(x).start()
        return carry

    lax.fori_loop(0, nx // 2, cells_of, 0)
    table_copy.wait()
    class_copy.wait()
    lax.fori_loop(0, nx // 4, four, 0)
    xlo[ny, 0:ny, :] = perm_ref[0]
    xhi[ny, 0:ny, :] = perm_ref[nx - 1]
    for y in range(ny):
        xlo[y] = field_ref[0, y]
        xhi[y] = field_ref[nx - 1, y]
    for x in range(nx):
        leaving(x).wait()


def pack(perm_class, perm_table, start_guess):
    columns, nx, ny, nz = start_guess.shape
    face = shaped(ny + 1, columns, nz)
    return pl.pallas_call(
        pack_kernel,
        in_specs=[HBM] * 3,
        out_specs=[HBM] + [VMEM] * 6,
        out_shape=[
            pltpu.HBM((nx, ny, columns, nz), F32),
            shaped(nx, ny, nz),
            face,
            face,
            shaped(nx + 1, columns, nz),
            shaped(nx + 1, columns, nz),
            shaped(5, columns, nz),
        ],
        scratch_shapes=[
            pltpu.VMEM((nx, ny, nz), jnp.int32),
            pltpu.SMEM(perm_table.shape, F32),
            pltpu.VMEM((nx, columns + 1, ny, nz), F32),
            pltpu.VMEM((nx, ny, columns, nz), F32),
            pltpu.SemaphoreType.DMA((nx,)),
            pltpu.SemaphoreType.DMA((nx,)),
            pltpu.SemaphoreType.DMA(()),
            pltpu.SemaphoreType.DMA(()),
        ],
        compiler_params=pltpu.CompilerParams(vmem_limit_bytes=VMEM_LIMIT),
        name="pack_guess",
    )(perm_class, perm_table, start_guess)


def face_weight(center_k, beside_k):
    summed = center_k + beside_k
    divisor = jnp.where(summed > 0.0, summed, 1.0)
    return jnp.where(summed > 0.0, 2.0 * center_k * beside_k / divisor, 0.0)


def arrived(left, right, left_scale=None, right_scale=None):
    after = pltpu.roll(right, 127, 1)
    before = pltpu.roll(left, 1, 1)
    if left_scale is not None:
        after, before = after * right_scale, before * left_scale
    return jnp.where(lanes(left.shape[0]) % 2 == 0, after, before)


def inner_weights(perm_ref, inside, hz, wx, wy, wzm, wzp, wze):
    nx, ny, nz = perm_ref.shape
    lane = lanes(ny)
    row = rows_of(ny)

    def at_x(x):
        center = perm_ref[x]
        wx[x] = face_weight(center, perm_ref[jnp.maximum(x - 1, 0)])
        below = jnp.concatenate([center[:1], center[: ny - 1]], axis=0)
        wy[x, 0:ny, :] = face_weight(center, below)
        ends = arrived(
            hz[0][4, pl.ds(x // 4, 1), :], hz[1][4, pl.ds(x // 4, 1), :], inside[4:5], inside[5:6]
        )
        ends = jnp.broadcast_to(ends, (ny, nz))
        offset = (x % 4) * 32 + 2 * row
        after = jnp.sum(jnp.where(lane == offset, ends, 0.0), axis=1, keepdims=True)
        ahead = jnp.sum(jnp.where(lane == offset + 1, ends, 0.0), axis=1, keepdims=True)
        down = face_weight(center, jnp.where(lane == 0, ahead, pltpu.roll(center, 1, 1)))
        up = face_weight(center, jnp.where(lane == nz - 1, after, pltpu.roll(center, nz - 1, 1)))
        wzm[x] = down
        wzp[x] = up
        first = jnp.broadcast_to(down[:, 0:1], (ny, nz))
        final = jnp.broadcast_to(up[:, nz - 1 : nz], (ny, nz))
        both = jnp.where(lane == 2 * row, final, jnp.where(lane == 2 * row + 1, first, 0.0))
        return jnp.sum(both, axis=0, keepdims=True)

    def at_four(block, carry):
        edges = [at_x(4 * block + step) for step in range(4)]
        for step in range(4):
            wze[pl.ds(4 * block + step, 1), :] = edges[step]
        return carry

    lax.fori_loop(0, nx // 4, at_four, 0)


def outer_weights(perm_ref, inside, hx, hy, wx, wy):
    nx, ny, nz = perm_ref.shape
    wx[0] = face_weight(perm_ref[0], hx[0][...] * inside[0:1])
    wx[nx] = face_weight(perm_ref[nx - 1], hx[1][...] * inside[1:2])
    low = jnp.concatenate([perm_ref[x, 0:1, :] for x in range(nx)], axis=0)
    high = jnp.concatenate([perm_ref[x, ny - 1 : ny, :] for x in range(nx)], axis=0)
    low = face_weight(low, hy[0][0:nx] * inside[2:3])
    high = face_weight(high, hy[1][0:nx] * inside[3:4])
    for x in range(nx):
        wy[x, 0:1, :] = low[x : x + 1]
        wy[x, ny : ny + 1, :] = high[x : x + 1]


def local_sources(boreholes, anchors, nx, ny, nz, total_y, total_z):
    cell = jnp.broadcast_to(boreholes, (boreholes.shape[0], nz))
    along_z = cell % total_z - anchors[2]
    along_y = (cell // total_z) % total_y - anchors[1]
    along_x = cell // (total_z * total_y) - anchors[0]
    inside = (along_x >= 0) & (along_x < nx) & (along_y >= 0) & (along_y < ny)
    matched = inside & (along_z == lanes(boreholes.shape[0]))
    return jnp.where(matched, along_x * ny + along_y, -1)


def difference_matrix(matrix):
    size = matrix.shape[0] // 2
    source = lax.broadcasted_iota(jnp.int32, matrix.shape, 0) % size
    target = lax.broadcasted_iota(jnp.int32, matrix.shape, 1)
    beside = jnp.where(target < size, target + 1, target - size - 1)
    same = jnp.where(source == target % size, 1.0, 0.0)
    matrix[...] = (same - jnp.where(source == beside, 1.0, 0.0)).astype(BF16)


def first_kernel(
    away, hzl, hzr, perm, inside, code, out, ends, wx, wy, wzm, wzp, wze, flux, field, plane_sem
):
    nx, ny, columns, nz = field.shape

    def plane(x):
        return pltpu.make_async_copy(away.at[x], field.at[x], plane_sem.at[x])

    for x in range(nx):
        plane(x).start()
    ends[...] = jnp.zeros_like(ends)
    inner_weights(perm, inside, (hzl, hzr), wx, wy, wzm, wzp, wze)
    flux[...] = jnp.zeros_like(flux)
    plane(0).wait()

    def at_x(x, beside):
        block = x // 4
        beyond = arrived(hzl[block], hzr[block])
        beyond = pltpu.roll(beyond, (128 - (x % 4) * 32) % 128, 1)
        lane = lanes(columns)
        center = field[x, 0]
        flux_y = None
        mine = jnp.zeros((columns, nz), F32)
        for y in range(ny):
            applied = LEAKAGE * center - flux[y]
            if beside is not None:
                flux_x = wx[x + 1, y : y + 1, :] * (center - beside[y])
                applied = applied + flux_x
                flux[y] = flux_x
            if flux_y is not None:
                applied = applied - flux_y
            if y + 1 < ny:
                following = field[x, y + 1]
                flux_y = wy[x, y + 1 : y + 2, :] * (center - following)
                applied = applied + flux_y
            edge = pltpu.roll(beyond, (128 - (2 * y + 1)) % 128, 1)
            after = jnp.where(lane == nz - 1, edge, pltpu.roll(center, nz - 1, 1))
            before = jnp.where(lane == 0, edge, pltpu.roll(center, 1, 1))
            applied = applied + wzp[x, y : y + 1, :] * (center - after)
            applied = applied + wzm[x, y : y + 1, :] * (center - before)
            applied = jnp.where(code[...] == x * ny + y, 1.0, 0.0) - applied
            out[x, y] = applied
            mine = packed_ends(applied, y, mine)
            center = following
        place_x(mine, x, ends, block, slice(None))

    def inner(x, carry):
        plane(x + 1).wait()
        at_x(x, field.at[x + 1])
        return carry

    lax.fori_loop(0, nx - 1, inner, 0)
    at_x(nx - 1, None)


def inner_kernel(last, *refs):
    refs = list(refs)
    take = lambda count: [refs.pop(0) for _ in range(count)]
    field, hzl, hzr, wx, wy, wzm, wzp, wze, out = take(9)
    if not last:
        (ends,) = take(1)
    total, flux, matrix, even, odd, even_halves, odd_halves = take(7)
    nx, ny, columns, nz = field.shape
    if not last:
        ends[...] = jnp.zeros_like(ends)
    difference_matrix(matrix)
    total[...] = jnp.zeros_like(total)
    flux[...] = jnp.zeros_like(flux)

    def differences(x, across, halves):
        plane = field[x].reshape(ny * columns, nz)
        high = plane.astype(BF16)
        low = (plane - high.astype(F32)).astype(BF16)
        both = jnp.concatenate([high, low], axis=1)
        halves[...] = both
        across[...] = jnp.dot(both, matrix[...], preferred_element_type=F32)

    def products(x, halves):
        left = jnp.concatenate(
            [
                jnp.concatenate(
                    [halves[y * columns : (y + 1) * columns, half] for y in range(ny)], axis=1
                )
                for half in (slice(0, nz), slice(nz, 2 * nz))
            ],
            axis=0,
        )
        right = split([jnp.concatenate([out[x, y] for y in range(ny)], axis=1)])
        total[...] += gram(left, jnp.concatenate([left, right], axis=0))

    def stencil(x, across, beside):
        block = x // 4
        beyond = arrived(hzl[block], hzr[block])
        beyond = pltpu.roll(beyond, (128 - (x % 4) * 32) % 128, 1)
        beyond = beyond * wze[pl.ds(x, 1), :]
        lane = lanes(columns)
        outer = (lane == 0) | (lane == nz - 1)
        center = field[x, 0]
        flux_y = None
        mine = jnp.zeros((columns, nz), F32)
        for y in range(ny):
            rows = slice(y * columns, (y + 1) * columns)
            applied = LEAKAGE * center - flux[y]
            if beside is not None:
                flux_x = wx[x + 1, y : y + 1, :] * (center - beside[y])
                applied = applied + flux_x
                flux[y] = flux_x
            if flux_y is not None:
                applied = applied - flux_y
            if y + 1 < ny:
                following = field[x, y + 1]
                flux_y = wy[x, y + 1 : y + 2, :] * (center - following)
                applied = applied + flux_y
            applied = applied + wzp[x, y : y + 1, :] * across[rows, 0:nz]
            applied = applied + wzm[x, y : y + 1, :] * across[rows, nz : 2 * nz]
            edge = pltpu.roll(beyond, (128 - (2 * y + 1)) % 128, 1)
            applied = applied - jnp.where(outer, edge, 0.0)
            out[x, y] = applied
            if not last:
                mine = packed_ends(applied, y, mine)
            center = following
        if not last:
            place_x(mine, x, ends, block, slice(None))

    def step(x, here, there, halves):
        products(x - 1, halves)
        differences(x + 1, there, halves)
        stencil(x, here, field.at[x + 1])

    def pair(place, carry):
        step(2 * place + 1, odd, even, even_halves)
        step(2 * place + 2, even, odd, odd_halves)
        return carry

    differences(0, even, even_halves)
    differences(1, odd, odd_halves)
    stencil(0, even, field.at[1])
    lax.fori_loop(0, nx // 2 - 1, pair, 0)
    products(nx - 2, even_halves)
    stencil(nx - 1, odd, None)
    products(nx - 1, odd_halves)


def sides_kernel(first, last, *refs):
    refs = list(refs)
    take = lambda count: [refs.pop(0) for _ in range(count)]
    part = take(1)[0]
    if first:
        own_faces = take(4)
    else:
        (field,) = take(1)
    hxl, hxr, hyl, hyr = take(4)
    if not last:
        take(1)
    if first:
        take(2)
        perm, inside = take(2)
    else:
        wx, wy, total = take(3)
    if last:
        (earlier,) = take(1)
    (out,) = take(1)
    if not last:
        (ends,) = take(1)
    if first:
        wx, wy = take(2)
    else:
        (sums,) = take(1)
    if not last:
        xlo, xhi, ylo, yhi = take(4)
    nx, ny, columns, nz = part.shape
    lane = lanes(columns)
    if first:
        hx = (hxl.at[ny, 0:ny], hxr.at[ny, 0:ny])
        outer_weights(perm, inside, hx, (hyl.at[ny], hyr.at[ny]), wx, wy)

    added = None
    faces = (
        (hxl, [(0, y) for y in range(ny)], [(0, y) for y in range(ny)], wx),
        (hxr, [(nx - 1, y) for y in range(ny)], [(nx, y) for y in range(ny)], wx),
        (hyl, [(x, 0) for x in range(nx)], [(x, 0) for x in range(nx)], wy),
        (hyr, [(x, ny - 1) for x in range(nx)], [(x, ny) for x in range(nx)], wy),
    )
    for side, (halo, rows, weight_rows, weight) in enumerate(faces):
        own, fluxes = [], []
        for place, ((x, y), (p, q)) in enumerate(zip(rows, weight_rows)):
            center = own_faces[side][place] if first else field[x, y]
            flux = weight[p, q : q + 1, :] * (center - halo[place])
            if first:
                out[x, y] -= flux
            else:
                out[x, y] += flux
                own.append(center)
                fluxes.append(flux)
        if not first:
            left = split([jnp.concatenate(own, axis=1)])
            right = split([jnp.concatenate(fluxes, axis=1)])
            part = gram(left, right)
            added = part if added is None else added + part
    if not last:
        for x in range(nx):
            tile = ends[x // 4]
            for y in range(ny):
                if x in (0, nx - 1) or y in (0, ny - 1):
                    tile = packed_ends(out[x, y], (x % 4) * 16 + y, tile)
            ends[x // 4] = tile
        for y in range(ny):
            xlo[y] = out[0, y]
            xhi[y] = out[nx - 1, y]
        for x in range(nx):
            ylo[x] = out[x, 0]
            yhi[x] = out[x, ny - 1]
    if not first:
        held = total[...]
        held = held[0:32] + held[32:64]
        held = held + pltpu.roll(held, 96, 1)
        held = jnp.where(lane < 32, held, pltpu.roll(held, 96, 1))
        fixed = added[0:32] + added[32:64]
        fixed = fixed[:, 0:32] + fixed[:, 32:64]
        fixed = jnp.concatenate([fixed, jnp.zeros((columns, 96), F32)], axis=1)
        held = jnp.where(lane < 32, held, held + pltpu.roll(fixed, 32, 1))
        if last:
            held = jnp.where(lane < 64, earlier[...], pltpu.roll(held, 64, 1))
        sums[...] = held


def split(fields):
    high = [field.astype(BF16) for field in fields]
    low = [(field - top.astype(F32)).astype(BF16) for field, top in zip(fields, high)]
    return jnp.concatenate(high + low, axis=0)


def gram(left, right):
    return lax.dot_general(left, right, (((1,), (1,)), ((), ())), preferred_element_type=F32)


def fold(products, fields):
    half = products.shape[0] // 2
    summed = products[:half] + products[half:]
    return summed[:, :half] + summed[:, half:]


def inner_part(field, halos, extra, first, last):
    nx, ny, columns, nz = field.shape
    in_specs = [HBM if first else VMEM] + [VMEM] * (len(halos) + len(extra))
    scratch = [pltpu.VMEM((ny, columns, nz), F32)]
    out_shape = [shaped(nx, ny, columns, nz)]
    if not last:
        out_shape += [shaped(4, columns, nz)]
    if first:
        scratch += [pltpu.VMEM(field.shape, F32), pltpu.SemaphoreType.DMA((nx,))]
        out_shape += [
            shaped(nx + 1, ny, nz),
            shaped(nx, ny + 8, nz),
            shaped(nx, ny, nz),
            shaped(nx, ny, nz),
            shaped(nx, nz),
        ]
    else:
        scratch += [pltpu.VMEM((2 * nz, 2 * nz), BF16)]
        scratch += [pltpu.VMEM((ny * columns, 2 * nz), F32)] * 2
        scratch += [pltpu.VMEM((ny * columns, 2 * nz), BF16)] * 2
        out_shape += [shaped(2 * columns, 4 * columns)]
    return pl.pallas_call(
        first_kernel if first else functools.partial(inner_kernel, last),
        in_specs=in_specs,
        out_specs=[VMEM] * len(out_shape),
        out_shape=out_shape,
        scratch_shapes=scratch,
        compiler_params=params(),
        cost_estimate=pl.CostEstimate(
            flops=20 * field.size, bytes_accessed=6 * field.size * 4, transcendentals=0
        ),
        name="inner_first" if first else "inner_last" if last else "inner_next",
    )(field, *halos, *extra)


def sides_part(part, own, halos, ends, extra, first, last):
    nx, ny, columns, nz = part.shape
    operands = [part, *own, *halos]
    place = len(operands)
    if not last:
        operands += [ends]
    operands += extra
    in_specs = [VMEM] * len(operands)
    aliases = {0: 0}
    out_shape = [shaped(*part.shape)]
    if not last:
        aliases[place] = 1
        out_shape += [shaped(*ends.shape)]
    if first:
        aliases[place + 1] = 2
        aliases[place + 2] = 3
        out_shape += [shaped(*extra[0].shape), shaped(*extra[1].shape)]
    else:
        out_shape += [shaped(columns, 128)]
    if not last:
        out_shape += [shaped(ny, columns, nz)] * 2 + [shaped(nx, columns, nz)] * 2
    return pl.pallas_call(
        functools.partial(sides_kernel, first, last),
        in_specs=in_specs,
        out_specs=[VMEM] * len(out_shape),
        out_shape=out_shape,
        input_output_aliases=aliases,
        compiler_params=params(),
        name="sides_first" if first else "sides_last" if last else "sides_next",
    )(*operands)


def exchanged(xlo, xhi, ylo, yhi, ends):
    ahead = lambda axis: [(i, (i + 1) % lax.axis_size(axis)) for i in range(lax.axis_size(axis))]
    back = lambda axis: [(j, i) for i, j in ahead(axis)]
    near = (
        lax.ppermute(ends, "layer", ahead("layer")),
        lax.ppermute(ends, "layer", back("layer")),
    )
    near, yhi = lax.optimization_barrier((near, yhi))
    far = (
        lax.ppermute(xhi, "strike", ahead("strike")),
        lax.ppermute(xlo, "strike", back("strike")),
        lax.ppermute(yhi, "dip", ahead("dip")),
        lax.ppermute(ylo, "dip", back("dip")),
    )
    return near, far


def dot(left, right, contract=(1, 0)):
    dims = (((contract[0],), (contract[1],)), ((), ()))
    return lax.dot_general(left, right, dims, precision=HIGHEST, preferred_element_type=F32)


def eliminate(tables):
    row = rows_of(32)
    for k in range(0, 32, 2):
        done = []
        for table in tables:
            one = jnp.broadcast_to(table[:, k : k + 1], table.shape)
            two = jnp.broadcast_to(table[:, k + 1 : k + 2], table.shape)
            a, b = one[k : k + 1], two[k : k + 1]
            c, d = one[k + 1 : k + 2], two[k + 1 : k + 2]
            scale = 1.0 / (a * d - b * c)
            upper, lower = table[k : k + 1], table[k + 1 : k + 2]
            first = (d * upper - b * lower) * scale
            second = (a * lower - c * upper) * scale
            rest = (table - one * first) - two * second
            done.append(jnp.where(row == k, first, jnp.where(row == k + 1, second, rest)))
        tables = done
    return tables


def solve_kernel(*refs):
    out_ref = refs[-1]
    sums = refs[0][...]
    for ref in refs[1:-1]:
        sums = sums + ref[...]
    lane = lanes(32)
    row = rows_of(32)
    table = jnp.where(lane < 32, pltpu.roll(sums, 96, 1), pltpu.roll(sums, 32, 1))
    table = jnp.where(lane < 64, table, jnp.where(lane == row + 64, 1.0, 0.0))
    (table,) = eliminate([table])
    norm = sums[:, 0:32]
    square = sums[:, 64:96]
    cube = sums[:, 96:128]
    advance = table[:, 32:64]
    inverse = table[:, 64:96]
    advance_t = advance.T
    turned = dot(square, advance)
    tripled = dot(advance, dot(cube, advance), (0, 0))
    mixing = dot(inverse, turned)
    norm_next = dot(advance, turned, (0, 0)) - norm
    curvature = tripled - dot(turned, mixing, (0, 0))
    wide = jnp.concatenate([curvature, norm_next, jnp.zeros((32, 64), F32)], axis=1)
    (wide,) = eliminate([wide])
    later = wide[:, 32:64]
    taken_t = advance_t + dot(later, mixing, (0, 1))
    beyond_t = dot(later, advance, (0, 1))
    nothing = jnp.zeros((32, 32), F32)
    out_ref[0:32, :] = jnp.concatenate([taken_t, -beyond_t, nothing, nothing], axis=1)
    out_ref[32:64, :] = jnp.concatenate([nothing, -taken_t, beyond_t, nothing], axis=1)


def solve(parts):
    return pl.pallas_call(
        solve_kernel,
        in_specs=[VMEM] * len(parts),
        out_specs=VMEM,
        out_shape=shaped(64, 128),
        compiler_params=params(),
        name="solve_small",
    )(*parts)


def combine_kernel(
    mix_ref, guess_ref, one_ref, two_ref, three_ref, solution_hbm, residual_hbm,
    solution, residual, sem,
):
    nx, ny, columns, nz = guess_ref.shape
    slots = solution.shape[0]

    mix = mix_ref[...]
    high = mix.astype(BF16)
    low = (mix - high.astype(F32)).astype(BF16)
    mixing = jnp.concatenate(
        [
            jnp.concatenate([half[:, : 3 * columns], half[:, : 3 * columns]], axis=1)
            for half in (high, low)
        ],
        axis=0,
    )

    def leaving(x):
        slot = x % slots
        copies = []
        for place, (held, away) in enumerate(((solution, solution_hbm), (residual, residual_hbm))):
            for half in range(ny // 8):
                copies.append(
                    pltpu.make_async_copy(
                        held.at[slot, half, 0:columns],
                        away.at[:, x, 8 * half : 8 * half + 8],
                        sem.at[place, half, slot],
                    )
                )
        return copies

    mix = mix_ref[...]
    high = mix.astype(BF16)
    low = (mix - high.astype(F32)).astype(BF16)
    mixing = jnp.concatenate(
        [
            jnp.concatenate([half[:, : 3 * columns], half[:, : 3 * columns]], axis=1)
            for half in (high, low)
        ],
        axis=0,
    )

    def at_pair(pair, carry):
        @pl.when(2 * pair >= slots)
        def _():
            for step in range(2):
                for copy in leaving(2 * pair + step - slots):
                    copy.wait()

        for step in range(2):
            x = 2 * pair + step
            slot = lax.rem(x, slots)
            solution_rows = solution.at[slot].reshape((columns + 1) * ny, nz)
            residual_rows = residual.at[slot].reshape((columns + 1) * ny, nz)
            for y in range(0, ny, 2):
                fields = [
                    jnp.concatenate([ref[x, y], ref[x, y + 1]], axis=1)
                    for ref in (one_ref, two_ref, three_ref)
                ]
                mixed = jnp.dot(mixing, split(fields), preferred_element_type=F32)
                mixed = mixed[0:64] + mixed[64:128]
                for z in range(2):
                    own = y + z
                    rows = pl.ds((own // 8) * 8 * (columns + 1) + own % 8, columns, stride=8)
                    part = mixed[:, z * nz : (z + 1) * nz]
                    solution_rows[rows, :] = guess_ref[x, own] + part[0:32]
                    residual_rows[rows, :] = one_ref[x, own] + part[32:64]
        for step in range(2):
            for copy in leaving(2 * pair + step):
                copy.start()
        return carry

    lax.fori_loop(0, nx // 2, at_pair, 0)
    for x in range(nx - slots, nx):
        for copy in leaving(x):
            copy.wait()


def combine(mix, guess, one, two, three):
    nx, ny, columns, nz = guess.shape
    return pl.pallas_call(
        combine_kernel,
        in_specs=[VMEM] * 5,
        out_specs=[HBM] * 2,
        out_shape=[jax.ShapeDtypeStruct((columns, nx, ny, nz), F32)] * 2,
        scratch_shapes=[
            pltpu.VMEM((8, ny // 8, columns + 1, 8, nz), F32),
            pltpu.VMEM((8, ny // 8, columns + 1, 8, nz), F32),
            pltpu.SemaphoreType.DMA((2, ny // 8, 8)),
        ],
        compiler_params=params(),
        name="combine_fields",
    )(mix, guess, one, two, three)


def swaps(axis, mask, stride=1):
    return [(i, i ^ (mask * stride)) for i in range(lax.axis_size(axis))]


def summed_but_last(values):
    groups = []
    for axis in AXES[::-1]:
        size, stride = lax.axis_size(axis), 1
        while size // stride > 4:
            values = values + lax.ppermute(values, axis, swaps(axis, 1, stride))
            stride *= 2
        groups.append((axis, stride))
    for place, (axis, stride) in enumerate(groups):
        others = [
            lax.ppermute(values, axis, swaps(axis, mask, stride))
            for mask in (1, 3, 2)
            if mask * stride < lax.axis_size(axis)
        ]
        if place + 1 < len(groups):
            for other in others:
                values = values + other
    return [values, *others]


def shards(perm_class, perm_table, boreholes, start_guess):
    columns, nx, ny, nz = start_guess.shape
    places = [lax.axis_index(axis) for axis in AXES]
    sizes = [lax.axis_size(axis) for axis in AXES]
    anchors = [place * size for place, size in zip(places, (nx, ny, nz))]
    totals = tuple(size * count for size, count in zip((nx, ny, nz), sizes))
    inside = []
    for place, size in zip(places, sizes):
        inside += [place > 0, place < size - 1]
    inside = jnp.broadcast_to(jnp.stack(inside + inside[:2]).astype(F32)[:, None], (8, nz))

    in_hbm = [
        pltpu.with_memory_space_constraint(held, pltpu.HBM)
        for held in (perm_class, perm_table, start_guess)
    ]
    guess, perm, *faces = pack(*in_hbm)
    guess = pltpu.with_memory_space_constraint(guess, pltpu.HBM)
    near, far = exchanged(*faces)
    code = local_sources(boreholes[:, None], anchors, nx, ny, nz, totals[1], totals[2])
    extra = (perm, inside, code)
    part, ends, wx, wy, *along_z = inner_part(guess, near, extra, True, False)
    residual, ends, wx, wy, *faces = sides_part(
        part, faces[:4], far, ends, [wx, wy, perm, inside], True, False
    )
    weights = (wx, wy, *along_z)
    near, far = exchanged(*faces, ends)
    part, ends, total = inner_part(residual, near, weights, False, False)
    once, ends, sums, *faces = sides_part(
        part, [residual], far, ends, [wx, wy, total], False, False
    )
    near, far = exchanged(*faces, ends)
    part, total = inner_part(once, near, weights, False, True)
    twice, sums = sides_part(part, [once], far, None, [wx, wy, total, sums], False, True)
    mix = solve(summed_but_last(sums))
    guess = pltpu.with_memory_space_constraint(guess, pltpu.VMEM)
    return tuple(combine(mix, guess, residual, once, twice))


def solution(mesh):
    placed = (P("strike", "dip", "layer"), P(), P(), P(None, "strike", "dip", "layer"))
    return jax.shard_map(
        shards,
        mesh=mesh,
        in_specs=placed,
        out_specs=(P(None, "strike", "dip", "layer"), P(None, "strike", "dip", "layer")),
        check_vma=False,
    )
```
